32 devices in a mesh: dp: 8 (over y, x, core), mp: 4 (over z).
Axes of the slice: x: 2, y: 2, z: 4, core: 2. Of those that a mesh axis runs over, the one named last changes fastest.
Arguments:
- images_in: bfloat16 [192, 50, 1024], P('dp'), may hold values from -6 to 6
- out_cotangent: bfloat16 [192, 50, 1024], P('dp'), may hold values from -6 to 6
- norm1_gain: float32 [2, 1024], replicated, may hold values from 0.5 to 1.5
- norm1_bias: float32 [2, 1024], replicated, may hold values from -3 to 3
- qkv_weight: bfloat16 [2, 1024, 3, 1024], P(None, None, None, 'mp'), may hold values from -0.1875 to 0.1875
- qv_bias: float32 [2, 2, 1024], P(None, None, 'mp'), may hold values from -3 to 3
- proj_weight: bfloat16 [2, 1024, 1024], P(None, 'mp'), may hold values from -0.375 to 0.375
- proj_bias: float32 [2, 1024], replicated, may hold values from -3 to 3
- norm2_gain: float32 [2, 1024], replicated, may hold values from 0.5 to 1.5
- norm2_bias: float32 [2, 1024], replicated, may hold values from -3 to 3
- fc1_weight: bfloat16 [2, 1024, 4096], P(None, None, 'mp'), may hold values from -0.1875 to 0.1875
- fc1_bias: float32 [2, 4096], P(None, 'mp'), may hold values from -3 to 3
- fc2_weight: bfloat16 [2, 4096, 1024], P(None, 'mp'), may hold values from -0.09375 to 0.09375
- fc2_bias: float32 [2, 1024], replicated, may hold values from -3 to 3
Outputs:
- block_out: bfloat16 [192, 50, 1024], P('dp')
- input_grad: float32 [192, 50, 1024], P('dp')
- grad_norm1_gain: float32 [2, 1024], replicated
- grad_norm1_bias: float32 [2, 1024], replicated
- grad_qkv_weight: float32 [2, 1024, 3, 1024], P(None, 'dp', None, 'mp')
- grad_qv_bias: float32 [2, 2, 1024], P(None, None, 'mp')
- grad_proj_weight: float32 [2, 1024, 1024], P(None, 'mp', 'dp')
- grad_proj_bias: float32 [2, 1024], replicated
- grad_norm2_gain: float32 [2, 1024], replicated
- grad_norm2_bias: float32 [2, 1024], replicated
- grad_fc1_weight: float32 [2, 1024, 4096], P(None, 'dp', 'mp')
- grad_fc1_bias: float32 [2, 4096], P(None, 'mp')
- grad_fc2_weight: float32 [2, 4096, 1024], P(None, 'mp', 'dp')
- grad_fc2_bias: float32 [2, 1024], replicated
The draws below stay inside these ranges and needn't reach their ends.
All inputs are finite; a program needn't handle non-finite values.
Results may differ from the reference program's by a relative error of at most 0.025.
Values may be sent and summed in bfloat16 or wider, within the bound.
No kernel may reach another device: no remote copies, remote signals or barrier semaphores. Data moves between devices by JAX's collectives and lax.ppermute only.
A program may use at most 192 MiB of HBM per device.

```python
import jax
import jax.numpy as jnp
from jax import lax

D = 1024
HEADS = 16
HEAD_DIM = 64
FF = 4096
SEQ = 50
LAYERS = 2
IMG_DEV = 24
IMAGES = 192
N_MP = 4


def steps_of(rng, dims, split, smallest, top_value):
    factor_of, own = 1.0, jax.random.fold_in(rng, 6)
    for dim, shards_of in split:
        heights = jnp.exp(jax.random.uniform(jax.random.fold_in(own, dim), (shards_of,), jnp.float32, smallest / len(split), top_value / len(split)))
        factor_of = factor_of * jnp.repeat(heights, dims[dim] // shards_of).reshape([-1 if axis == dim else 1 for axis in range(len(dims))])
    return factor_of


def centred(rng, shape, width, reach, cuts=(), kind=jnp.bfloat16):
    values = width * jax.random.normal(rng, shape, jnp.float32)
    if cuts:
        values = values * steps_of(rng, shape, cuts, -0.22, 0.18)
    return jnp.clip(values, -reach, reach).astype(kind)


def setup_inputs(seed: int = 0) -> dict:
    key_list = jax.random.split(jax.random.key(seed), 15)
    return {
        "images_in": centred(key_list[0], (IMAGES, SEQ, D), 1.0, 6.0, ((0, 8),)),
        "out_cotangent": centred(key_list[1], (IMAGES, SEQ, D), 1.0, 6.0, ((0, 8),)),
        "norm1_gain": jnp.clip(1.0 + 0.1 * jax.random.normal(key_list[2], (LAYERS, D), jnp.float32), 0.5, 1.5),
        "norm1_bias": centred(key_list[3], (LAYERS, D), 0.5, 3.0, (), jnp.float32),
        "qkv_weight": centred(key_list[4], (LAYERS, D, 3, D), D ** -0.5, 0.1875, ((3, 4),)),
        "qv_bias": centred(key_list[5], (LAYERS, 2, D), 0.5, 3.0, ((2, 4),), jnp.float32),
        "proj_weight": centred(key_list[6], (LAYERS, D, D), (D // 4) ** -0.5, 0.375, ((1, 4),)),
        "proj_bias": centred(key_list[7], (LAYERS, D), 0.5, 3.0, (), jnp.float32),
        "norm2_gain": jnp.clip(1.0 + 0.1 * jax.random.normal(key_list[8], (LAYERS, D), jnp.float32), 0.5, 1.5),
        "norm2_bias": centred(key_list[9], (LAYERS, D), 0.5, 3.0, (), jnp.float32),
        "fc1_weight": centred(key_list[10], (LAYERS, D, FF), D ** -0.5, 0.1875, ((2, 4),)),
        "fc1_bias": centred(key_list[11], (LAYERS, FF), 0.5, 3.0, ((1, 4),), jnp.float32),
        "fc2_weight": centred(key_list[12], (LAYERS, FF, D), FF ** -0.5, 0.09375, ((1, 4),)),
        "fc2_bias": centred(key_list[13], (LAYERS, D), 0.5, 3.0, (), jnp.float32),
    }


@jax.custom_vjp
def low(v):
    return lax.optimization_barrier(v.astype(jnp.bfloat16)).astype(jnp.float32)

@jax.custom_vjp
def low_back(v):
    return v

def low_keep(v):
    return (low(v), None)

def low_pass(kept, grad):
    return (grad,)

def back_keep(v):
    return (v, None)

def back_low(kept, grad):
    return (low(grad),)
low.defvjp(low_keep, low_pass)
low_back.defvjp(back_keep, back_low)
EPS = 1e-06
HIGH = lax.Precision.HIGHEST

def layer_norm(rows, gain, bias):
    mean = lax.optimization_barrier(jnp.mean(rows, axis=-1, keepdims=True))
    centered = rows - mean
    variance = lax.optimization_barrier(jnp.mean(centered * centered, axis=-1, keepdims=True))
    return centered * lax.rsqrt(variance + EPS) * gain + bias

def one_layer(rows, images, params):
    gain1, bias1, wqkv, bqv, wproj, bproj, gain2, bias2, wfc1, bfc1, wfc2, bfc2 = params
    count = rows.shape[0]
    cols = D // N_MP
    hidden_cols = FF // N_MP
    group_heads = HEADS // N_MP
    scale = HEAD_DIM ** (-0.5)
    normed = low(layer_norm(rows, gain1, bias1))
    parts = []
    for group in range(N_MP):
        feed = low_back(normed)
        lo_col = group * cols
        wpart = wqkv[:, :, lo_col:lo_col + cols]
        qkv = jnp.einsum('nd,dtc->ntc', feed, wpart, precision=HIGH)
        query = low(low_back(qkv[:, 0] + bqv[0, lo_col:lo_col + cols]))
        key = low(low_back(qkv[:, 1]))
        value = low(low_back(qkv[:, 2] + bqv[1, lo_col:lo_col + cols]))
        shape4 = (images, SEQ, group_heads, HEAD_DIM)
        scores = jnp.einsum('bqhe,bkhe->bhqk', query.reshape(shape4), key.reshape(shape4), precision=HIGH) * scale
        scores = low_back(scores)
        probs = low(jax.nn.softmax(scores, axis=-1))
        mixed = jnp.einsum('bhqk,bkhe->bqhe', probs, value.reshape(shape4), precision=HIGH)
        mixed = low(low_back(mixed.reshape(count, cols)))
        parts.append(low(jnp.dot(mixed, wproj[lo_col:lo_col + cols], precision=HIGH)))
    attended = low_back(sum(parts))
    middle = rows + attended + bproj
    normed2 = low(layer_norm(middle, gain2, bias2))
    parts2 = []
    for group in range(N_MP):
        feed = low_back(normed2)
        lo_col = group * hidden_cols
        hidden = jnp.dot(feed, wfc1[:, lo_col:lo_col + hidden_cols], precision=HIGH) + bfc1[lo_col:lo_col + hidden_cols]
        hidden = low_back(hidden)
        active = low(jax.nn.gelu(hidden, approximate=False))
        parts2.append(low(jnp.dot(active, wfc2[lo_col:lo_col + hidden_cols], precision=HIGH)))
    return middle + low_back(sum(parts2)) + bfc2

def forward(tokens, params):
    images = tokens.shape[0]
    rows = tokens.reshape(images * SEQ, D)
    for layer in range(LAYERS):
        rows = one_layer(rows, images, tuple((p[layer] for p in params)))
    return rows.reshape(images, SEQ, D)

def reference(images_in, out_cotangent, norm1_gain, norm1_bias, qkv_weight, qv_bias, proj_weight, proj_bias, norm2_gain, norm2_bias, fc1_weight, fc1_bias, fc2_weight, fc2_bias):
    params = tuple((p.astype(jnp.float32) for p in (norm1_gain, norm1_bias, qkv_weight, qv_bias, proj_weight, proj_bias, norm2_gain, norm2_bias, fc1_weight, fc1_bias, fc2_weight, fc2_bias)))
    blocks = IMAGES // IMG_DEV
    inputs = images_in.reshape(blocks, IMG_DEV, SEQ, D)
    cotangents = out_cotangent.reshape(blocks, IMG_DEV, SEQ, D)
    zeros = jax.tree.map(jnp.zeros_like, params)

    def step(totals, pair):
        block_in, block_cot = pair
        result, pull = jax.vjp(forward, block_in.astype(jnp.float32), params)
        grad_in, grad_params = pull(block_cot.astype(jnp.float32))
        totals = jax.tree.map(jnp.add, totals, grad_params)
        return (totals, (result.astype(jnp.bfloat16), grad_in))
    totals, (results, grads_in) = lax.scan(step, zeros, (inputs, cotangents))
    return (results.reshape(IMAGES, SEQ, D), grads_in.reshape(IMAGES, SEQ, D), totals[0], totals[1], totals[2], totals[3], totals[4], totals[5], totals[6], totals[7], totals[8], totals[9], totals[10], totals[11])
```

```python
import functools

import jax
import jax.numpy as jnp
from jax import lax
from jax.experimental import pallas as pl
from jax.experimental.pallas import tpu as pltpu
from jax.sharding import PartitionSpec as P

HEAD_DIM = 64
EPS = 1e-06
F32 = jnp.float32
BF16 = jnp.bfloat16
ROWS = 304
WIN = 112
WIN_STEP = 96
BIG_NEG = -1e30
VMEM_LIMIT = 60 * 1024 * 1024


def dot_nn(a, b):
    return lax.dot_general(a, b, (((1,), (0,)), ((), ())), preferred_element_type=F32)


def dot_nt(a, b):
    return lax.dot_general(a, b, (((1,), (1,)), ((), ())), preferred_element_type=F32)


def dot_tn(a, b):
    return lax.dot_general(a, b, (((0,), (0,)), ((), ())), preferred_element_type=F32)


def params(micros):
    return dict(
        compiler_params=pltpu.CompilerParams(vmem_limit_bytes=VMEM_LIMIT),
        cost_estimate=pl.CostEstimate(
            flops=int(micros * 1e9), bytes_accessed=0, transcendentals=0
        ),
    )


VM = pl.BlockSpec(memory_space=pltpu.VMEM)
SM = pl.BlockSpec(memory_space=pltpu.SMEM)
HB = pl.BlockSpec(memory_space=pl.ANY)


def layer_norm(x, gain, bias):
    mean = jnp.mean(x, axis=-1, keepdims=True)
    centered = x - mean
    variance = jnp.mean(centered * centered, axis=-1, keepdims=True)
    return centered * lax.rsqrt(variance + EPS) * gain + bias


def own_selector(place, seq, mine):
    images = 4 * mine
    row = lax.broadcasted_iota(jnp.int32, (ROWS, images * seq), 0)
    col = lax.broadcasted_iota(jnp.int32, (ROWS, images * seq), 1)
    token = col // images
    image = col - token * images - place[DEPTH] * mine
    hit = (image >= 0) & (image < mine) & (row == image * seq + token)
    return jnp.where(hit, 1.0, 0.0).astype(BF16)


def enter_kernel(seq, mine, place, x_ref, gain_ref, beta_ref, x1_ref, a_ref):
    x = dot_nn(own_selector(place, seq, mine), x_ref[...])
    x1_ref[...] = x
    a_ref[...] = layer_norm(x, gain_ref[...], beta_ref[...]).astype(BF16)


def enter_back_kernel(seq, mine, place, x_ref, g_ref, gb_ref, sum_ref):
    g = dot_nn(own_selector(place, seq, mine), x_ref[...])
    g_ref[...] = g
    gb_ref[...] = g.astype(BF16)
    sum_ref[...] = jnp.broadcast_to(jnp.sum(g, axis=0, keepdims=True), sum_ref.shape)


def leave_kernel(seq, mine, parts_ref, out_ref):
    images = 4 * mine
    count = images * seq
    total = None
    for depth in range(4):
        row = lax.broadcasted_iota(jnp.int32, (count, ROWS), 0)
        col = lax.broadcasted_iota(jnp.int32, (count, ROWS), 1)
        token = row // images
        image = row - token * images - depth * mine
        hit = (image >= 0) & (image < mine) & (col == image * seq + token)
        part = dot_nn(jnp.where(hit, 1.0, 0.0).astype(BF16), parts_ref[depth])
        total = part if total is None else total + part
    out_ref[...] = total.astype(out_ref.dtype)


def residual_norm_kernel(
    x_ref, own_ref, far_ref, bias_ref, gain_ref, beta_ref, x1_ref, a_ref
):
    keep = lax.broadcasted_iota(jnp.int32, (ROWS, 1), 0) < 300
    bias = jnp.where(keep, bias_ref[...], 0.0)
    x1 = x_ref[...] + own_ref[...].astype(F32) + far_ref[...].astype(F32) + bias
    x1_ref[...] = x1
    a_ref[...] = layer_norm(x1, gain_ref[...], beta_ref[...]).astype(BF16)


def residual_kernel(x_ref, own_ref, far_ref, bias_ref, x1_ref):
    x1 = x_ref[...] + own_ref[...].astype(F32) + far_ref[...].astype(F32) + bias_ref[...]
    x1_ref[...] = x1.astype(BF16)


def norm_back_kernel(g_ref, own_ref, far_ref, x_ref, gain_ref, g1_ref, g1b_ref, sums_ref):
    x = x_ref[...]
    mean = jnp.mean(x, axis=-1, keepdims=True)
    centered = x - mean
    variance = jnp.mean(centered * centered, axis=-1, keepdims=True)
    inverse = lax.rsqrt(variance + EPS)
    xhat = centered * inverse
    da = own_ref[...].astype(F32) + far_ref[...].astype(F32)
    inner = da * gain_ref[...]
    mean_inner = jnp.mean(inner, axis=-1, keepdims=True)
    mean_proj = jnp.mean(inner * xhat, axis=-1, keepdims=True)
    g1 = g_ref[...] + inverse * (inner - mean_inner - xhat * mean_proj)
    g1_ref[...] = g1
    g1b_ref[...] = g1.astype(BF16)
    sums_ref[...] = jnp.zeros(sums_ref.shape, F32)
    sums_ref[0:1, :] = jnp.sum(da * xhat, axis=0, keepdims=True)
    sums_ref[1:2, :] = jnp.sum(da, axis=0, keepdims=True)
    sums_ref[2:3, :] = jnp.sum(g1, axis=0, keepdims=True)


def run_enter(place, images, mine, gain, beta):
    count, seq, width = images.shape
    flat = images.transpose(1, 0, 2).reshape(count * seq, width)
    return pl.pallas_call(
        functools.partial(enter_kernel, seq, mine),
        out_shape=(
            jax.ShapeDtypeStruct((ROWS, width), F32),
            jax.ShapeDtypeStruct((ROWS, width), BF16),
        ),
        in_specs=[SM, VM, VM, VM],
        out_specs=(VM, VM),
        **params(5),
    )(place, flat, gain[None], beta[None])


def run_enter_back(place, images, mine):
    count, seq, width = images.shape
    flat = images.transpose(1, 0, 2).reshape(count * seq, width)
    return pl.pallas_call(
        functools.partial(enter_back_kernel, seq, mine),
        out_shape=(
            jax.ShapeDtypeStruct((ROWS, width), F32),
            jax.ShapeDtypeStruct((ROWS, width), BF16),
            jax.ShapeDtypeStruct((8, width), F32),
        ),
        in_specs=[SM, VM],
        out_specs=(VM, VM, VM),
        **params(5),
    )(place, flat)


def run_leave(parts, seq, mine, dtype):
    images, width = 4 * mine, parts.shape[2]
    flat = pl.pallas_call(
        functools.partial(leave_kernel, seq, mine),
        out_shape=jax.ShapeDtypeStruct((images * seq, width), dtype),
        in_specs=[VM],
        out_specs=VM,
        **params(6),
    )(parts)
    return flat.reshape(seq, images, width).transpose(1, 0, 2)


def run_residual_norm(x, own, far, bias, gain, beta):
    return pl.pallas_call(
        residual_norm_kernel,
        out_shape=(
            jax.ShapeDtypeStruct(x.shape, F32),
            jax.ShapeDtypeStruct(x.shape, BF16),
        ),
        in_specs=[VM] * 6,
        out_specs=(VM, VM),
        **params(3),
    )(x, own, far, bias[None], gain[None], beta[None])


def run_residual(x, own, far, bias):
    return pl.pallas_call(
        residual_kernel,
        out_shape=jax.ShapeDtypeStruct(x.shape, BF16),
        in_specs=[VM] * 4,
        out_specs=VM,
        **params(2),
    )(x, own, far, bias[None])


def run_norm_back(g, own, far, x, gain):
    return pl.pallas_call(
        norm_back_kernel,
        out_shape=(
            jax.ShapeDtypeStruct(x.shape, F32),
            jax.ShapeDtypeStruct(x.shape, BF16),
            jax.ShapeDtypeStruct((8, x.shape[1]), F32),
        ),
        in_specs=[VM] * 5,
        out_specs=(VM, VM, VM),
        **params(4),
    )(g, own, far, x, gain[None])


SIDE, CORE, PAIR, DEPTH, PARTS = 0, 1, 2, 3, 4


def exact_rows(bias):
    high = bias.astype(BF16)
    rest = bias - high.astype(F32)
    mid = rest.astype(BF16)
    low = (rest - mid.astype(F32)).astype(BF16)
    return jnp.concatenate([high, mid, low, jnp.zeros((13, bias.shape[1]), BF16)], axis=0)


def pack_kernel(
    place, wqkv, wproj, w1, w2, bqv, b1, attn0, mlp0, attn1, mlp1, sems
):
    row = aligned(place[PARTS], 256)
    narrow, wide = aligned(place[PAIR], 128), aligned(place[PAIR], 512)
    copies = []
    for layer, (attn, mlp) in enumerate(((attn0, mlp0), (attn1, mlp1))):
        for item in range(3):
            copies.append(
                (
                    wqkv.at[layer, item, pl.ds(row, 256), pl.ds(narrow, 128)],
                    attn.at[0:256, pl.ds(item * 128, 128)],
                )
            )
        for half in range(2):
            copies.append(
                (
                    wproj.at[layer, pl.ds(narrow, 128), pl.ds(row + half * 128, 128)],
                    attn.at[pl.ds(half * 128, 128), 384:512],
                )
            )
            copies.append(
                (
                    w2.at[layer, pl.ds(wide + half * 256, 256), pl.ds(row, 256)],
                    mlp.at[256:512, pl.ds(half * 256, 256)],
                )
            )
        copies.append(
            (w1.at[layer, pl.ds(row, 256), pl.ds(wide, 512)], mlp.at[0:256, :])
        )
    copies = [
        pltpu.make_async_copy(src, dst, sems.at[index])
        for index, (src, dst) in enumerate(copies)
    ]
    for copy in copies:
        copy.start()
    for layer, (attn, mlp) in enumerate(((attn0, mlp0), (attn1, mlp1))):
        zero = jnp.zeros((1, 128), F32)
        bias = [bqv[layer, pl.ds(item, 1), pl.ds(narrow, 128)] for item in range(2)]
        attn[256:272, :] = exact_rows(jnp.concatenate([bias[0], zero, bias[1], zero], axis=1))
        mlp[512:528, :] = exact_rows(b1[pl.ds(layer, 1), pl.ds(wide, 512)])
    for copy in copies:
        copy.wait()


def run_pack(place, wqkv, wproj, w1, w2, bqv, b1):
    attn = jax.ShapeDtypeStruct((272, 512), BF16)
    mlp = jax.ShapeDtypeStruct((528, 512), BF16)
    return pl.pallas_call(
        pack_kernel,
        out_shape=(attn, mlp, attn, mlp),
        in_specs=[SM, HB, HB, HB, HB, VM, VM],
        out_specs=(VM, VM, VM, VM),
        scratch_shapes=[pltpu.SemaphoreType.DMA((16,))],
        **params(3),
    )(place, wqkv, wproj, w1, w2, bqv, b1)


def piece_sources(place, pieces, chunk):
    return [
        (src, place[PARTS + slot]) for slot, src in enumerate(pieces[4 * chunk - 4 : 4 * chunk])
    ]


def aligned(index, step):
    if isinstance(index, int):
        return index * step
    return pl.multiple_of(index * step, step)


def start_attention_copies(layer, place, wqkv, wproj, bqv, pieces, wq, wp, sems, bs=None):
    narrow = aligned(place[PAIR], 128)
    for item in range(3):
        pltpu.make_async_copy(
            wqkv.at[layer, item, :, pl.ds(narrow, 128)],
            wq.at[0, :, pl.ds(item * 128, 128)],
            sems.at[0, 0],
        ).start()
    pltpu.make_async_copy(
        wproj.at[layer, pl.ds(narrow, 128), :], wp.at[0], sems.at[1, 0]
    ).start()
    for chunk in range(1, 4):
        for slot, (src, index) in enumerate(piece_sources(place, pieces, chunk)):
            row = aligned(index, 256)
            pltpu.make_async_copy(
                src.at[0:256, 0:384], wq.at[chunk, pl.ds(row, 256), :], sems.at[0, chunk]
            ).start()
            for side in range(2):
                pltpu.make_async_copy(
                    src.at[pl.ds(side * 128, 128), 384:512],
                    wp.at[chunk, :, pl.ds(row + side * 128, 128)],
                    sems.at[1, chunk],
                ).start()
            if bs is not None and slot == 0:
                pltpu.make_async_copy(
                    src.at[256:272, 0:384], bs.at[chunk], sems.at[2, chunk]
                ).start()
    if bs is not None:
        bias = [bqv[layer, pl.ds(item, 1), pl.ds(narrow, 128)] for item in range(2)]
        zero = jnp.zeros((1, 128), F32)
        bs[0] = exact_rows(jnp.concatenate([bias[0], zero, bias[1]], axis=1))


def start_mlp_copies(layer, place, first, second, bias, pieces, w1, w2, sems, bs=None):
    wide = aligned(place[PAIR], 512)
    pltpu.make_async_copy(first.at[layer, :, pl.ds(wide, 512)], w1.at[0], sems.at[0, 0]).start()
    pltpu.make_async_copy(second.at[layer, pl.ds(wide, 512), :], w2.at[0], sems.at[1, 0]).start()
    for chunk in range(1, 4):
        for slot, (src, index) in enumerate(piece_sources(place, pieces, chunk)):
            row = aligned(index, 256)
            pltpu.make_async_copy(
                src.at[0:256, :], w1.at[chunk, pl.ds(row, 256), :], sems.at[0, chunk]
            ).start()
            for side in range(2):
                pltpu.make_async_copy(
                    src.at[256:512, pl.ds(side * 256, 256)],
                    w2.at[chunk, pl.ds(side * 256, 256), pl.ds(row, 256)],
                    sems.at[1, chunk],
                ).start()
            if bs is not None and slot == 0:
                pltpu.make_async_copy(
                    src.at[512:528, :], bs.at[chunk], sems.at[2, chunk]
                ).start()
    if bs is not None:
        bs[0] = exact_rows(bias[layer : layer + 1, pl.ds(wide, 512)])


def start_rows(own, far, rows, sems):
    copies = [
        pltpu.make_async_copy(own, rows.at[0:ROWS, :], sems.at[3, 0]),
        pltpu.make_async_copy(far, rows.at[pl.ds(ROWS, ROWS), :], sems.at[3, 1]),
    ]
    for copy in copies:
        copy.start()
    return copies


def wait_all(copies):
    for copy in copies:
        copy.wait()


def wait_chunk(chunk, bufs, sems):
    for slot, buf in enumerate(bufs):
        pltpu.make_async_copy(buf.at[chunk], buf.at[chunk], sems.at[slot, chunk]).wait()


def wait_bias(chunk, bs, sems):
    @pl.when(chunk > 0)
    def _():
        pltpu.make_async_copy(bs.at[chunk], bs.at[chunk], sems.at[2, chunk]).wait()


def window_masks(window):
    shape = (2 * WIN, WIN)
    row = lax.broadcasted_iota(jnp.int32, shape, 0)
    row = jnp.where(row >= WIN, row - WIN, row) - 4 * window
    col = lax.broadcasted_iota(jnp.int32, shape, 1) - 4 * window
    row_ok = (row >= 0) & (row < 100)
    col_ok = (col >= 0) & (col < 100)
    same = row_ok & col_ok & ((row >= 50) == (col >= 50))
    return jnp.where(same, 0.0, BIG_NEG).astype(F32)


def window_rows_ok(window):
    row = lax.broadcasted_iota(jnp.int32, (2 * WIN, 1), 0)
    row = jnp.where(row >= WIN, row - WIN, row) - 4 * window
    return (row >= 0) & (row < 100)


def stack_heads(values, first):
    zero = jnp.zeros_like(values)
    return jnp.concatenate(
        [jnp.where(first, values, zero), jnp.where(first, zero, values)], axis=0
    )


def first_head_lanes():
    return lax.broadcasted_iota(jnp.int32, (WIN, 2 * HEAD_DIM), 1) < HEAD_DIM


def window_probs(query, key, mask, rows_ok):
    scores = dot_nt(query, key) * (HEAD_DIM**-0.5) + mask
    top = jnp.max(scores, axis=-1, keepdims=True)
    expo = jnp.exp(scores - top)
    total = jnp.sum(expo, axis=-1, keepdims=True)
    return expo * jnp.where(rows_ok, 1.0 / total, 0.0)


def join_windows(parts):
    first, second, third = parts
    over = WIN - WIN_STEP
    return jnp.concatenate(
        [
            first[:WIN_STEP],
            first[WIN_STEP:] + second[:over],
            second[over:WIN_STEP],
            second[WIN_STEP:] + third[:over],
            third[over:],
        ],
        axis=0,
    )


def attention_forward_kernel(
    layer, place, a_own, a_far, wqkv, wproj, bqv, *refs
):
    pieces = refs[:12]
    qkv_ref, o_ref, r_own, r_far, wq, wp, bs, rows, total, masks, sems = refs[12:]
    copies = start_rows(a_own, a_far, rows, sems)
    start_attention_copies(layer, place, wqkv, wproj, bqv, pieces, wq, wp, sems, bs)
    for window in range(3):
        masks[window] = window_masks(window)
    wait_all(copies)

    def chunk_step(chunk, carry):
        wait_chunk(chunk, (wq, wp), sems)
        wait_bias(chunk, bs, sems)
        bias = jnp.sum(bs[chunk].astype(F32), axis=0, keepdims=True)
        qkv_ref[chunk] = (dot_nn(rows[...], wq[chunk]) + bias).astype(BF16)
        first = first_head_lanes()
        for block in range(2):
            outs = []
            for window in range(3):
                span = pl.ds(block * ROWS + window * WIN_STEP, WIN)
                query = stack_heads(qkv_ref[chunk, span, 0:128], first)
                probs = window_probs(
                    query, qkv_ref[chunk, span, 128:256], masks[window], window_rows_ok(window)
                )
                mixed = dot_nn(probs.astype(BF16), qkv_ref[chunk, span, 256:384])
                outs.append(jnp.where(first, mixed[:WIN], mixed[WIN:]))
            o_ref[chunk, pl.ds(block * ROWS, ROWS), :] = join_windows(outs).astype(BF16)
        part = dot_nn(o_ref[chunk], wp[chunk])

        @pl.when(chunk == 0)
        def _():
            total[...] = part

        @pl.when(chunk > 0)
        def _():
            total[...] += part

        return carry

    lax.fori_loop(0, 4, chunk_step, 0)
    r_own[...] = total[0:ROWS, :].astype(BF16)
    r_far[...] = total[ROWS:, :].astype(BF16)


def run_attention_forward(layer, place, a_own, a_far, weights, pieces):
    rows, width = 2 * ROWS, a_own.shape[1]
    return pl.pallas_call(
        functools.partial(attention_forward_kernel, layer),
        out_shape=(
            jax.ShapeDtypeStruct((4, rows, 384), BF16),
            jax.ShapeDtypeStruct((4, rows, 128), BF16),
            jax.ShapeDtypeStruct((ROWS, width), BF16),
            jax.ShapeDtypeStruct((ROWS, width), BF16),
        ),
        in_specs=[SM, HB, HB, HB, HB, VM] + [HB] * 12,
        out_specs=(VM, VM, VM, VM),
        scratch_shapes=[
            pltpu.VMEM((4, width, 384), BF16),
            pltpu.VMEM((4, 128, width), BF16),
            pltpu.VMEM((4, 16, 384), BF16),
            pltpu.VMEM((rows, width), BF16),
            pltpu.VMEM((rows, width), F32),
            pltpu.VMEM((3, 2 * WIN, WIN), F32),
            pltpu.SemaphoreType.DMA((4, 4)),
        ],
        **params(13),
    )(place, a_own, a_far, *weights, *pieces)


def attention_backward_kernel(
    layer, place, g_own, g_far, qkv_ref, wqkv, wproj, *refs
):
    pieces = refs[:12]
    dqkv_ref, sums_ref, d_own, d_far, wq, wp, rows, total, masks, gmix, sems = refs[12:]
    copies = start_rows(g_own, g_far, rows, sems)
    start_attention_copies(layer, place, wqkv, wproj, None, pieces, wq, wp, sems)
    for window in range(3):
        masks[window] = window_masks(window)
    wait_all(copies)

    def chunk_step(chunk, carry):
        wait_chunk(chunk, (wq, wp), sems)
        gmix[...] = dot_nt(rows[...], wp[chunk]).astype(BF16)
        first = first_head_lanes()
        scale = HEAD_DIM**-0.5
        sums = jnp.zeros((1, 384), F32)
        for block in range(2):
            outs = []
            for window in range(3):
                span = pl.ds(block * ROWS + window * WIN_STEP, WIN)
                query = stack_heads(qkv_ref[chunk, span, 0:128], first)
                key = qkv_ref[chunk, span, 128:256]
                grad = stack_heads(gmix[span, :], first)
                probs = window_probs(query, key, masks[window], window_rows_ok(window))
                gprobs = dot_nt(grad, qkv_ref[chunk, span, 256:384])
                gvalue = dot_tn(probs.astype(BF16), grad)
                inner = jnp.sum(gprobs * probs, axis=-1, keepdims=True)
                gscores = (probs * (gprobs - inner)).astype(BF16)
                gquery = dot_nn(gscores, key) * scale
                gkey = dot_tn(gscores, query) * scale
                outs.append((jnp.where(first, gquery[:WIN], gquery[WIN:]), gkey, gvalue))
            joined = jnp.concatenate(
                [join_windows([out[item] for out in outs]) for item in range(3)], axis=1
            ).astype(BF16)
            dqkv_ref[chunk, pl.ds(block * ROWS, ROWS), :] = joined
            sums += jnp.sum(joined.astype(F32), axis=0, keepdims=True)
        sums_ref[chunk] = jnp.broadcast_to(sums, (8, 384))
        part = dot_nt(dqkv_ref[chunk], wq[chunk])

        @pl.when(chunk == 0)
        def _():
            total[...] = part

        @pl.when(chunk > 0)
        def _():
            total[...] += part

        return carry

    lax.fori_loop(0, 4, chunk_step, 0)
    d_own[...] = total[0:ROWS, :].astype(BF16)
    d_far[...] = total[ROWS:, :].astype(BF16)


def run_attention_backward(layer, place, g_own, g_far, qkv, weights, pieces):
    rows, width = 2 * ROWS, g_own.shape[1]
    return pl.pallas_call(
        functools.partial(attention_backward_kernel, layer),
        out_shape=(
            jax.ShapeDtypeStruct((4, rows, 384), BF16),
            jax.ShapeDtypeStruct((4, 8, 384), F32),
            jax.ShapeDtypeStruct((ROWS, width), BF16),
            jax.ShapeDtypeStruct((ROWS, width), BF16),
        ),
        in_specs=[SM, HB, HB, VM, HB, HB] + [HB] * 12,
        out_specs=(VM, VM, VM, VM),
        scratch_shapes=[
            pltpu.VMEM((4, width, 384), BF16),
            pltpu.VMEM((4, 128, width), BF16),
            pltpu.VMEM((rows, width), BF16),
            pltpu.VMEM((rows, width), F32),
            pltpu.VMEM((3, 2 * WIN, WIN), F32),
            pltpu.VMEM((rows, 128), BF16),
            pltpu.SemaphoreType.DMA((4, 4)),
        ],
        **params(23),
    )(place, g_own, g_far, qkv, *weights[:2], *pieces)


def gelu_pair(u):
    size = jnp.abs(u) * (0.5**0.5)
    t = 1.0 / (1.0 + 0.3275911 * size)
    poly = t * (
        0.254829592
        + t * (-0.284496736 + t * (1.421413741 + t * (-1.453152027 + t * 1.061405429)))
    )
    bell = jnp.exp(-0.5 * u * u)
    tail = 0.5 * poly * bell
    phi = jnp.where(u >= 0.0, 1.0 - tail, tail)
    return u * phi, phi + u * bell * 0.3989422804014327


def mlp_forward_kernel(
    layer, place, a_own, a_far, first, second, bias_ref, *refs
):
    pieces = refs[:12]
    h_ref, slope_ref, m_own, m_far, w1, w2, bs, rows, total, sems = refs[12:]
    copies = start_rows(a_own, a_far, rows, sems)
    start_mlp_copies(layer, place, first, second, bias_ref, pieces, w1, w2, sems, bs)
    wait_all(copies)

    def chunk_step(chunk, carry):
        wait_chunk(chunk, (w1, w2), sems)
        wait_bias(chunk, bs, sems)
        bias = jnp.sum(bs[chunk].astype(F32), axis=0, keepdims=True)
        value, slope = gelu_pair(dot_nn(rows[...], w1[chunk]) + bias)
        h_ref[chunk] = value.astype(BF16)
        slope_ref[chunk] = slope.astype(BF16)
        part = dot_nn(h_ref[chunk], w2[chunk])

        @pl.when(chunk == 0)
        def _():
            total[...] = part

        @pl.when(chunk > 0)
        def _():
            total[...] += part

        return carry

    lax.fori_loop(0, 4, chunk_step, 0)
    m_own[...] = total[0:ROWS, :].astype(BF16)
    m_far[...] = total[ROWS:, :].astype(BF16)


def run_mlp_forward(layer, place, a_own, a_far, weights, pieces):
    rows, width = 2 * ROWS, a_own.shape[1]
    return pl.pallas_call(
        functools.partial(mlp_forward_kernel, layer),
        out_shape=(
            jax.ShapeDtypeStruct((4, rows, 512), BF16),
            jax.ShapeDtypeStruct((4, rows, 512), BF16),
            jax.ShapeDtypeStruct((ROWS, width), BF16),
            jax.ShapeDtypeStruct((ROWS, width), BF16),
        ),
        in_specs=[SM, HB, HB, HB, HB, VM] + [HB] * 12,
        out_specs=(VM, VM, VM, VM),
        scratch_shapes=[
            pltpu.VMEM((4, width, 512), BF16),
            pltpu.VMEM((4, 512, width), BF16),
            pltpu.VMEM((4, 16, 512), BF16),
            pltpu.VMEM((rows, width), BF16),
            pltpu.VMEM((rows, width), F32),
            pltpu.SemaphoreType.DMA((4, 4)),
        ],
        **params(17),
    )(place, a_own, a_far, *weights, *pieces)


def mlp_backward_kernel(
    layer, place, g_own, g_far, slope_ref, first, second, *refs
):
    pieces = refs[:12]
    du_ref, sums_ref, d_own, d_far, w1, w2, rows, total, sems = refs[12:]
    copies = start_rows(g_own, g_far, rows, sems)
    start_mlp_copies(layer, place, first, second, None, pieces, w1, w2, sems)
    wait_all(copies)

    def chunk_step(chunk, carry):
        wait_chunk(chunk, (w1, w2), sems)
        grad = dot_nt(rows[...], w2[chunk]) * slope_ref[chunk].astype(F32)
        grad = grad.astype(BF16)
        du_ref[chunk] = grad
        sums_ref[chunk] = jnp.broadcast_to(
            jnp.sum(grad.astype(F32), axis=0, keepdims=True), (8, 512)
        )
        part = dot_nt(du_ref[chunk], w1[chunk])

        @pl.when(chunk == 0)
        def _():
            total[...] = part

        @pl.when(chunk > 0)
        def _():
            total[...] += part

        return carry

    lax.fori_loop(0, 4, chunk_step, 0)
    d_own[...] = total[0:ROWS, :].astype(BF16)
    d_far[...] = total[ROWS:, :].astype(BF16)


def run_mlp_backward(layer, place, g_own, g_far, slope, weights, pieces):
    rows, width = 2 * ROWS, g_own.shape[1]
    return pl.pallas_call(
        functools.partial(mlp_backward_kernel, layer),
        out_shape=(
            jax.ShapeDtypeStruct((4, rows, 512), BF16),
            jax.ShapeDtypeStruct((4, 8, 512), F32),
            jax.ShapeDtypeStruct((ROWS, width), BF16),
            jax.ShapeDtypeStruct((ROWS, width), BF16),
        ),
        in_specs=[SM, HB, HB, VM, HB, HB] + [HB] * 12,
        out_specs=(VM, VM, VM, VM),
        scratch_shapes=[
            pltpu.VMEM((4, width, 512), BF16),
            pltpu.VMEM((4, 512, width), BF16),
            pltpu.VMEM((rows, width), BF16),
            pltpu.VMEM((rows, width), F32),
            pltpu.SemaphoreType.DMA((4, 4)),
        ],
        **params(13),
    )(place, g_own, g_far, slope, *weights[:2], *pieces)


def weight_grad_kernel(
    place, x1_own, x1_far, y1_ref, x2_own, x2_far, y2_ref,
    near_ref, away_ref, send_ref, rows, turned,
):
    span1 = y1_ref.shape[2]
    for index, (own, far) in enumerate(((x1_own, x1_far), (x2_own, x2_far))):
        rows[0:ROWS, :] = own[...]
        rows[ROWS:, :] = far[...]
        for c_side in range(2):
            for y_side in range(2):
                start = (place[SIDE] ^ y_side) * 512 + (place[CORE] ^ c_side) * 128
                start = pl.multiple_of(start, 128)
                cols = jnp.concatenate(
                    [rows[:, pl.ds(start, 128)], rows[:, pl.ds(start + 256, 128)]], axis=1
                )
                turned[index, 2 * c_side + y_side] = cols.T

    def chunk_step(chunk, carry):
        for slot, out in enumerate((near_ref, away_ref, send_ref.at[0], send_ref.at[1])):
            out[chunk, :, 0:span1] = dot_nn(turned[0, slot], y1_ref[chunk]).astype(BF16)
            out[chunk, :, span1:] = dot_nn(turned[1, slot], y2_ref[chunk]).astype(BF16)
        return carry

    lax.fori_loop(0, 4, chunk_step, 0)


def run_weight_grad(place, x1, y1, x2, y2):
    rows, width = 2 * ROWS, x1[0].shape[1]
    span = y1.shape[2] + y2.shape[2]
    half = jax.ShapeDtypeStruct((4, width // 4, span), BF16)
    both = jax.ShapeDtypeStruct((2, 4, width // 4, span), BF16)
    return pl.pallas_call(
        weight_grad_kernel,
        out_shape=(half, half, both),
        in_specs=[SM, VM, VM, VM, VM, VM, VM],
        out_specs=(VM, VM, VM),
        scratch_shapes=[
            pltpu.VMEM((rows, width), BF16),
            pltpu.VMEM((2, 4, width // 4, rows), BF16),
        ],
        **params(14),
    )(place, *x1, y1, *x2, y2)


def add_core_kernel(near, away, got, near_out, away_out):
    near_out[...] = (near[...].astype(F32) + got[0].astype(F32)).astype(BF16)
    away_out[...] = (away[...].astype(F32) + got[1].astype(F32)).astype(BF16)


def run_add_core(near, away, got):
    chunks, rows, span = near.shape
    one = pl.BlockSpec((1, rows, span), lambda step: (step, 0, 0))
    two = pl.BlockSpec((2, 1, rows, span), lambda step: (0, step, 0, 0))
    shape = jax.ShapeDtypeStruct(near.shape, BF16)
    return pl.pallas_call(
        add_core_kernel,
        grid=(chunks,),
        out_shape=(shape, shape),
        in_specs=[one, one, two],
        out_specs=(one, one),
        **params(4),
    )(near, away, got)


def add_side_kernel(near, got, *outs):
    for step, out in enumerate(outs):
        out[...] = (near[step].astype(F32) + got[step].astype(F32)).astype(out.dtype)


def run_add_side(near, got):
    chunks, rows, span = near.shape
    return pl.pallas_call(
        add_side_kernel,
        out_shape=tuple(
            jax.ShapeDtypeStruct((rows, span), BF16 if step else F32) for step in range(chunks)
        ),
        in_specs=[VM, VM],
        out_specs=(VM,) * chunks,
        **params(3),
    )(near, got)


def add_depth_kernel(place, first, second, third, fourth, stay, move):
    total = first[...]
    for part in (second, third, fourth):
        total += part[...].astype(F32)
    half = total.shape[0] // 2
    low, high = total[:half], total[half:]
    even = place[PAIR] == 0
    stay[...] = jnp.where(even, low, high).astype(BF16)
    move[...] = jnp.where(even, high, low).astype(BF16)


def run_add_depth(place, parts):
    rows, span = parts[0].shape
    shape = jax.ShapeDtypeStruct((rows // 2, span), BF16)
    return pl.pallas_call(
        add_depth_kernel,
        out_shape=(shape, shape),
        in_specs=[SM] + [VM] * 4,
        out_specs=(VM, VM),
        **params(2),
    )(place, *parts)


def finish_kernel(place, *refs):
    layers = (len(refs) - 4) // 4
    ins, (qkv, proj, fc1, fc2) = refs[: 4 * layers], refs[4 * layers :]
    for layer in range(layers):
        for side in range(2):
            attn, mlp = ins[4 * layer + side], ins[4 * layer + 2 + side]
            pair = place[PAIR] if side == 0 else 1 - place[PAIR]
            narrow, wide = aligned(pair, 128), aligned(pair, 512)
            for item in range(3):
                qkv[layer, item, :, pl.ds(narrow, 128)] = attn[
                    :, item * 128 : item * 128 + 128
                ].astype(F32)
            proj[layer, pl.ds(narrow, 128), :] = attn[:, 384:512].astype(F32).T
            fc1[layer, :, pl.ds(wide, 512)] = mlp[:, 0:512].astype(F32)
            fc2[layer, pl.ds(wide, 512), :] = mlp[:, 512:1024].astype(F32).T


def run_finish(place, parts):
    rows = parts[0].shape[0]
    return pl.pallas_call(
        finish_kernel,
        out_shape=(
            jax.ShapeDtypeStruct((2, 3, rows, 256), F32),
            jax.ShapeDtypeStruct((2, 256, rows), F32),
            jax.ShapeDtypeStruct((2, rows, 1024), F32),
            jax.ShapeDtypeStruct((2, 1024, rows), F32),
        ),
        in_specs=[SM] + [VM] * len(parts),
        out_specs=(VM,) * 4,
        **params(4),
    )(place, *parts)


def on_device(n_dp, n_mp, *args):
    (
        images_in, out_cotangent, norm1_gain, norm1_bias, qkv_weight, qv_bias, proj_weight,
        proj_bias, norm2_gain, norm2_bias, fc1_weight, fc1_bias, fc2_weight, fc2_bias,
    ) = args
    images, seq, width = images_in.shape
    layers = qkv_weight.shape[0]
    mine = images // n_mp
    count = mine * seq

    place = lax.axis_index("dp")
    depth = lax.axis_index("mp")
    core, pair, side = place & 1, (place >> 1) & 1, (place >> 2) & 1
    here = jnp.stack(
        [
            side, core, pair, depth,
            side * 2 + core, (1 - side) * 2 + core, side * 2 + 1 - core, (1 - side) * 2 + 1 - core,
        ]
    ).astype(jnp.int32)

    def swap(value, bit):
        return lax.ppermute(value, "dp", [(index, index ^ bit) for index in range(n_dp)])

    def shift(value, step):
        return lax.ppermute(
            value, "mp", [(index, (index + step) % n_mp) for index in range(n_mp)]
        )

    def after(value, *others):
        return lax.optimization_barrier((value, *others))[0]

    def shifts(piece):
        return {step: shift(piece, step) for step in (1, 3, 2)}

    def spread(gathered):
        out = []
        for step in range(1, n_mp):
            same = gathered[step]
            other = swap(same, 4)
            out += [same, other, swap(same, 1), swap(other, 1)]
        return out

    def sum_everywhere(value):
        for bit in range(n_dp.bit_length() - 1):
            value = value + swap(value, 1 << bit)
        for bit in range(n_mp.bit_length() - 1):
            pairs = [(index, index ^ (1 << bit)) for index in range(n_mp)]
            value = value + lax.ppermute(value, "mp", pairs)
        return value

    wqkv = qkv_weight.transpose(0, 2, 1, 3)
    attn_weights = (wqkv, proj_weight, qv_bias)
    mlp_weights = (fc1_weight, fc2_weight, fc1_bias)
    packed = run_pack(here, wqkv, proj_weight, fc1_weight, fc2_weight, qv_bias, fc1_bias)
    moved = shifts(packed[0])
    attn_pieces, mlp_pieces = [spread(moved)], []

    stream, normed = run_enter(here, images_in, mine, norm1_gain[0], norm1_bias[0])
    grad, grad_b, fc2_sum = run_enter_back(here, out_cotangent, mine)
    grad_b_far = swap(grad_b, 2)

    saved = []
    for layer in range(layers):
        moved = shifts(after(packed[2 * layer + 1], moved[2]))
        normed_far = swap(normed, 2)
        if layer == 0:
            normed = after(normed, moved[1], grad_b_far)
            mlp_pieces.append(spread(moved))
        qkv, mixed, own, away = run_attention_forward(
            layer, here, normed, normed_far, attn_weights, attn_pieces[layer]
        )
        if layer > 0:
            mlp_pieces.append(spread({step: after(moved[step], own) for step in moved}))
        middle, normed2 = run_residual_norm(
            stream, own, swap(away, 2), proj_bias[layer], norm2_gain[layer], norm2_bias[layer]
        )
        normed2_far = swap(normed2, 2)
        active, slope, own, away = run_mlp_forward(
            layer, here, normed2, normed2_far, mlp_weights, mlp_pieces[layer]
        )
        if layer + 1 < layers:
            moved = shifts(after(packed[2 * layer + 2], moved[2]))
            attn_pieces.append(spread({step: after(moved[step], own) for step in moved}))
        saved.append(
            (stream, (normed, normed_far), qkv, mixed, middle, (normed2, normed2_far), active, slope)
        )
        if layer + 1 < layers:
            stream, normed = run_residual_norm(
                middle, own, swap(away, 2), fc2_bias[layer], norm1_gain[layer + 1],
                norm1_bias[layer + 1],
            )
        else:
            last = run_residual(middle, own, swap(away, 2), fc2_bias[layer])
    block_out = run_leave(lax.all_gather(last, "mp"), seq, mine, BF16)

    class Sum:
        def start(self, x1, y1, x2, y2):
            self.near, self.away, send = run_weight_grad(here, x1, y1, x2, y2)
            self.got = swap(send, 1)
            return self.near

        def add_core(self):
            self.near, away = run_add_core(self.near, self.away, self.got)
            self.got = swap(away, 4)
            return self.near

        def add_side(self):
            parts = run_add_side(self.near, self.got)
            self.parts = [parts[0]] + [shift(parts[step], -step) for step in range(1, n_mp)]
            return parts[0]

        def add_depth(self):
            self.stay, move = run_add_depth(here, self.parts)
            if n_dp == 8:
                move = swap(move, 2)
            self.move = move
            return self.stay

    sums = {(layer, kind): Sum() for layer in range(layers) for kind in ("attn", "mlp")}
    small = [None] * layers
    fc2_sum = fc2_sum[0]
    for layer in reversed(range(layers)):
        stream, normed, qkv, mixed, middle, normed2, active, slope = saved[layer]
        mlp, attn = sums[layer, "mlp"], sums[layer, "attn"]
        upper_mlp, upper_attn = sums.get((layer + 1, "mlp")), sums.get((layer + 1, "attn"))
        if upper_attn:
            grad_b = after(grad_b, upper_attn.add_core())
        du, fc1_sum, own, away = run_mlp_backward(
            layer, here, grad_b, grad_b_far, slope, mlp_weights, mlp_pieces[layer]
        )
        waits = [mlp.start(normed2, du, (grad_b, grad_b_far), active)]
        if upper_attn:
            waits.append(upper_attn.add_side())
        grad, grad_b, sums2 = run_norm_back(
            after(grad, *waits), own, swap(away, 2), middle, norm2_gain[layer]
        )
        grad_b_far = swap(grad_b, 2)
        waits = [mlp.add_core()]
        if upper_mlp:
            waits.append(upper_mlp.add_depth())
        grad_b = after(grad_b, *waits)
        dqkv, qv_sum, own, away = run_attention_backward(
            layer, here, grad_b, grad_b_far, qkv, attn_weights, attn_pieces[layer]
        )
        waits = [attn.start(normed, dqkv, (grad_b, grad_b_far), mixed), mlp.add_side()]
        if upper_attn:
            waits.append(upper_attn.add_depth())
        grad, grad_b, sums1 = run_norm_back(
            after(grad, *waits), own, swap(away, 2), stream, norm1_gain[layer]
        )
        if layer:
            grad_b_far = swap(grad_b, 2)

        def by_quarter(value):
            quarter = lax.broadcasted_iota(jnp.int32, (n_mp, 1, 1), 0)
            half = lax.broadcasted_iota(jnp.int32, (1, 2, 1), 1)
            full = sum(
                jnp.where(quarter == (depth - step) % n_mp, value[step][None, None, :], 0.0)
                for step in range(n_mp)
            )
            return jnp.where(half == pair, full, 0.0)

        qv = qv_sum[:, 0]
        small[layer] = (
            jnp.stack([sums1[0], sums1[1], sums2[2], sums2[0], sums2[1], fc2_sum]),
            jnp.stack([by_quarter(qv[:, 0:128]), by_quarter(qv[:, 256:384])], axis=1),
            by_quarter(fc1_sum[:, 0]),
        )
        fc2_sum = sums1[2]

    input_grad = run_leave(lax.all_gather(grad_b, "mp"), seq, mine, F32)
    first = sums[0, "attn"]
    first.add_core()
    first.add_side()
    sums[0, "mlp"].add_depth()
    first.add_depth()

    stacked = [jnp.stack([small[layer][item] for layer in range(layers)]) for item in range(3)]
    flat = sum_everywhere(jnp.concatenate([part.reshape(-1, 128) for part in stacked]))
    ends = [part.size // 128 for part in stacked]
    rows = flat[: ends[0]].reshape(stacked[0].shape)
    qv = flat[ends[0] : ends[0] + ends[1]].reshape(stacked[1].shape)
    fc1 = flat[ends[0] + ends[1] :].reshape(stacked[2].shape)
    qv = lax.dynamic_index_in_dim(qv, depth, 1, keepdims=False).reshape(layers, 2, -1)
    fc1 = lax.dynamic_index_in_dim(fc1, depth, 1, keepdims=False).reshape(layers, -1)

    order = [sums[layer, kind] for layer in range(layers) for kind in ("attn", "mlp")]
    if n_dp == 8:
        parts = [part for item in order for part in (item.stay, item.move)]
    else:
        parts = [part for item in order for part in spread_rows(item, n_dp, place, pair)]
    g_qkv, g_proj, g_fc1, g_fc2 = run_finish(here, parts)
    return (
        block_out, input_grad, rows[:, 0], rows[:, 1], g_qkv.transpose(0, 2, 1, 3), qv, g_proj,
        rows[:, 2], rows[:, 3], rows[:, 4], g_fc1, fc1, g_fc2, rows[:, 5],
    )


def spread_rows(item, n_dp, place, pair):
    far = n_dp // 8
    value = jnp.stack(
        [jnp.where(pair == 0, item.stay, item.move), jnp.where(pair == 0, item.move, item.stay)]
    ).astype(F32)
    groups = [[8 * group + index for group in range(far)] for index in range(8)]
    value = lax.psum(value, "dp", axis_index_groups=groups)
    groups = [[8 * group + index for index in range(8)] for group in range(far)]
    value = lax.all_gather(value, "dp", axis_index_groups=groups)
    rows, span = value.shape[2:]
    value = value.reshape(2, 2, 2, 2, rows, span).transpose(0, 3, 2, 4, 1, 5)
    value = value.reshape(8 * rows, 2, span)
    value = lax.dynamic_slice_in_dim(value, place * (8 * rows // n_dp), 8 * rows // n_dp, 0)
    mine = lax.dynamic_index_in_dim(value, pair, 1, keepdims=False)
    other = lax.dynamic_index_in_dim(value, 1 - pair, 1, keepdims=False)
    return mine, other


def solution(mesh):
    n_dp, n_mp = mesh.shape["dp"], mesh.shape["mp"]
    return jax.shard_map(
        functools.partial(on_device, n_dp, n_mp),
        mesh=mesh,
        in_specs=(
            P("dp", None, None),
            P("dp", None, None),
            P(),
            P(),
            P(None, None, None, "mp"),
            P(None, None, "mp"),
            P(None, "mp", None),
            P(),
            P(),
            P(),
            P(None, None, "mp"),
            P(None, "mp"),
            P(None, "mp", None),
            P(),
        ),
        out_specs=(
            P("dp", None, None),
            P("dp", None, None),
            P(),
            P(),
            P(None, "dp", None, "mp"),
            P(None, None, "mp"),
            P(None, "mp", "dp"),
            P(),
            P(),
            P(),
            P(None, "dp", "mp"),
            P(None, "mp"),
            P(None, "mp", "dp"),
            P(),
        ),
        check_vma=False,
    )
```

```python
import functools

import jax
import jax.numpy as jnp
from jax import lax
from jax.experimental import pallas as pl
from jax.experimental.pallas import tpu as pltpu
from jax.sharding import Mesh
from jax.sharding import PartitionSpec as P

HEAD_DIM = 64
EPS = 1e-06
F32 = jnp.float32
BF16 = jnp.bfloat16
ROWS = 304
WIN = 112
WIN_STEP = 96
BIG_NEG = -1e30
VMEM_LIMIT = 60 * 1024 * 1024


def dot_nn(a, b):
    return lax.dot_general(a, b, (((1,), (0,)), ((), ())), preferred_element_type=F32)


def dot_nt(a, b):
    return lax.dot_general(a, b, (((1,), (1,)), ((), ())), preferred_element_type=F32)


def dot_tn(a, b):
    return lax.dot_general(a, b, (((0,), (0,)), ((), ())), preferred_element_type=F32)


def params(micros):
    return dict(
        compiler_params=pltpu.CompilerParams(vmem_limit_bytes=VMEM_LIMIT),
        cost_estimate=pl.CostEstimate(
            flops=int(micros * 4e9), bytes_accessed=0, transcendentals=0
        ),
    )


VM = pl.BlockSpec(memory_space=pltpu.VMEM)
SM = pl.BlockSpec(memory_space=pltpu.SMEM)
HB = pl.BlockSpec(memory_space=pl.ANY)


def layer_norm(x, gain, bias):
    mean = jnp.mean(x, axis=-1, keepdims=True)
    centered = x - mean
    variance = jnp.mean(centered * centered, axis=-1, keepdims=True)
    return centered * lax.rsqrt(variance + EPS) * gain + bias


def own_selector(place, seq, mine):
    images = 4 * mine
    row = lax.broadcasted_iota(jnp.int32, (ROWS, images * seq), 0)
    col = lax.broadcasted_iota(jnp.int32, (ROWS, images * seq), 1)
    token = col // images
    image = col - token * images - place[DEPTH] * mine
    hit = (image >= 0) & (image < mine) & (row == image * seq + token)
    return jnp.where(hit, 1.0, 0.0).astype(BF16)


def enter_kernel(seq, mine, place, x_ref, gain_ref, beta_ref, x1_ref, a_ref):
    x = dot_nn(own_selector(place, seq, mine), x_ref[...])
    x1_ref[...] = x
    a_ref[...] = layer_norm(x, gain_ref[...], beta_ref[...]).astype(BF16)


def enter_back_kernel(seq, mine, place, x_ref, g_ref, gb_ref, sum_ref):
    g = dot_nn(own_selector(place, seq, mine), x_ref[...])
    g_ref[...] = g
    gb_ref[...] = g.astype(BF16)
    sum_ref[...] = jnp.broadcast_to(jnp.sum(g, axis=0, keepdims=True), sum_ref.shape)


def leave_kernel(seq, mine, place, *refs):
    parts, out_ref = refs[:-1], refs[-1]
    images = 4 * mine
    count = images * seq
    row = lax.broadcasted_iota(jnp.int32, (count, ROWS), 0)
    col = lax.broadcasted_iota(jnp.int32, (count, ROWS), 1)
    token = row // images
    want = row - token * images
    total = None
    for step, part_ref in zip((0, 1, 3, 2), parts):
        image = want - ((place[DEPTH] - step) & 3) * mine
        hit = (image >= 0) & (image < mine) & (col == image * seq + token)
        part = dot_nn(jnp.where(hit, 1.0, 0.0).astype(BF16), part_ref[...])
        total = part if total is None else total + part
    out_ref[...] = total.astype(out_ref.dtype)


def residual_norm_kernel(
    x_ref, own_ref, far_ref, bias_ref, gain_ref, beta_ref, x1_ref, a_ref, far, sem
):
    copy = pltpu.make_async_copy(far_ref, far, sem)
    copy.start()
    keep = lax.broadcasted_iota(jnp.int32, (ROWS, 1), 0) < 300
    bias = jnp.where(keep, bias_ref[...], 0.0)
    copy.wait()
    x1 = x_ref[...] + own_ref[...].astype(F32) + far[...].astype(F32) + bias
    x1_ref[...] = x1
    a_ref[...] = layer_norm(x1, gain_ref[...], beta_ref[...]).astype(BF16)


def residual_kernel(x_ref, own_ref, far_ref, bias_ref, x1_ref, far, sem):
    copy = pltpu.make_async_copy(far_ref, far, sem)
    copy.start()
    copy.wait()
    x1 = x_ref[...] + own_ref[...].astype(F32) + far[...].astype(F32) + bias_ref[...]
    x1_ref[...] = x1.astype(BF16)


def norm_back_kernel(
    g_ref, own_ref, far_ref, x_ref, gain_ref, g1_ref, g1b_ref, sums_ref, far, sem
):
    copy = pltpu.make_async_copy(far_ref, far, sem)
    copy.start()
    x = x_ref[...]
    mean = jnp.mean(x, axis=-1, keepdims=True)
    centered = x - mean
    variance = jnp.mean(centered * centered, axis=-1, keepdims=True)
    inverse = lax.rsqrt(variance + EPS)
    xhat = centered * inverse
    copy.wait()
    da = own_ref[...].astype(F32) + far[...].astype(F32)
    inner = da * gain_ref[...]
    mean_inner = jnp.mean(inner, axis=-1, keepdims=True)
    mean_proj = jnp.mean(inner * xhat, axis=-1, keepdims=True)
    g1 = g_ref[...] + inverse * (inner - mean_inner - xhat * mean_proj)
    g1_ref[...] = g1
    g1b_ref[...] = g1.astype(BF16)
    sums_ref[...] = jnp.zeros(sums_ref.shape, F32)
    sums_ref[0:1, :] = jnp.sum(da * xhat, axis=0, keepdims=True)
    sums_ref[1:2, :] = jnp.sum(da, axis=0, keepdims=True)
    sums_ref[2:3, :] = jnp.sum(g1, axis=0, keepdims=True)


def run_enter(place, images, mine, gain, beta):
    count, seq, width = images.shape
    flat = images.transpose(1, 0, 2).reshape(count * seq, width)
    return pl.pallas_call(
        functools.partial(enter_kernel, seq, mine),
        out_shape=(
            jax.ShapeDtypeStruct((ROWS, width), F32),
            jax.ShapeDtypeStruct((ROWS, width), BF16),
        ),
        in_specs=[SM, VM, VM, VM],
        out_specs=(VM, VM),
        **params(5),
    )(place, flat, gain[None], beta[None])


def run_enter_back(place, images, mine):
    count, seq, width = images.shape
    flat = images.transpose(1, 0, 2).reshape(count * seq, width)
    return pl.pallas_call(
        functools.partial(enter_back_kernel, seq, mine),
        out_shape=(
            jax.ShapeDtypeStruct((ROWS, width), F32),
            jax.ShapeDtypeStruct((ROWS, width), BF16),
            jax.ShapeDtypeStruct((8, width), F32),
        ),
        in_specs=[SM, VM],
        out_specs=(VM, VM, VM),
        **params(5),
    )(place, flat)


def run_leave(place, parts, seq, mine, dtype):
    images, width = 4 * mine, parts[0].shape[1]
    flat = pl.pallas_call(
        functools.partial(leave_kernel, seq, mine),
        out_shape=jax.ShapeDtypeStruct((images * seq, width), dtype),
        in_specs=[SM, VM, VM, VM, VM],
        out_specs=VM,
        **params(9),
    )(place, *parts)
    return flat.reshape(seq, images, width).transpose(1, 0, 2)


def run_residual_norm(x, own, far, bias, gain, beta):
    return pl.pallas_call(
        residual_norm_kernel,
        out_shape=(
            jax.ShapeDtypeStruct(x.shape, F32),
            jax.ShapeDtypeStruct(x.shape, BF16),
        ),
        in_specs=[VM, VM, HB, VM, VM, VM],
        out_specs=(VM, VM),
        scratch_shapes=[pltpu.VMEM((ROWS, x.shape[1]), BF16), pltpu.SemaphoreType.DMA],
        **params(3),
    )(x, own, far, bias[None], gain[None], beta[None])


def run_residual(x, own, far, bias):
    return pl.pallas_call(
        residual_kernel,
        out_shape=jax.ShapeDtypeStruct(x.shape, BF16),
        in_specs=[VM, VM, HB, VM],
        out_specs=VM,
        scratch_shapes=[pltpu.VMEM((ROWS, x.shape[1]), BF16), pltpu.SemaphoreType.DMA],
        **params(2),
    )(x, own, far, bias[None])


def run_norm_back(g, own, far, x, gain):
    return pl.pallas_call(
        norm_back_kernel,
        out_shape=(
            jax.ShapeDtypeStruct(x.shape, F32),
            jax.ShapeDtypeStruct(x.shape, BF16),
            jax.ShapeDtypeStruct((8, x.shape[1]), F32),
        ),
        in_specs=[VM, VM, HB, VM, VM],
        out_specs=(VM, VM, VM),
        scratch_shapes=[pltpu.VMEM((ROWS, x.shape[1]), BF16), pltpu.SemaphoreType.DMA],
        **params(4),
    )(g, own, far, x, gain[None])


SIDE, CORE, PAIR, DEPTH, PARTS = 0, 1, 2, 3, 4

ATTN_ROWS, MLP_ROWS = 272, 528
ATTN_SPAN, MLP_SPAN = pl.ds(MLP_ROWS, ATTN_ROWS), pl.ds(0, MLP_ROWS)


def exact_rows(bias):
    high = bias.astype(BF16)
    rest = bias - high.astype(F32)
    mid = rest.astype(BF16)
    low = (rest - mid.astype(F32)).astype(BF16)
    return jnp.concatenate([high, mid, low, jnp.zeros((13, bias.shape[1]), BF16)], axis=0)


def pack_kernel(
    place, wqkv, wproj, w1, w2, bqv, b1, attn0, middle, mlp1, sems
):
    row = aligned(place[PARTS], 256)
    narrow, wide = aligned(place[PAIR], 128), aligned(place[PAIR], 512)
    copies = []
    mlp0, attn1 = middle.at[0:MLP_ROWS], middle.at[MLP_ROWS:]
    for layer, (attn, mlp) in enumerate(((attn0, mlp0), (attn1, mlp1))):
        for item in range(3):
            copies.append(
                (
                    wqkv.at[layer, item, pl.ds(row, 256), pl.ds(narrow, 128)],
                    attn.at[0:256, pl.ds(item * 128, 128)],
                )
            )
        for half in range(2):
            copies.append(
                (
                    wproj.at[layer, pl.ds(narrow, 128), pl.ds(row + half * 128, 128)],
                    attn.at[pl.ds(half * 128, 128), 384:512],
                )
            )
            copies.append(
                (
                    w2.at[layer, pl.ds(wide + half * 256, 256), pl.ds(row, 256)],
                    mlp.at[256:512, pl.ds(half * 256, 256)],
                )
            )
        copies.append(
            (w1.at[layer, pl.ds(row, 256), pl.ds(wide, 512)], mlp.at[0:256, :])
        )
    copies = [
        pltpu.make_async_copy(src, dst, sems.at[index])
        for index, (src, dst) in enumerate(copies)
    ]
    for copy in copies:
        copy.start()
    for layer, (attn, mlp) in enumerate(((attn0, mlp0), (attn1, mlp1))):
        zero = jnp.zeros((1, 128), F32)
        bias = [bqv[layer, pl.ds(item, 1), pl.ds(narrow, 128)] for item in range(2)]
        attn[256:272, :] = exact_rows(jnp.concatenate([bias[0], zero, bias[1], zero], axis=1))
        mlp[512:528, :] = exact_rows(b1[pl.ds(layer, 1), pl.ds(wide, 512)])
    for copy in copies:
        copy.wait()


def run_pack(place, wqkv, wproj, w1, w2, bqv, b1):
    return pl.pallas_call(
        pack_kernel,
        out_shape=tuple(
            jax.ShapeDtypeStruct((rows, 512), BF16)
            for rows in (ATTN_ROWS, MLP_ROWS + ATTN_ROWS, MLP_ROWS)
        ),
        in_specs=[SM, HB, HB, HB, HB, VM, VM],
        out_specs=(VM, VM, VM),
        scratch_shapes=[pltpu.SemaphoreType.DMA((16,))],
        **params(3),
    )(place, wqkv, wproj, w1, w2, bqv, b1)


def piece_sources(place, pieces, own):
    if not own:
        array, rows = pieces
        return [
            (depth, 2 * side + core, array.at[side, core, depth, rows])
            for depth in range(4)
            for side in range(2)
            for core in range(2)
        ]
    return [
        ((place[DEPTH] - step) & 3, place[PARTS + slot], pieces[4 * step - 4 + slot])
        for step in range(1, 4)
        for slot in range(4)
    ]


def aligned(index, step):
    if isinstance(index, int):
        return index * step
    return pl.multiple_of(index * step, step)


def start_attention_copies(layer, place, wqkv, wproj, bqv, pieces, wq, wp, sems, bs=None):
    own = len(pieces) > 2
    for index, (depth, part, src) in enumerate(piece_sources(place, pieces, own)):
        row = aligned(part, 256)
        pltpu.make_async_copy(
            src.at[0:256, 0:384], wq.at[depth, pl.ds(row, 256), :], sems.at[0, depth]
        ).start()
        for side in range(2):
            pltpu.make_async_copy(
                src.at[pl.ds(side * 128, 128), 384:512],
                wp.at[depth, :, pl.ds(row + side * 128, 128)],
                sems.at[1, depth],
            ).start()
        if bs is not None and index % 4 == 0:
            pltpu.make_async_copy(src.at[256:272, 0:384], bs.at[depth], sems.at[2, depth]).start()
    if own:
        depth, narrow = place[DEPTH], aligned(place[PAIR], 128)
        for item in range(3):
            pltpu.make_async_copy(
                wqkv.at[layer, item, :, pl.ds(narrow, 128)],
                wq.at[depth, :, pl.ds(item * 128, 128)],
                sems.at[0, depth],
            ).start()
        pltpu.make_async_copy(
            wproj.at[layer, pl.ds(narrow, 128), :], wp.at[depth], sems.at[1, depth]
        ).start()
        if bs is not None:
            bias = [bqv[layer, pl.ds(item, 1), pl.ds(narrow, 128)] for item in range(2)]
            zero = jnp.zeros((1, 128), F32)
            bs[depth] = exact_rows(jnp.concatenate([bias[0], zero, bias[1]], axis=1))


def start_mlp_copies(pieces, w1, w2, sems, bs=None):
    for index, (depth, part, src) in enumerate(piece_sources(None, pieces, False)):
        row = part * 256
        pltpu.make_async_copy(
            src.at[0:256, :], w1.at[depth, pl.ds(row, 256), :], sems.at[0, depth]
        ).start()
        for side in range(2):
            pltpu.make_async_copy(
                src.at[256:512, pl.ds(side * 256, 256)],
                w2.at[depth, pl.ds(side * 256, 256), pl.ds(row, 256)],
                sems.at[1, depth],
            ).start()
        if bs is not None and index % 4 == 0:
            pltpu.make_async_copy(src.at[512:528, :], bs.at[depth], sems.at[2, depth]).start()


def start_rows(source, rows, sems):
    copy = pltpu.make_async_copy(source, rows, sems.at[3, 0])
    copy.start()
    return copy


def wait_chunk(chunk, bufs, sems):
    for slot, buf in enumerate(bufs):
        pltpu.make_async_copy(buf.at[chunk], buf.at[chunk], sems.at[slot, chunk]).wait()


def wait_bias(chunk, bs, sems, own=None):
    def wait():
        pltpu.make_async_copy(bs.at[chunk], bs.at[chunk], sems.at[2, chunk]).wait()

    if own is None:
        wait()
    else:
        pl.when(chunk != own)(wait)


def window_masks(window):
    shape = (2 * WIN, WIN)
    row = lax.broadcasted_iota(jnp.int32, shape, 0)
    row = jnp.where(row >= WIN, row - WIN, row) - 4 * window
    col = lax.broadcasted_iota(jnp.int32, shape, 1) - 4 * window
    row_ok = (row >= 0) & (row < 100)
    col_ok = (col >= 0) & (col < 100)
    same = row_ok & col_ok & ((row >= 50) == (col >= 50))
    return jnp.where(same, 0.0, BIG_NEG).astype(F32)


def window_rows_ok(window):
    row = lax.broadcasted_iota(jnp.int32, (2 * WIN, 1), 0)
    row = jnp.where(row >= WIN, row - WIN, row) - 4 * window
    return (row >= 0) & (row < 100)


def stack_heads(values, first):
    zero = jnp.zeros_like(values)
    return jnp.concatenate(
        [jnp.where(first, values, zero), jnp.where(first, zero, values)], axis=0
    )


def first_head_lanes():
    return lax.broadcasted_iota(jnp.int32, (WIN, 2 * HEAD_DIM), 1) < HEAD_DIM


def window_probs(query, key, mask, rows_ok):
    scores = dot_nt(query, key) * (HEAD_DIM**-0.5) + mask
    top = jnp.max(scores, axis=-1, keepdims=True)
    expo = jnp.exp(scores - top)
    total = jnp.sum(expo, axis=-1, keepdims=True)
    return expo * jnp.where(rows_ok, 1.0 / total, 0.0)


def join_windows(parts):
    first, second, third = parts
    over = WIN - WIN_STEP
    return jnp.concatenate(
        [
            first[:WIN_STEP],
            first[WIN_STEP:] + second[:over],
            second[over:WIN_STEP],
            second[WIN_STEP:] + third[:over],
            third[over:],
        ],
        axis=0,
    )


def attention_forward_kernel(layer, count, place, a_ref, wqkv, wproj, bqv, *refs):
    pieces = refs[:count] if count > 1 else (refs[0], ATTN_SPAN)
    qkv_ref, o_ref, r_ref, wq, wp, bs, rows, total, masks, sems = refs[count:]
    own_quarter = place[DEPTH] if count > 1 else None
    copy = start_rows(a_ref, rows, sems)
    start_attention_copies(layer, place, wqkv, wproj, bqv, pieces, wq, wp, sems, bs)
    for window in range(3):
        masks[window] = window_masks(window)
    copy.wait()

    def chunk_step(chunk, carry):
        wait_chunk(chunk, (wq, wp), sems)
        wait_bias(chunk, bs, sems, own_quarter)
        bias = jnp.sum(bs[chunk].astype(F32), axis=0, keepdims=True)
        qkv_ref[chunk] = (dot_nn(rows[...], wq[chunk]) + bias).astype(BF16)
        first = first_head_lanes()
        outs = []
        for window in range(3):
            span = pl.ds(window * WIN_STEP, WIN)
            query = stack_heads(qkv_ref[chunk, span, 0:128], first)
            probs = window_probs(
                query, qkv_ref[chunk, span, 128:256], masks[window], window_rows_ok(window)
            )
            mixed = dot_nn(probs.astype(BF16), qkv_ref[chunk, span, 256:384])
            outs.append(jnp.where(first, mixed[:WIN], mixed[WIN:]))
        o_ref[chunk] = join_windows(outs).astype(BF16)
        add_part(chunk, total, dot_nn(o_ref[chunk], wp[chunk]))
        return carry

    lax.fori_loop(0, 4, chunk_step, 0)
    r_ref[...] = total[...].astype(BF16)


def add_part(chunk, total, part):
    @pl.when(chunk == 0)
    def _():
        total[...] = part

    @pl.when(chunk > 0)
    def _():
        total[...] += part


def run_attention_forward(layer, place, rows, weights, pieces):
    width = rows.shape[1]
    return pl.pallas_call(
        functools.partial(attention_forward_kernel, layer, len(pieces)),
        out_shape=(
            jax.ShapeDtypeStruct((4, ROWS, 384), BF16),
            jax.ShapeDtypeStruct((4, ROWS, 128), BF16),
            jax.ShapeDtypeStruct((ROWS, width), BF16),
        ),
        in_specs=[SM, HB, HB, HB, VM] + [HB] * len(pieces),
        out_specs=(VM,) * 3,
        scratch_shapes=[
            pltpu.VMEM((4, width, 384), BF16),
            pltpu.VMEM((4, 128, width), BF16),
            pltpu.VMEM((4, 16, 384), BF16),
            pltpu.VMEM((ROWS, width), BF16),
            pltpu.VMEM((ROWS, width), F32),
            pltpu.VMEM((3, 2 * WIN, WIN), F32),
            pltpu.SemaphoreType.DMA((4, 4)),
        ],
        **params(7),
    )(place, rows, *weights, *pieces)


def attention_backward_kernel(layer, count, place, g_ref, qkv_ref, wqkv, wproj, *refs):
    pieces = refs[:count] if count > 1 else (refs[0], ATTN_SPAN)
    dqkv_ref, sums_ref, d_ref, wq, wp, rows, total, masks, gmix, sems = refs[count:]
    copy = start_rows(g_ref, rows, sems)
    start_attention_copies(layer, place, wqkv, wproj, None, pieces, wq, wp, sems)
    for window in range(3):
        masks[window] = window_masks(window)
    copy.wait()

    def chunk_step(chunk, carry):
        wait_chunk(chunk, (wq, wp), sems)
        gmix[...] = dot_nt(rows[...], wp[chunk]).astype(BF16)
        first = first_head_lanes()
        scale = HEAD_DIM**-0.5
        outs = []
        for window in range(3):
            span = pl.ds(window * WIN_STEP, WIN)
            query = stack_heads(qkv_ref[chunk, span, 0:128], first)
            key = qkv_ref[chunk, span, 128:256]
            grad = stack_heads(gmix[span, :], first)
            probs = window_probs(query, key, masks[window], window_rows_ok(window))
            gprobs = dot_nt(grad, qkv_ref[chunk, span, 256:384])
            gvalue = dot_tn(probs.astype(BF16), grad)
            inner = jnp.sum(gprobs * probs, axis=-1, keepdims=True)
            gscores = (probs * (gprobs - inner)).astype(BF16)
            gquery = dot_nn(gscores, key) * scale
            gkey = dot_tn(gscores, query) * scale
            outs.append((jnp.where(first, gquery[:WIN], gquery[WIN:]), gkey, gvalue))
        joined = jnp.concatenate(
            [join_windows([out[item] for out in outs]) for item in range(3)], axis=1
        ).astype(BF16)
        dqkv_ref[chunk] = joined
        sums_ref[chunk] = jnp.broadcast_to(
            jnp.sum(joined.astype(F32), axis=0, keepdims=True), (8, 384)
        )
        add_part(chunk, total, dot_nt(dqkv_ref[chunk], wq[chunk]))
        return carry

    lax.fori_loop(0, 4, chunk_step, 0)
    d_ref[...] = total[...].astype(BF16)


def run_attention_backward(layer, place, grad, qkv, weights, pieces):
    width = grad.shape[1]
    return pl.pallas_call(
        functools.partial(attention_backward_kernel, layer, len(pieces)),
        out_shape=(
            jax.ShapeDtypeStruct((4, ROWS, 384), BF16),
            jax.ShapeDtypeStruct((4, 8, 384), F32),
            jax.ShapeDtypeStruct((ROWS, width), BF16),
        ),
        in_specs=[SM, HB, VM, HB, HB] + [HB] * len(pieces),
        out_specs=(VM,) * 3,
        scratch_shapes=[
            pltpu.VMEM((4, width, 384), BF16),
            pltpu.VMEM((4, 128, width), BF16),
            pltpu.VMEM((ROWS, width), BF16),
            pltpu.VMEM((ROWS, width), F32),
            pltpu.VMEM((3, 2 * WIN, WIN), F32),
            pltpu.VMEM((ROWS, 128), BF16),
            pltpu.SemaphoreType.DMA((4, 4)),
        ],
        **params(12),
    )(place, grad, qkv, *weights[:2], *pieces)


def gelu_pair(u):
    size = jnp.abs(u) * (0.5**0.5)
    t = 1.0 / (1.0 + 0.3275911 * size)
    poly = t * (
        0.254829592
        + t * (-0.284496736 + t * (1.421413741 + t * (-1.453152027 + t * 1.061405429)))
    )
    bell = jnp.exp(-0.5 * u * u)
    tail = 0.5 * poly * bell
    phi = jnp.where(u >= 0.0, 1.0 - tail, tail)
    return u * phi, phi + u * bell * 0.3989422804014327


def mlp_forward_kernel(
    a_ref, pieces, h_ref, slope_ref, m_ref, w1, w2, bs, rows, total, sems
):
    copy = start_rows(a_ref, rows, sems)
    start_mlp_copies((pieces, MLP_SPAN), w1, w2, sems, bs)
    copy.wait()

    def chunk_step(chunk, carry):
        wait_chunk(chunk, (w1, w2), sems)
        wait_bias(chunk, bs, sems)
        bias = jnp.sum(bs[chunk].astype(F32), axis=0, keepdims=True)
        value, slope = gelu_pair(dot_nn(rows[...], w1[chunk]) + bias)
        h_ref[chunk] = value.astype(BF16)
        slope_ref[chunk] = slope.astype(BF16)
        add_part(chunk, total, dot_nn(h_ref[chunk], w2[chunk]))
        return carry

    lax.fori_loop(0, 4, chunk_step, 0)
    m_ref[...] = total[...].astype(BF16)


def run_mlp_forward(rows, pieces):
    width = rows.shape[1]
    return pl.pallas_call(
        mlp_forward_kernel,
        out_shape=(
            jax.ShapeDtypeStruct((4, ROWS, 512), BF16),
            jax.ShapeDtypeStruct((4, ROWS, 512), BF16),
            jax.ShapeDtypeStruct((ROWS, width), BF16),
        ),
        in_specs=[HB, HB],
        out_specs=(VM,) * 3,
        scratch_shapes=[
            pltpu.VMEM((4, width, 512), BF16),
            pltpu.VMEM((4, 512, width), BF16),
            pltpu.VMEM((4, 16, 512), BF16),
            pltpu.VMEM((ROWS, width), BF16),
            pltpu.VMEM((ROWS, width), F32),
            pltpu.SemaphoreType.DMA((4, 4)),
        ],
        **params(8),
    )(rows, pieces)


def mlp_backward_kernel(
    g_ref, slope_ref, pieces, du_ref, sums_ref, d_ref, w1, w2, rows, total, sems
):
    copy = start_rows(g_ref, rows, sems)
    start_mlp_copies((pieces, MLP_SPAN), w1, w2, sems)
    copy.wait()

    def chunk_step(chunk, carry):
        wait_chunk(chunk, (w1, w2), sems)
        grad = dot_nt(rows[...], w2[chunk]) * slope_ref[chunk].astype(F32)
        grad = grad.astype(BF16)
        du_ref[chunk] = grad
        sums_ref[chunk] = jnp.broadcast_to(
            jnp.sum(grad.astype(F32), axis=0, keepdims=True), (8, 512)
        )
        add_part(chunk, total, dot_nt(du_ref[chunk], w1[chunk]))
        return carry

    lax.fori_loop(0, 4, chunk_step, 0)
    d_ref[...] = total[...].astype(BF16)


def run_mlp_backward(grad, slope, pieces):
    width = grad.shape[1]
    return pl.pallas_call(
        mlp_backward_kernel,
        out_shape=(
            jax.ShapeDtypeStruct((4, ROWS, 512), BF16),
            jax.ShapeDtypeStruct((4, 8, 512), F32),
            jax.ShapeDtypeStruct((ROWS, width), BF16),
        ),
        in_specs=[HB, VM, HB],
        out_specs=(VM,) * 3,
        scratch_shapes=[
            pltpu.VMEM((4, width, 512), BF16),
            pltpu.VMEM((4, 512, width), BF16),
            pltpu.VMEM((ROWS, width), BF16),
            pltpu.VMEM((ROWS, width), F32),
            pltpu.SemaphoreType.DMA((4, 4)),
        ],
        **params(7),
    )(grad, slope, pieces)


def weight_grad_kernel(
    kind, place, x1_own, x1_far, y1_own, y1_far, x2_own, x2_far, y2_own, y2_far, *refs
):
    (xs, y1, y2, turned, sems), refs = refs[-5:], refs[:-5]
    if kind == "relative":
        near_ref, away_ref, send_ref = refs
        outs = (near_ref, send_ref.at[0], away_ref, send_ref.at[1])
    else:
        outs = [refs[-1].at[side, core] for side in range(2) for core in range(2)]
    top, low = pl.ds(0, ROWS), pl.ds(ROWS, ROWS)
    pairs = [
        (x1_own, xs.at[0, top]),
        (x1_far, xs.at[0, low]),
        (x2_own, xs.at[1, top]),
        (x2_far, xs.at[1, low]),
        (y1_own, y1.at[:, top]),
        (y1_far, y1.at[:, low]),
        (y2_own, y2.at[:, top]),
        (y2_far, y2.at[:, low]),
    ]
    if kind == "extra":
        pairs += [
            (refs[0].at[slot // 2, slot % 2], out.at[:, 256:384, :])
            for slot, out in enumerate(outs)
        ]
    copies = [
        pltpu.make_async_copy(src, dst, sems.at[index]) for index, (src, dst) in enumerate(pairs)
    ]
    for copy in copies:
        copy.start()
    span1, span2 = y1.shape[2], y2.shape[2]
    span = span1 + span2
    for index in range(2):
        copies[2 * index].wait()
        copies[2 * index + 1].wait()
        for slot in range(4):
            side, core = slot // 2, slot % 2
            if kind == "relative":
                start = (place[SIDE] ^ side) * 512 + (place[CORE] ^ core) * 128
                start = pl.multiple_of(start, 128)
            else:
                start = side * 512 + core * 128
            cols = jnp.concatenate(
                [xs[index, :, pl.ds(start, 128)], xs[index, :, pl.ds(start + 256, 128)]], axis=1
            )
            turned[index, slot] = cols.T
    for copy in copies[4:8]:
        copy.wait()

    def chunk_step(chunk, carry):
        for slot, out in enumerate(outs):
            first = dot_nn(turned[0, slot], y1[chunk]).astype(BF16)
            second = dot_nn(turned[1, slot], y2[chunk]).astype(BF16)
            if kind == "compact":
                for side in range(2):
                    rows = slice(128 * side, 128 * side + 128)
                    out[chunk, :, span * side : span * side + span1] = first[rows]
                    out[chunk, :, span * side + span1 : span * side + span] = second[rows]
            else:
                out[chunk, 0:256, 0:span1] = first
                out[chunk, 0:256, span1:span] = second
        return carry

    lax.fori_loop(0, 4, chunk_step, 0)
    for copy in copies[8:]:
        copy.wait()


def run_weight_grad(kind, place, x1, y1, x2, y2, *extra):
    rows, width = 2 * ROWS, x1[0].shape[1]
    span1, span2 = y1[0].shape[2], y2[0].shape[2]
    span = span1 + span2
    if kind == "relative":
        half = jax.ShapeDtypeStruct((4, width // 4, span), BF16)
        shapes = (half, half, jax.ShapeDtypeStruct((2, *half.shape), BF16))
    else:
        shape = {"plain": (256, span), "compact": (128, 2 * span), "extra": (384, span)}[kind]
        shapes = (jax.ShapeDtypeStruct((2, 2, 4, *shape), BF16),)
    return pl.pallas_call(
        functools.partial(weight_grad_kernel, kind),
        out_shape=shapes,
        in_specs=[SM] + [HB] * (8 + len(extra)),
        out_specs=(VM,) * len(shapes),
        scratch_shapes=[
            pltpu.VMEM((2, rows, width), BF16),
            pltpu.VMEM((4, rows, span1), BF16),
            pltpu.VMEM((4, rows, span2), BF16),
            pltpu.VMEM((2, 4, width // 4, rows), BF16),
            pltpu.SemaphoreType.DMA((12,)),
        ],
        **params(14 if span1 > 384 else 10),
    )(place, *x1, *y1, *x2, *y2, *extra)


def add_core_kernel(near, away, got, near_out, away_out):
    near_out[...] = (near[...].astype(F32) + got[0].astype(F32)).astype(BF16)
    away_out[...] = (away[...].astype(F32) + got[1].astype(F32)).astype(BF16)


def run_add_core(near, away, got):
    chunks, rows, span = near.shape
    one = pl.BlockSpec((1, rows, span), lambda step: (step, 0, 0))
    two = pl.BlockSpec((2, 1, rows, span), lambda step: (0, step, 0, 0))
    shape = jax.ShapeDtypeStruct(near.shape, BF16)
    return pl.pallas_call(
        add_core_kernel,
        grid=(chunks,),
        out_shape=(shape, shape),
        in_specs=[one, one, two],
        out_specs=(one, one),
        **params(4),
    )(near, away, got)


def add_side_kernel(place, near, got, *outs):
    for step, out in enumerate(outs):
        depth = (place[DEPTH] + step) & 3
        out[...] = (near[depth].astype(F32) + got[depth].astype(F32)).astype(out.dtype)


def run_add_side(place, near, got):
    chunks, rows, span = near.shape
    return pl.pallas_call(
        add_side_kernel,
        out_shape=tuple(
            jax.ShapeDtypeStruct((rows, span), BF16 if step else F32) for step in range(chunks)
        ),
        in_specs=[SM, VM, VM],
        out_specs=(VM,) * chunks,
        **params(3),
    )(place, near, got)


def add_depth_kernel(place, *refs):
    parts, (stay, move) = refs[:-2], refs[-2:]
    total = parts[0][...].astype(F32)
    for part in parts[1:]:
        total += part[...].astype(F32)
    half = total.shape[0] // 2
    low, high = total[:half], total[half:]
    even = place[PAIR] == 0
    stay[...] = jnp.where(even, low, high).astype(BF16)
    move[...] = jnp.where(even, high, low).astype(BF16)


def run_add_depth(place, parts):
    rows, span = parts[0].shape
    shape = jax.ShapeDtypeStruct((rows // 2, span), BF16)
    return pl.pallas_call(
        add_depth_kernel,
        out_shape=(shape, shape),
        in_specs=[SM] + [VM] * len(parts),
        out_specs=(VM, VM),
        **params(2),
    )(place, *parts)


def collect_kernel(place, fc2_last, *refs):
    out = refs[-1]
    layers = (len(refs) - 1) // 6
    narrow, wide = aligned(place[PAIR], 128), aligned(place[PAIR], 512)
    out[...] = jnp.zeros(out.shape, F32)
    for layer in range(layers):
        sums1, sums2, qv_own, qv_far, fc1_own, fc1_far = refs[6 * layer : 6 * layer + 6]
        row = 12 * layer
        out[row : row + 2, :] = sums1[0:2, :]
        out[row + 2 : row + 3, :] = sums2[2:3, :]
        out[row + 3 : row + 5, :] = sums2[0:2, :]
        above = refs[6 * layer + 6][2:3, :] if layer + 1 < layers else fc2_last[0:1, :]
        out[row + 5 : row + 6, :] = above
        for depth in range(4):
            qv = qv_own[depth, 0:1, :] + qv_far[depth, 0:1, :]
            for item in range(2):
                out[row + 6 + item, pl.ds(depth * 256 + narrow, 128)] = qv[
                    0, 256 * item : 256 * item + 128
                ]
            fc1 = fc1_own[depth, 0:1, :] + fc1_far[depth, 0:1, :]
            out[pl.ds(row + 8 + depth, 1), pl.ds(wide, 512)] = fc1


def run_collect(place, fc2_last, parts):
    layers = len(parts) // 6
    return pl.pallas_call(
        collect_kernel,
        out_shape=jax.ShapeDtypeStruct((12 * layers, 1024), F32),
        in_specs=[SM] + [VM] * (1 + len(parts)),
        out_specs=VM,
        **params(2),
    )(place, fc2_last, *parts)


def release_kernel(place, total, *outs):
    rows, (qv, fc1) = outs[:6], outs[6:]
    quarter = aligned(place[DEPTH], 256)
    for layer in range(fc1.shape[0]):
        for index, out in enumerate(rows):
            out[layer : layer + 1, :] = total[pl.ds(12 * layer + index, 1), :]
        for item in range(2):
            qv[layer, item : item + 1, :] = total[
                pl.ds(12 * layer + 6 + item, 1), pl.ds(quarter, 256)
            ]
        fc1[layer : layer + 1, :] = total[pl.ds(12 * layer + 8 + place[DEPTH], 1), :]


def run_release(place, total):
    layers = total.shape[0] // 12
    row = jax.ShapeDtypeStruct((layers, 1024), F32)
    return pl.pallas_call(
        release_kernel,
        out_shape=(row,) * 6 + (jax.ShapeDtypeStruct((layers, 2, 256), F32), row),
        in_specs=[SM, VM],
        out_specs=(VM,) * 8,
        **params(2),
    )(place, total)


def split_kernel(place, total, *outs):
    even = place[PAIR] == 0
    stay, move = outs[:2]
    low, high = total[0:128, :], total[128:256, :]
    stay[...] = jnp.where(even, low, high)
    move[...] = jnp.where(even, high, low)
    if len(outs) > 2:
        stay, move = outs[2:]
        low, high = total[256:384, 0:512], total[256:384, 512:1024]
        stay[...] = jnp.where(even, low, high)
        move[...] = jnp.where(even, high, low)


def run_split(place, total):
    spans = (1024, 1024, 512, 512) if total.shape[0] > 256 else (1024, 1024)
    return pl.pallas_call(
        split_kernel,
        out_shape=tuple(jax.ShapeDtypeStruct((128, span), BF16) for span in spans),
        in_specs=[SM, VM],
        out_specs=(VM,) * len(spans),
        **params(2),
    )(place, total)


def finish_kernel(place, *refs):
    layers = (len(refs) - 4) // 4
    ins, (qkv, proj, fc1, fc2) = refs[: 4 * layers], refs[4 * layers :]
    for layer in range(layers):
        for side in range(2):
            attn, mlp = ins[4 * layer + side], ins[4 * layer + 2 + side]
            pair = place[PAIR] if side == 0 else 1 - place[PAIR]
            narrow, wide = aligned(pair, 128), aligned(pair, 512)
            for item in range(3):
                qkv[layer, item, :, pl.ds(narrow, 128)] = attn[
                    :, item * 128 : item * 128 + 128
                ].astype(F32)
            proj[layer, pl.ds(narrow, 128), :] = attn[:, 384:512].astype(F32).T
            fc1[layer, :, pl.ds(wide, 512)] = mlp[:, 0:512].astype(F32)
            fc2[layer, pl.ds(wide, 512), :] = mlp[:, 512:1024].astype(F32).T


def run_finish(place, parts):
    rows = parts[0].shape[0]
    return pl.pallas_call(
        finish_kernel,
        out_shape=(
            jax.ShapeDtypeStruct((2, 3, rows, 256), F32),
            jax.ShapeDtypeStruct((2, 256, rows), F32),
            jax.ShapeDtypeStruct((2, rows, 1024), F32),
            jax.ShapeDtypeStruct((2, 1024, rows), F32),
        ),
        in_specs=[SM] + [VM] * len(parts),
        out_specs=(VM,) * 4,
        **params(4),
    )(place, *parts)


def on_device(*args):
    (
        images_in, out_cotangent, norm1_gain, norm1_bias, qkv_weight, qv_bias, proj_weight,
        proj_bias, norm2_gain, norm2_bias, fc1_weight, fc1_bias, fc2_weight, fc2_bias,
    ) = args
    images, seq, _ = images_in.shape
    layers = qkv_weight.shape[0]
    n_far, n_mp = lax.axis_size("far"), lax.axis_size("mp")
    mine = images // n_mp

    side, pair, core = lax.axis_index("y"), lax.axis_index("x"), lax.axis_index("core")
    depth = lax.axis_index("mp")
    here = jnp.stack(
        [
            side, core, pair, depth,
            side * 2 + core, (1 - side) * 2 + core, side * 2 + 1 - core, (1 - side) * 2 + 1 - core,
        ]
    ).astype(jnp.int32)

    def swap(value, axis):
        return lax.ppermute(value, axis, [(0, 1), (1, 0)])

    def shift(value, step):
        return lax.ppermute(
            value, "mp", [(index, (index + step) % n_mp) for index in range(n_mp)]
        )

    def after(value, *others):
        return lax.optimization_barrier((value, *others))[0]

    wqkv = qkv_weight.transpose(0, 2, 1, 3)
    attn_weights = (wqkv, proj_weight, qv_bias)
    packed = run_pack(here, wqkv, proj_weight, fc1_weight, fc2_weight, qv_bias, fc1_bias)
    attn_pieces, mlp_pieces = [[]], []
    moved = []
    for step in (1, 3, 2):
        same = shift(packed[0], step)
        moved.append(same)
        other = swap(same, "y")
        attn_pieces[0].append((step, [same, other, swap(same, "core"), swap(other, "core")]))
    attn_pieces[0] = [array for _, arrays in sorted(attn_pieces[0]) for array in arrays]
    stream, normed = run_enter(here, images_in, mine, norm1_gain[0], norm1_bias[0])
    grad, grad_b, fc2_sum = run_enter_back(here, out_cotangent, mine)
    grad_b_far = swap(grad_b, "x")
    gathered = [*moved, normed, grad_b]
    for index in (1, 2):
        gathered = lax.all_gather(after(packed[index], *gathered), ("y", "core", "mp"))
        value = gathered.reshape(2, 2, n_mp, *gathered.shape[1:])
        mlp_pieces.append(value)
        attn_pieces.append([value])
        gathered = [gathered]

    def both(run, own, far, *waits):
        results = run(own)
        return list(zip(results, run(after(far, *waits) if waits else far)))

    saved = []
    for layer in range(layers):
        normed_far = swap(normed, "x")
        qkv, mixed, part = both(
            lambda rows: run_attention_forward(layer, here, rows, attn_weights, attn_pieces[layer]),
            normed, normed_far,
        )
        middle, normed2 = run_residual_norm(
            stream, part[0], swap(part[1], "x"), proj_bias[layer], norm2_gain[layer],
            norm2_bias[layer],
        )
        normed2_far = swap(normed2, "x")
        active, slope, part = both(
            lambda rows: run_mlp_forward(rows, mlp_pieces[layer]), normed2, normed2_far
        )
        saved.append(
            (stream, (normed, normed_far), qkv, mixed, middle, (normed2, normed2_far), active, slope)
        )
        if layer + 1 < layers:
            stream, normed = run_residual_norm(
                middle, part[0], swap(part[1], "x"), fc2_bias[layer], norm1_gain[layer + 1],
                norm1_bias[layer + 1],
            )
        else:
            last = run_residual(middle, part[0], swap(part[1], "x"), fc2_bias[layer])

    gathered = lax.all_gather(last, "mp")
    block_out = run_leave(
        here,
        [lax.dynamic_index_in_dim(gathered, (depth - step) % n_mp, 0, False) for step in (0, 1, 3, 2)],
        seq, mine, BF16,
    )

    def gather_sum(grads):
        flat = grads.reshape(-1, grads.shape[-1])
        return run_split(here, lax.psum_scatter(flat, ("y", "core", "mp"), tiled=True))

    above, ready = (), [None] * (2 * layers)
    small = [None] * layers
    for layer in reversed(range(layers)):
        stream, normed, qkv, mixed, middle, normed2, active, slope = saved[layer]
        slopes, qkvs = list(slope), list(qkv)
        du, fc1_sum, part = both(
            lambda rows: run_mlp_backward(rows, slopes.pop(0), mlp_pieces[layer]),
            grad_b, grad_b_far,
        )
        (grads,) = run_weight_grad(
            "extra" if above else "plain", here, normed2, du, (grad_b, grad_b_far), active, *above
        )
        sums = gather_sum(grads)
        ready[2 * layer + 1] = sums[:2]
        if above:
            ready[2 * layer + 2] = sums[2:]
        grad, grad_b, sums2 = run_norm_back(
            grad, part[0], swap(part[1], "x"), middle, norm2_gain[layer]
        )
        grad_b_far = swap(grad_b, "x")
        dqkv, qv_sum, part = both(
            lambda rows: run_attention_backward(
                layer, here, rows, qkvs.pop(0), attn_weights, attn_pieces[layer]
            ),
            grad_b, grad_b_far,
        )
        above = run_weight_grad(
            "compact" if layer else "relative", here, normed, dqkv, (grad_b, grad_b_far), mixed
        )
        grad, grad_b, sums1 = run_norm_back(
            grad, part[0], swap(part[1], "x"), stream, norm1_gain[layer]
        )
        if layer:
            grad_b_far = swap(grad_b, "x")
        small[layer] = [sums1, sums2, *qv_sum, *fc1_sum]

    parts = {step: shift(grad_b, step) for step in (1, 3, 2)}
    input_grad = run_leave(here, [grad_b] + [parts[step] for step in (1, 3, 2)], seq, mine, F32)

    near, away, send = above
    near, away = run_add_core(near, away, swap(send, "core"))
    pieces = run_add_side(here, near, swap(away, "y"))
    pieces = [pieces[0]] + [shift(pieces[step], step) for step in range(1, n_mp)]
    ready[0] = run_add_depth(here, pieces)

    total = run_collect(here, fc2_sum, [part for parts in small for part in parts])
    for axis in ("core", "x", "y"):
        total = total + swap(total, axis)
    for bit in range(n_far.bit_length() - 1):
        pairs = [(index, index ^ (1 << bit)) for index in range(n_far)]
        total = total + lax.ppermute(total, "far", pairs)
    total = after(total, *parts.values())
    for bit in range(n_mp.bit_length() - 1):
        pairs = [(index, index ^ (1 << bit)) for index in range(n_mp)]
        total = total + lax.ppermute(total, "mp", pairs)
    n1g, n1b, pb, n2g, n2b, f2b, qv, fc1 = run_release(here, total)

    if n_far == 1:
        parts = [part for stay, move in ready for part in (stay, swap(move, "x"))]
    else:
        parts = [part for stay, move in ready for part in spread_rows(stay, move)]
    g_qkv, g_proj, g_fc1, g_fc2 = run_finish(here, parts)
    return (
        block_out, input_grad, n1g, n1b, g_qkv.transpose(0, 2, 1, 3), qv, g_proj, pb, n2g, n2b,
        g_fc1, fc1, g_fc2, f2b,
    )


def spread_rows(stay, move):
    pair = lax.axis_index("x")
    value = jnp.stack(
        [jnp.where(pair == 0, stay, move), jnp.where(pair == 0, move, stay)]
    ).astype(F32)
    value = lax.psum(value, "far")
    value = lax.all_gather(value, ("y", "x", "core"))
    rows, span = value.shape[2:]
    value = value.reshape(2, 2, 2, 2, rows, span).transpose(0, 3, 2, 4, 1, 5)
    value = value.reshape(8 * rows, 2, span)
    count = rows // lax.axis_size("far")
    place = lax.axis_index(("far", "y", "x", "core"))
    value = lax.dynamic_slice_in_dim(value, place * count, count, 0)
    mine = lax.dynamic_index_in_dim(value, pair, 1, keepdims=False)
    other = lax.dynamic_index_in_dim(value, 1 - pair, 1, keepdims=False)
    return mine, other


def solution(mesh):
    n_dp, n_mp = mesh.shape["dp"], mesh.shape["mp"]
    fine = Mesh(mesh.devices.reshape(n_dp // 8, 2, 2, 2, n_mp), ("far", "y", "x", "core", "mp"))
    dp = ("far", "y", "x", "core")
    return jax.shard_map(
        on_device,
        mesh=fine,
        in_specs=(
            P(dp, None, None),
            P(dp, None, None),
            P(),
            P(),
            P(None, None, None, "mp"),
            P(None, None, "mp"),
            P(None, "mp", None),
            P(),
            P(),
            P(),
            P(None, None, "mp"),
            P(None, "mp"),
            P(None, "mp", None),
            P(),
        ),
        out_specs=(
            P(dp, None, None),
            P(dp, None, None),
            P(),
            P(),
            P(None, dp, None, "mp"),
            P(None, None, "mp"),
            P(None, "mp", dp),
            P(),
            P(),
            P(),
            P(None, dp, "mp"),
            P(None, "mp"),
            P(None, "mp", dp),
            P(),
        ),
        check_vma=False,
    )
```

```python
import functools

import jax
import jax.numpy as jnp
from jax import lax
from jax.experimental import pallas as pl
from jax.experimental.pallas import tpu as pltpu
from jax.sharding import Mesh
from jax.sharding import PartitionSpec as P

HEAD_DIM = 64
EPS = 1e-06
F32 = jnp.float32
BF16 = jnp.bfloat16
ROWS = 304
WIN = 112
WIN_STEP = 96
BIG_NEG = -1e30
VMEM_LIMIT = 60 * 1024 * 1024


def dot_nn(a, b):
    return lax.dot_general(a, b, (((1,), (0,)), ((), ())), preferred_element_type=F32)


def dot_nt(a, b):
    return lax.dot_general(a, b, (((1,), (1,)), ((), ())), preferred_element_type=F32)


def dot_tn(a, b):
    return lax.dot_general(a, b, (((0,), (0,)), ((), ())), preferred_element_type=F32)


COST = 4e9


def params(micros):
    return dict(
        compiler_params=pltpu.CompilerParams(vmem_limit_bytes=VMEM_LIMIT),
        cost_estimate=pl.CostEstimate(
            flops=int(micros * COST), bytes_accessed=0, transcendentals=0
        ),
    )


VM = pl.BlockSpec(memory_space=pltpu.VMEM)
SM = pl.BlockSpec(memory_space=pltpu.SMEM)
HB = pl.BlockSpec(memory_space=pl.ANY)


def layer_norm(x, gain, bias):
    mean = jnp.mean(x, axis=-1, keepdims=True)
    centered = x - mean
    variance = jnp.mean(centered * centered, axis=-1, keepdims=True)
    return centered * lax.rsqrt(variance + EPS) * gain + bias


def own_selector(place, seq, mine):
    images = 4 * mine
    row = lax.broadcasted_iota(jnp.int32, (ROWS, images * seq), 0)
    col = lax.broadcasted_iota(jnp.int32, (ROWS, images * seq), 1)
    token = col // images
    image = col - token * images - place[DEPTH] * mine
    hit = (image >= 0) & (image < mine) & (row == image * seq + token)
    return jnp.where(hit, 1.0, 0.0).astype(BF16)


def enter_kernel(seq, mine, place, x_ref, gain_ref, beta_ref, x1_ref, a_ref):
    x = dot_nn(own_selector(place, seq, mine), x_ref[...])
    x1_ref[...] = x
    a_ref[...] = layer_norm(x, gain_ref[...], beta_ref[...]).astype(BF16)


def enter_back_kernel(seq, mine, place, x_ref, g_ref, gb_ref, sum_ref):
    g = dot_nn(own_selector(place, seq, mine), x_ref[...])
    g_ref[...] = g
    gb_ref[...] = g.astype(BF16)
    sum_ref[...] = jnp.broadcast_to(jnp.sum(g, axis=0, keepdims=True), sum_ref.shape)


def leave_kernel(seq, mine, place, *refs):
    parts, out_ref = refs[:-1], refs[-1]
    images = 4 * mine
    count = images * seq
    row = lax.broadcasted_iota(jnp.int32, (count, ROWS), 0)
    col = lax.broadcasted_iota(jnp.int32, (count, ROWS), 1)
    token = row // images
    want = row - token * images
    total = None
    for index, step in enumerate((0, 1, 3, 2)):
        depth, rows = index, parts[0].at[index] if len(parts) == 1 else parts[index]
        if len(parts) > 1:
            depth = (place[DEPTH] - step) & 3
        image = want - depth * mine
        hit = (image >= 0) & (image < mine) & (col == image * seq + token)
        part = dot_nn(jnp.where(hit, 1.0, 0.0).astype(BF16), rows[...])
        total = part if total is None else total + part
    out_ref[...] = total.astype(out_ref.dtype)


def residual_norm_kernel(
    x_ref, own_ref, far_ref, bias_ref, gain_ref, beta_ref, x1_ref, a_ref, far, sem
):
    copy = pltpu.make_async_copy(far_ref, far, sem)
    copy.start()
    keep = lax.broadcasted_iota(jnp.int32, (ROWS, 1), 0) < 300
    bias = jnp.where(keep, bias_ref[...], 0.0)
    copy.wait()
    x1 = x_ref[...] + own_ref[...].astype(F32) + far[...].astype(F32) + bias
    x1_ref[...] = x1
    a_ref[...] = layer_norm(x1, gain_ref[...], beta_ref[...]).astype(BF16)


def residual_kernel(x_ref, own_ref, far_ref, bias_ref, x1_ref, far, sem):
    copy = pltpu.make_async_copy(far_ref, far, sem)
    copy.start()
    copy.wait()
    x1 = x_ref[...] + own_ref[...].astype(F32) + far[...].astype(F32) + bias_ref[...]
    x1_ref[...] = x1.astype(BF16)


def norm_back_kernel(
    g_ref, own_ref, far_ref, x_ref, gain_ref, g1_ref, g1b_ref, sums_ref, far, sem
):
    copy = pltpu.make_async_copy(far_ref, far, sem)
    copy.start()
    x = x_ref[...]
    mean = jnp.mean(x, axis=-1, keepdims=True)
    centered = x - mean
    variance = jnp.mean(centered * centered, axis=-1, keepdims=True)
    inverse = lax.rsqrt(variance + EPS)
    xhat = centered * inverse
    copy.wait()
    da = own_ref[...].astype(F32) + far[...].astype(F32)
    inner = da * gain_ref[...]
    mean_inner = jnp.mean(inner, axis=-1, keepdims=True)
    mean_proj = jnp.mean(inner * xhat, axis=-1, keepdims=True)
    g1 = g_ref[...] + inverse * (inner - mean_inner - xhat * mean_proj)
    g1_ref[...] = g1
    g1b_ref[...] = g1.astype(BF16)
    sums_ref[...] = jnp.zeros(sums_ref.shape, F32)
    sums_ref[0:1, :] = jnp.sum(da * xhat, axis=0, keepdims=True)
    sums_ref[1:2, :] = jnp.sum(da, axis=0, keepdims=True)
    sums_ref[2:3, :] = jnp.sum(g1, axis=0, keepdims=True)


def run_enter(place, images, mine, gain, beta):
    count, seq, width = images.shape
    flat = images.transpose(1, 0, 2).reshape(count * seq, width)
    return pl.pallas_call(
        functools.partial(enter_kernel, seq, mine),
        out_shape=(
            jax.ShapeDtypeStruct((ROWS, width), F32),
            jax.ShapeDtypeStruct((ROWS, width), BF16),
        ),
        in_specs=[SM, VM, VM, VM],
        out_specs=(VM, VM),
        **params(5),
    )(place, flat, gain[None], beta[None])


def run_enter_back(place, images, mine):
    count, seq, width = images.shape
    flat = images.transpose(1, 0, 2).reshape(count * seq, width)
    return pl.pallas_call(
        functools.partial(enter_back_kernel, seq, mine),
        out_shape=(
            jax.ShapeDtypeStruct((ROWS, width), F32),
            jax.ShapeDtypeStruct((ROWS, width), BF16),
            jax.ShapeDtypeStruct((8, width), F32),
        ),
        in_specs=[SM, VM],
        out_specs=(VM, VM, VM),
        **params(5),
    )(place, flat)


def run_leave(place, parts, seq, mine, dtype):
    images, width = 4 * mine, parts[0].shape[-1]
    flat = pl.pallas_call(
        functools.partial(leave_kernel, seq, mine),
        out_shape=jax.ShapeDtypeStruct((images * seq, width), dtype),
        in_specs=[SM] + [VM] * len(parts),
        out_specs=VM,
        **params(9),
    )(place, *parts)
    return flat


def run_residual_norm(x, own, far, bias, gain, beta):
    return pl.pallas_call(
        residual_norm_kernel,
        out_shape=(
            jax.ShapeDtypeStruct(x.shape, F32),
            jax.ShapeDtypeStruct(x.shape, BF16),
        ),
        in_specs=[VM, VM, HB, VM, VM, VM],
        out_specs=(VM, VM),
        scratch_shapes=[pltpu.VMEM((ROWS, x.shape[1]), BF16), pltpu.SemaphoreType.DMA],
        **params(3),
    )(x, own, far, bias[None], gain[None], beta[None])


def run_residual(x, own, far, bias):
    return pl.pallas_call(
        residual_kernel,
        out_shape=jax.ShapeDtypeStruct(x.shape, BF16),
        in_specs=[VM, VM, HB, VM],
        out_specs=VM,
        scratch_shapes=[pltpu.VMEM((ROWS, x.shape[1]), BF16), pltpu.SemaphoreType.DMA],
        **params(2),
    )(x, own, far, bias[None])


def run_norm_back(g, own, far, x, gain):
    return pl.pallas_call(
        norm_back_kernel,
        out_shape=(
            jax.ShapeDtypeStruct(x.shape, F32),
            jax.ShapeDtypeStruct(x.shape, BF16),
            jax.ShapeDtypeStruct((8, x.shape[1]), F32),
        ),
        in_specs=[VM, VM, HB, VM, VM],
        out_specs=(VM, VM, VM),
        scratch_shapes=[pltpu.VMEM((ROWS, x.shape[1]), BF16), pltpu.SemaphoreType.DMA],
        **params(4),
    )(g, own, far, x, gain[None])


SIDE, CORE, PAIR, DEPTH, PARTS = 0, 1, 2, 3, 4

ATTN_ROWS, MLP_ROWS = 272, 528
ATTN_SPAN, MLP_SPAN = pl.ds(MLP_ROWS, ATTN_ROWS), pl.ds(0, MLP_ROWS)


def exact_rows(bias):
    high = bias.astype(BF16)
    rest = bias - high.astype(F32)
    mid = rest.astype(BF16)
    low = (rest - mid.astype(F32)).astype(BF16)
    return jnp.concatenate([high, mid, low, jnp.zeros((13, bias.shape[1]), BF16)], axis=0)


def pack_kernel(
    place, wqkv, wproj, w1, w2, bqv, b1, attn0, middle, mlp1, sems
):
    row = aligned(place[PARTS], 256)
    narrow, wide = aligned(place[PAIR], 128), aligned(place[PAIR], 512)
    copies = []
    mlp0, attn1 = middle.at[0:MLP_ROWS], middle.at[MLP_ROWS:]
    for layer, (attn, mlp) in enumerate(((attn0, mlp0), (attn1, mlp1))):
        for item in range(3):
            copies.append(
                (
                    wqkv.at[layer, item, pl.ds(row, 256), pl.ds(narrow, 128)],
                    attn.at[0:256, pl.ds(item * 128, 128)],
                )
            )
        for half in range(2):
            copies.append(
                (
                    wproj.at[layer, pl.ds(narrow, 128), pl.ds(row + half * 128, 128)],
                    attn.at[pl.ds(half * 128, 128), 384:512],
                )
            )
            copies.append(
                (
                    w2.at[layer, pl.ds(wide + half * 256, 256), pl.ds(row, 256)],
                    mlp.at[256:512, pl.ds(half * 256, 256)],
                )
            )
        copies.append(
            (w1.at[layer, pl.ds(row, 256), pl.ds(wide, 512)], mlp.at[0:256, :])
        )
    copies = [
        pltpu.make_async_copy(src, dst, sems.at[index])
        for index, (src, dst) in enumerate(copies)
    ]
    for copy in copies:
        copy.start()
    for layer, (attn, mlp) in enumerate(((attn0, mlp0), (attn1, mlp1))):
        zero = jnp.zeros((1, 128), F32)
        bias = [bqv[layer, pl.ds(item, 1), pl.ds(narrow, 128)] for item in range(2)]
        attn[256:272, :] = exact_rows(jnp.concatenate([bias[0], zero, bias[1], zero], axis=1))
        mlp[512:528, :] = exact_rows(b1[pl.ds(layer, 1), pl.ds(wide, 512)])
    for copy in copies:
        copy.wait()


def run_pack(place, wqkv, wproj, w1, w2, bqv, b1):
    return pl.pallas_call(
        pack_kernel,
        out_shape=tuple(
            jax.ShapeDtypeStruct((rows, 512), BF16)
            for rows in (ATTN_ROWS, MLP_ROWS + ATTN_ROWS, MLP_ROWS)
        ),
        in_specs=[SM, HB, HB, HB, HB, VM, VM],
        out_specs=(VM, VM, VM),
        scratch_shapes=[pltpu.SemaphoreType.DMA((16,))],
        **params(3),
    )(place, wqkv, wproj, w1, w2, bqv, b1)


def piece_sources(place, pieces, own):
    if not own:
        array, rows = pieces
        return [
            (depth, 2 * side + core, array.at[side, core, depth, rows])
            for depth in range(4)
            for side in range(2)
            for core in range(2)
        ]
    return [
        ((place[DEPTH] - step) & 3, place[PARTS + slot], pieces[4 * step - 4 + slot])
        for step in range(1, 4)
        for slot in range(4)
    ]


def aligned(index, step):
    if isinstance(index, int):
        return index * step
    return pl.multiple_of(index * step, step)


def start_attention_copies(layer, place, wqkv, wproj, bqv, pieces, wq, wp, sems, bs=None):
    own = len(pieces) > 2
    for index, (depth, part, src) in enumerate(piece_sources(place, pieces, own)):
        row = aligned(part, 256)
        pltpu.make_async_copy(
            src.at[0:256, 0:384], wq.at[depth, pl.ds(row, 256), :], sems.at[0, depth]
        ).start()
        for side in range(2):
            pltpu.make_async_copy(
                src.at[pl.ds(side * 128, 128), 384:512],
                wp.at[depth, :, pl.ds(row + side * 128, 128)],
                sems.at[1, depth],
            ).start()
        if bs is not None and index % 4 == 0:
            pltpu.make_async_copy(src.at[256:272, 0:384], bs.at[depth], sems.at[2, depth]).start()
    if own:
        depth, narrow = place[DEPTH], aligned(place[PAIR], 128)
        for item in range(3):
            pltpu.make_async_copy(
                wqkv.at[layer, item, :, pl.ds(narrow, 128)],
                wq.at[depth, :, pl.ds(item * 128, 128)],
                sems.at[0, depth],
            ).start()
        pltpu.make_async_copy(
            wproj.at[layer, pl.ds(narrow, 128), :], wp.at[depth], sems.at[1, depth]
        ).start()
        if bs is not None:
            bias = [bqv[layer, pl.ds(item, 1), pl.ds(narrow, 128)] for item in range(2)]
            zero = jnp.zeros((1, 128), F32)
            bs[depth] = exact_rows(jnp.concatenate([bias[0], zero, bias[1]], axis=1))


def start_mlp_copies(pieces, w1, w2, sems, bs=None):
    for index, (depth, part, src) in enumerate(piece_sources(None, pieces, False)):
        row = part * 256
        pltpu.make_async_copy(
            src.at[0:256, :], w1.at[depth, pl.ds(row, 256), :], sems.at[0, depth]
        ).start()
        for side in range(2):
            pltpu.make_async_copy(
                src.at[256:512, pl.ds(side * 256, 256)],
                w2.at[depth, pl.ds(side * 256, 256), pl.ds(row, 256)],
                sems.at[1, depth],
            ).start()
        if bs is not None and index % 4 == 0:
            pltpu.make_async_copy(src.at[512:528, :], bs.at[depth], sems.at[2, depth]).start()


def start_rows(source, rows, sems):
    copy = pltpu.make_async_copy(source, rows, sems.at[3, 0])
    copy.start()
    return copy


def wait_chunk(chunk, bufs, sems):
    for slot, buf in enumerate(bufs):
        pltpu.make_async_copy(buf.at[chunk], buf.at[chunk], sems.at[slot, chunk]).wait()


def wait_bias(chunk, bs, sems, own=None):
    def wait():
        pltpu.make_async_copy(bs.at[chunk], bs.at[chunk], sems.at[2, chunk]).wait()

    if own is None:
        wait()
    else:
        pl.when(chunk != own)(wait)


def window_masks(window):
    shape = (2 * WIN, WIN)
    row = lax.broadcasted_iota(jnp.int32, shape, 0)
    row = jnp.where(row >= WIN, row - WIN, row) - 4 * window
    col = lax.broadcasted_iota(jnp.int32, shape, 1) - 4 * window
    row_ok = (row >= 0) & (row < 100)
    col_ok = (col >= 0) & (col < 100)
    same = row_ok & col_ok & ((row >= 50) == (col >= 50))
    return jnp.where(same, 0.0, BIG_NEG).astype(F32)


def window_rows_ok(window):
    row = lax.broadcasted_iota(jnp.int32, (2 * WIN, 1), 0)
    row = jnp.where(row >= WIN, row - WIN, row) - 4 * window
    return (row >= 0) & (row < 100)


def stack_heads(values, first):
    zero = jnp.zeros_like(values)
    return jnp.concatenate(
        [jnp.where(first, values, zero), jnp.where(first, zero, values)], axis=0
    )


def first_head_lanes():
    return lax.broadcasted_iota(jnp.int32, (WIN, 2 * HEAD_DIM), 1) < HEAD_DIM


def window_probs(query, key, mask, rows_ok):
    scores = dot_nt(query, key) * (HEAD_DIM**-0.5) + mask
    top = jnp.max(scores, axis=-1, keepdims=True)
    expo = jnp.exp(scores - top)
    total = jnp.sum(expo, axis=-1, keepdims=True)
    return expo * jnp.where(rows_ok, 1.0 / total, 0.0)


def join_windows(parts):
    first, second, third = parts
    over = WIN - WIN_STEP
    return jnp.concatenate(
        [
            first[:WIN_STEP],
            first[WIN_STEP:] + second[:over],
            second[over:WIN_STEP],
            second[WIN_STEP:] + third[:over],
            third[over:],
        ],
        axis=0,
    )


def attention_forward_kernel(layer, count, place, a_ref, wqkv, wproj, bqv, *refs):
    pieces = refs[:count] if count > 1 else (refs[0], ATTN_SPAN)
    qkv_ref, o_ref, r_ref, wq, wp, bs, rows, total, masks, sems = refs[count:]
    own_quarter = place[DEPTH] if count > 1 else None
    copy = start_rows(a_ref, rows, sems)
    start_attention_copies(layer, place, wqkv, wproj, bqv, pieces, wq, wp, sems, bs)
    for window in range(3):
        masks[window] = window_masks(window)
    copy.wait()

    def chunk_step(chunk, carry):
        wait_chunk(chunk, (wq, wp), sems)
        wait_bias(chunk, bs, sems, own_quarter)
        bias = jnp.sum(bs[chunk].astype(F32), axis=0, keepdims=True)
        qkv_ref[chunk] = (dot_nn(rows[...], wq[chunk]) + bias).astype(BF16)
        first = first_head_lanes()
        outs = []
        for window in range(3):
            span = pl.ds(window * WIN_STEP, WIN)
            query = stack_heads(qkv_ref[chunk, span, 0:128], first)
            probs = window_probs(
                query, qkv_ref[chunk, span, 128:256], masks[window], window_rows_ok(window)
            )
            mixed = dot_nn(probs.astype(BF16), qkv_ref[chunk, span, 256:384])
            outs.append(jnp.where(first, mixed[:WIN], mixed[WIN:]))
        o_ref[chunk] = join_windows(outs).astype(BF16)
        add_part(chunk, total, dot_nn(o_ref[chunk], wp[chunk]))
        return carry

    lax.fori_loop(0, 4, chunk_step, 0)
    r_ref[...] = total[...].astype(BF16)


def add_part(chunk, total, part):
    @pl.when(chunk == 0)
    def _():
        total[...] = part

    @pl.when(chunk > 0)
    def _():
        total[...] += part


def run_attention_forward(layer, place, rows, weights, pieces):
    width = rows.shape[1]
    return pl.pallas_call(
        functools.partial(attention_forward_kernel, layer, len(pieces)),
        out_shape=(
            jax.ShapeDtypeStruct((4, ROWS, 384), BF16),
            jax.ShapeDtypeStruct((4, ROWS, 128), BF16),
            jax.ShapeDtypeStruct((ROWS, width), BF16),
        ),
        in_specs=[SM, HB, HB, HB, VM] + [HB] * len(pieces),
        out_specs=(VM,) * 3,
        scratch_shapes=[
            pltpu.VMEM((4, width, 384), BF16),
            pltpu.VMEM((4, 128, width), BF16),
            pltpu.VMEM((4, 16, 384), BF16),
            pltpu.VMEM((ROWS, width), BF16),
            pltpu.VMEM((ROWS, width), F32),
            pltpu.VMEM((3, 2 * WIN, WIN), F32),
            pltpu.SemaphoreType.DMA((4, 4)),
        ],
        **params(7),
    )(place, rows, *weights, *pieces)


def attention_backward_kernel(layer, count, place, g_ref, qkv_ref, wqkv, wproj, *refs):
    pieces = refs[:count] if count > 1 else (refs[0], ATTN_SPAN)
    dqkv_ref, sums_ref, d_ref, wq, wp, rows, total, masks, gmix, sems = refs[count:]
    copy = start_rows(g_ref, rows, sems)
    start_attention_copies(layer, place, wqkv, wproj, None, pieces, wq, wp, sems)
    for window in range(3):
        masks[window] = window_masks(window)
    copy.wait()

    def chunk_step(chunk, carry):
        wait_chunk(chunk, (wq, wp), sems)
        gmix[...] = dot_nt(rows[...], wp[chunk]).astype(BF16)
        first = first_head_lanes()
        scale = HEAD_DIM**-0.5
        outs = []
        for window in range(3):
            span = pl.ds(window * WIN_STEP, WIN)
            query = stack_heads(qkv_ref[chunk, span, 0:128], first)
            key = qkv_ref[chunk, span, 128:256]
            grad = stack_heads(gmix[span, :], first)
            probs = window_probs(query, key, masks[window], window_rows_ok(window))
            gprobs = dot_nt(grad, qkv_ref[chunk, span, 256:384])
            gvalue = dot_tn(probs.astype(BF16), grad)
            inner = jnp.sum(gprobs * probs, axis=-1, keepdims=True)
            gscores = (probs * (gprobs - inner)).astype(BF16)
            gquery = dot_nn(gscores, key) * scale
            gkey = dot_tn(gscores, query) * scale
            outs.append((jnp.where(first, gquery[:WIN], gquery[WIN:]), gkey, gvalue))
        joined = jnp.concatenate(
            [join_windows([out[item] for out in outs]) for item in range(3)], axis=1
        ).astype(BF16)
        dqkv_ref[chunk] = joined
        sums_ref[chunk] = jnp.broadcast_to(
            jnp.sum(joined.astype(F32), axis=0, keepdims=True), (8, 384)
        )
        add_part(chunk, total, dot_nt(dqkv_ref[chunk], wq[chunk]))
        return carry

    lax.fori_loop(0, 4, chunk_step, 0)
    d_ref[...] = total[...].astype(BF16)


def run_attention_backward(layer, place, grad, qkv, weights, pieces):
    width = grad.shape[1]
    return pl.pallas_call(
        functools.partial(attention_backward_kernel, layer, len(pieces)),
        out_shape=(
            jax.ShapeDtypeStruct((4, ROWS, 384), BF16),
            jax.ShapeDtypeStruct((4, 8, 384), F32),
            jax.ShapeDtypeStruct((ROWS, width), BF16),
        ),
        in_specs=[SM, HB, VM, HB, HB] + [HB] * len(pieces),
        out_specs=(VM,) * 3,
        scratch_shapes=[
            pltpu.VMEM((4, width, 384), BF16),
            pltpu.VMEM((4, 128, width), BF16),
            pltpu.VMEM((ROWS, width), BF16),
            pltpu.VMEM((ROWS, width), F32),
            pltpu.VMEM((3, 2 * WIN, WIN), F32),
            pltpu.VMEM((ROWS, 128), BF16),
            pltpu.SemaphoreType.DMA((4, 4)),
        ],
        **params(12),
    )(place, grad, qkv, *weights[:2], *pieces)


def gelu_pair(u):
    size = jnp.abs(u) * (0.5**0.5)
    t = 1.0 / (1.0 + 0.3275911 * size)
    poly = t * (
        0.254829592
        + t * (-0.284496736 + t * (1.421413741 + t * (-1.453152027 + t * 1.061405429)))
    )
    bell = jnp.exp(-0.5 * u * u)
    tail = 0.5 * poly * bell
    phi = jnp.where(u >= 0.0, 1.0 - tail, tail)
    return u * phi, phi + u * bell * 0.3989422804014327


def mlp_forward_kernel(
    a_ref, pieces, h_ref, slope_ref, m_ref, w1, w2, bs, rows, total, sems
):
    copy = start_rows(a_ref, rows, sems)
    start_mlp_copies((pieces, MLP_SPAN), w1, w2, sems, bs)
    copy.wait()

    def chunk_step(chunk, carry):
        wait_chunk(chunk, (w1, w2), sems)
        wait_bias(chunk, bs, sems)
        bias = jnp.sum(bs[chunk].astype(F32), axis=0, keepdims=True)
        value, slope = gelu_pair(dot_nn(rows[...], w1[chunk]) + bias)
        h_ref[chunk] = value.astype(BF16)
        slope_ref[chunk] = slope.astype(BF16)
        add_part(chunk, total, dot_nn(h_ref[chunk], w2[chunk]))
        return carry

    lax.fori_loop(0, 4, chunk_step, 0)
    m_ref[...] = total[...].astype(BF16)


def run_mlp_forward(rows, pieces):
    width = rows.shape[1]
    return pl.pallas_call(
        mlp_forward_kernel,
        out_shape=(
            jax.ShapeDtypeStruct((4, ROWS, 512), BF16),
            jax.ShapeDtypeStruct((4, ROWS, 512), BF16),
            jax.ShapeDtypeStruct((ROWS, width), BF16),
        ),
        in_specs=[HB, HB],
        out_specs=(VM,) * 3,
        scratch_shapes=[
            pltpu.VMEM((4, width, 512), BF16),
            pltpu.VMEM((4, 512, width), BF16),
            pltpu.VMEM((4, 16, 512), BF16),
            pltpu.VMEM((ROWS, width), BF16),
            pltpu.VMEM((ROWS, width), F32),
            pltpu.SemaphoreType.DMA((4, 4)),
        ],
        **params(8),
    )(rows, pieces)


def mlp_backward_kernel(
    g_ref, slope_ref, pieces, du_ref, sums_ref, d_ref, w1, w2, rows, total, sems
):
    copy = start_rows(g_ref, rows, sems)
    start_mlp_copies((pieces, MLP_SPAN), w1, w2, sems)
    copy.wait()

    def chunk_step(chunk, carry):
        wait_chunk(chunk, (w1, w2), sems)
        grad = dot_nt(rows[...], w2[chunk]) * slope_ref[chunk].astype(F32)
        grad = grad.astype(BF16)
        du_ref[chunk] = grad
        sums_ref[chunk] = jnp.broadcast_to(
            jnp.sum(grad.astype(F32), axis=0, keepdims=True), (8, 512)
        )
        add_part(chunk, total, dot_nt(du_ref[chunk], w1[chunk]))
        return carry

    lax.fori_loop(0, 4, chunk_step, 0)
    d_ref[...] = total[...].astype(BF16)


def run_mlp_backward(grad, slope, pieces):
    width = grad.shape[1]
    return pl.pallas_call(
        mlp_backward_kernel,
        out_shape=(
            jax.ShapeDtypeStruct((4, ROWS, 512), BF16),
            jax.ShapeDtypeStruct((4, 8, 512), F32),
            jax.ShapeDtypeStruct((ROWS, width), BF16),
        ),
        in_specs=[HB, VM, HB],
        out_specs=(VM,) * 3,
        scratch_shapes=[
            pltpu.VMEM((4, width, 512), BF16),
            pltpu.VMEM((4, 512, width), BF16),
            pltpu.VMEM((ROWS, width), BF16),
            pltpu.VMEM((ROWS, width), F32),
            pltpu.SemaphoreType.DMA((4, 4)),
        ],
        **params(7),
    )(grad, slope, pieces)


SEND, AWAY, NEAR, ALL = 0, 1, 2, 3
STAGE_SLOTS = (((0, 1), (1, 1)), ((1, 0),), ((0, 0),), ((0, 0), (0, 1), (1, 0), (1, 1)))


def weight_grad_kernel(
    stage, place, x1_own, x1_far, y1_own, y1_far, x2_own, x2_far, y2_own, y2_far, *refs
):
    slots = STAGE_SLOTS[stage]
    (xs, y1, y2, turned, added, sems), refs = refs[-6:], refs[:-6]
    out_ref = refs[-1]
    got = [refs[0].at[0 if stage == NEAR else 1], *refs[1:-1]] if stage in (AWAY, NEAR) else []
    outs = [out_ref.at[slot] for slot in range(len(slots))] if len(slots) > 1 else [out_ref]
    copies = []
    for slot, (side, core) in enumerate(slots):
        if stage != ALL:
            side, core = place[SIDE] ^ side, place[CORE] ^ core
        start = aligned(4 * side + core, 128)
        for index, sources in enumerate(((x1_own, x1_far), (x2_own, x2_far))):
            for half, source in enumerate(sources):
                for run in range(2):
                    copies.append(
                        pltpu.make_async_copy(
                            source.at[:, pl.ds(start + 256 * run, 128)],
                            xs.at[index, slot, pl.ds(ROWS * half, ROWS), pl.ds(128 * run, 128)],
                            sems.at[4, 8 * slot + 4 * index + 2 * half + run],
                        )
                    )
    for copy in copies:
        copy.start()
    for chunk in range(4):
        for index, (source, target) in enumerate(
            ((y1_own, y1), (y1_far, y1), (y2_own, y2), (y2_far, y2))
        ):
            pltpu.make_async_copy(
                source.at[chunk],
                target.at[chunk, pl.ds(ROWS * (index % 2), ROWS)],
                sems.at[chunk, index],
            ).start()
        for index, source in enumerate(got):
            pltpu.make_async_copy(
                source.at[chunk], added.at[index, chunk], sems.at[chunk, 4 + index]
            ).start()
    for copy in copies:
        copy.wait()
    for slot in range(len(slots)):
        for index in range(2):
            turned[index, slot] = xs[index, slot].T
    span1 = y1.shape[2]

    def chunk_step(chunk, carry):
        for index, target in enumerate((y1, y1, y2, y2)):
            half = target.at[chunk, pl.ds(ROWS * (index % 2), ROWS)]
            pltpu.make_async_copy(half, half, sems.at[chunk, index]).wait()
        for index in range(len(got)):
            array = added.at[index, chunk]
            pltpu.make_async_copy(array, array, sems.at[chunk, 4 + index]).wait()
        for slot, out in enumerate(outs):
            first = dot_nn(turned[0, slot], y1[chunk])
            second = dot_nn(turned[1, slot], y2[chunk])
            for index in range(len(got)):
                first += added[index, chunk, :, 0:span1].astype(F32)
                second += added[index, chunk, :, span1:].astype(F32)
            out[chunk, :, 0:span1] = first.astype(BF16)
            out[chunk, :, span1:] = second.astype(BF16)
        return carry

    lax.fori_loop(0, 4, chunk_step, 0)


def run_weight_grad(stage, place, x1, y1, x2, y2, *got):
    rows, width = 2 * ROWS, x1[0].shape[1]
    span1, span2 = y1[0].shape[2], y2[0].shape[2]
    part = width // 4
    shape = (4, part, span1 + span2)
    slots = len(STAGE_SLOTS[stage])
    return pl.pallas_call(
        functools.partial(weight_grad_kernel, stage),
        out_shape=jax.ShapeDtypeStruct((slots, *shape) if slots > 1 else shape, BF16),
        in_specs=[SM] + [HB] * (8 + len(got)),
        out_specs=VM,
        scratch_shapes=[
            pltpu.VMEM((2, slots, rows, part), BF16),
            pltpu.VMEM((4, rows, span1), BF16),
            pltpu.VMEM((4, rows, span2), BF16),
            pltpu.VMEM((2, slots, part, rows), BF16),
            pltpu.VMEM((max(len(got), 1), *shape), BF16),
            pltpu.SemaphoreType.DMA((5, 32)),
        ],
        **params((4 if span1 > 384 else 3) * slots + 2),
    )(place, *x1, *y1, *x2, *y2, *got)


def add_depth_kernel(place, *refs):
    parts, (stay, move) = refs[:-2], refs[-2:]
    total = parts[0][...].astype(F32)
    for part in parts[1:]:
        total += part[...].astype(F32)
    half = total.shape[0] // 2
    low, high = total[:half], total[half:]
    even = place[PAIR] == 0
    stay[...] = jnp.where(even, low, high).astype(BF16)
    move[...] = jnp.where(even, high, low).astype(BF16)


def run_add_depth(place, parts):
    rows, span = parts[0].shape
    shape = jax.ShapeDtypeStruct((rows // 2, span), BF16)
    return pl.pallas_call(
        add_depth_kernel,
        out_shape=(shape, shape),
        in_specs=[SM] + [VM] * len(parts),
        out_specs=(VM, VM),
        **params(2),
    )(place, *parts)


def collect_kernel(place, fc2_last, *refs):
    out = refs[-1]
    layers = (len(refs) - 1) // 6
    narrow, wide = aligned(place[PAIR], 128), aligned(place[PAIR], 512)
    out[...] = jnp.zeros(out.shape, F32)
    for layer in range(layers):
        sums1, sums2, qv_own, qv_far, fc1_own, fc1_far = refs[6 * layer : 6 * layer + 6]
        row = 12 * layer
        out[row : row + 2, :] = sums1[0:2, :]
        out[row + 2 : row + 3, :] = sums2[2:3, :]
        out[row + 3 : row + 5, :] = sums2[0:2, :]
        above = refs[6 * layer + 6][2:3, :] if layer + 1 < layers else fc2_last[0:1, :]
        out[row + 5 : row + 6, :] = above
        for depth in range(4):
            qv = qv_own[depth, 0:1, :] + qv_far[depth, 0:1, :]
            for item in range(2):
                out[row + 6 + item, pl.ds(depth * 256 + narrow, 128)] = qv[
                    0, 256 * item : 256 * item + 128
                ]
            fc1 = fc1_own[depth, 0:1, :] + fc1_far[depth, 0:1, :]
            out[pl.ds(row + 8 + depth, 1), pl.ds(wide, 512)] = fc1


def run_collect(place, fc2_last, parts):
    layers = len(parts) // 6
    return pl.pallas_call(
        collect_kernel,
        out_shape=jax.ShapeDtypeStruct((12 * layers, 1024), F32),
        in_specs=[SM] + [VM] * (1 + len(parts)),
        out_specs=VM,
        **params(2),
    )(place, fc2_last, *parts)


def release_kernel(place, total, *outs):
    rows, (qv, fc1) = outs[:6], outs[6:]
    quarter = aligned(place[DEPTH], 256)
    for layer in range(fc1.shape[0]):
        for index, out in enumerate(rows):
            out[layer : layer + 1, :] = total[pl.ds(12 * layer + index, 1), :]
        for item in range(2):
            qv[layer, item : item + 1, :] = total[
                pl.ds(12 * layer + 6 + item, 1), pl.ds(quarter, 256)
            ]
        fc1[layer : layer + 1, :] = total[pl.ds(12 * layer + 8 + place[DEPTH], 1), :]


def run_release(place, total):
    layers = total.shape[0] // 12
    row = jax.ShapeDtypeStruct((layers, 1024), F32)
    return pl.pallas_call(
        release_kernel,
        out_shape=(row,) * 6 + (jax.ShapeDtypeStruct((layers, 2, 256), F32), row),
        in_specs=[SM, VM],
        out_specs=(VM,) * 8,
        **params(2),
    )(place, total)


def finish_kernel(place, *refs):
    layers = (len(refs) - 4) // 4
    ins, (qkv, proj, fc1, fc2) = refs[: 4 * layers], refs[4 * layers :]
    for layer in range(layers):
        for side in range(2):
            attn, mlp = ins[4 * layer + side], ins[4 * layer + 2 + side]
            pair = place[PAIR] if side == 0 else 1 - place[PAIR]
            narrow, wide = aligned(pair, 128), aligned(pair, 512)
            for item in range(3):
                qkv[layer, item, :, pl.ds(narrow, 128)] = attn[
                    :, item * 128 : item * 128 + 128
                ].astype(F32)
            proj[layer, pl.ds(narrow, 128), :] = attn[:, 384:512].astype(F32).T
            fc1[layer, :, pl.ds(wide, 512)] = mlp[:, 0:512].astype(F32)
            fc2[layer, pl.ds(wide, 512), :] = mlp[:, 512:1024].astype(F32).T


def run_finish(place, parts):
    rows = parts[0].shape[0]
    return pl.pallas_call(
        finish_kernel,
        out_shape=(
            jax.ShapeDtypeStruct((2, 3, rows, 256), F32),
            jax.ShapeDtypeStruct((2, 256, rows), F32),
            jax.ShapeDtypeStruct((2, rows, 1024), F32),
            jax.ShapeDtypeStruct((2, 1024, rows), F32),
        ),
        in_specs=[SM] + [VM] * len(parts),
        out_specs=(VM,) * 4,
        **params(4),
    )(place, *parts)


def on_device(*args):
    (
        images_in, out_cotangent, norm1_gain, norm1_bias, qkv_weight, qv_bias, proj_weight,
        proj_bias, norm2_gain, norm2_bias, fc1_weight, fc1_bias, fc2_weight, fc2_bias,
    ) = args
    images, seq, _ = images_in.shape
    layers = qkv_weight.shape[0]
    n_far, n_mp = lax.axis_size("far"), lax.axis_size("mp")
    mine = images // n_mp

    side, pair, core = lax.axis_index("y"), lax.axis_index("x"), lax.axis_index("core")
    depth = lax.axis_index("mp")
    here = jnp.stack(
        [
            side, core, pair, depth,
            side * 2 + core, (1 - side) * 2 + core, side * 2 + 1 - core, (1 - side) * 2 + 1 - core,
        ]
    ).astype(jnp.int32)

    def swap(value, axis):
        return lax.ppermute(value, axis, [(0, 1), (1, 0)])

    def shift(value, step):
        return lax.ppermute(
            value, "mp", [(index, (index + step) % n_mp) for index in range(n_mp)]
        )

    def after(value, *others):
        return lax.optimization_barrier((value, *others))[0]

    wqkv = qkv_weight.transpose(0, 2, 1, 3)
    attn_weights = (wqkv, proj_weight, qv_bias)
    packed = run_pack(here, wqkv, proj_weight, fc1_weight, fc2_weight, qv_bias, fc1_bias)
    attn_pieces, mlp_pieces = [[]], []
    moved = []
    for step in (1, 3, 2):
        same = shift(packed[0], step)
        moved.append(same)
        other = swap(same, "y")
        attn_pieces[0].append((step, [same, other, swap(same, "core"), swap(other, "core")]))
    attn_pieces[0] = [array for _, arrays in sorted(attn_pieces[0]) for array in arrays]
    stream, normed = run_enter(here, images_in, mine, norm1_gain[0], norm1_bias[0])
    grad, grad_b, fc2_sum = run_enter_back(here, out_cotangent, mine)
    grad_b_far = swap(grad_b, "x")
    gathered = []
    for index in (1, 2):
        gathered = lax.all_gather((after(packed[index], *gathered) if gathered else packed[index]), ("y", "core", "mp"))
        value = gathered.reshape(2, 2, n_mp, *gathered.shape[1:])
        mlp_pieces.append(value)
        attn_pieces.append([value])
        gathered = [gathered]

    def both(run, own, far, *waits):
        results = run(own)
        return list(zip(results, run(after(far, *waits) if waits else far)))

    saved = []
    for layer in range(layers):
        normed_far = swap(normed, "x")
        qkv, mixed, part = both(
            lambda rows: run_attention_forward(layer, here, rows, attn_weights, attn_pieces[layer]),
            normed, normed_far,
        )
        middle, normed2 = run_residual_norm(
            stream, part[0], swap(part[1], "x"), proj_bias[layer], norm2_gain[layer],
            norm2_bias[layer],
        )
        normed2_far = swap(normed2, "x")
        active, slope, part = both(
            lambda rows: run_mlp_forward(rows, mlp_pieces[layer]),
            after(normed2, grad_b_far), normed2_far,
        )
        saved.append(
            (stream, (normed, normed_far), qkv, mixed, middle, (normed2, normed2_far), active, slope)
        )
        if layer + 1 < layers:
            stream, normed = run_residual_norm(
                middle, part[0], swap(part[1], "x"), fc2_bias[layer], norm1_gain[layer + 1],
                norm1_bias[layer + 1],
            )
        else:
            last = run_residual(middle, part[0], swap(part[1], "x"), fc2_bias[layer])

    class Sum:
        def __init__(self, *arrays):
            self.arrays = arrays
            self.core = swap(run_weight_grad(SEND, here, *arrays), "core")

        def away(self):
            kept = run_weight_grad(AWAY, here, *self.arrays, self.core)
            self.side = swap(kept, "y")
            return kept

        def near(self, *waits):
            side = after(self.side, *waits) if waits else self.side
            kept = run_weight_grad(NEAR, here, *self.arrays, self.core, side)
            flat = kept.reshape(-1, kept.shape[-1])
            self.total = lax.psum_scatter(flat, "mp", tiled=True)
            return kept

        def result(self):
            return run_add_depth(here, [self.total])

    class SumAtOnce(Sum):
        def __init__(self, *arrays):
            grads = run_weight_grad(ALL, here, *arrays)
            flat = grads.reshape(-1, grads.shape[-1])
            self.total = lax.psum_scatter(flat, ("y", "core", "mp"), tiled=True)

    attn, mlp, groups = None, None, []
    small = [None] * layers
    for layer in reversed(range(layers)):
        stream, normed, qkv, mixed, middle, normed2, active, slope = saved[layer]
        slopes, qkvs = list(slope), list(qkv)
        du, fc1_sum, part = both(
            lambda rows: run_mlp_backward(rows, slopes.pop(0), mlp_pieces[layer]),
            grad_b, grad_b_far, *([attn.away()] if attn else []),
        )
        mlp = (SumAtOnce if layer else Sum)(normed2, du, (grad_b, grad_b_far), active)
        if layer:
            last = after(last, mlp.total)
        grad, grad_b, sums2 = run_norm_back(
            grad, part[0], swap(part[1], "x"), middle, norm2_gain[layer]
        )
        grad_b_far = swap(grad_b, "x")
        dqkv, qv_sum, part = both(
            lambda rows: run_attention_backward(
                layer, here, rows, qkvs.pop(0), attn_weights, attn_pieces[layer]
            ),
            grad_b, grad_b_far, *([] if layer else [mlp.away()]),
        )
        above, attn = attn, Sum(normed, dqkv, (grad_b, grad_b_far), mixed)
        if above:
            grad = after(grad, above.near())
        grad, grad_b, sums1 = run_norm_back(
            grad, part[0], swap(part[1], "x"), stream, norm1_gain[layer]
        )
        if layer:
            grad_b_far = swap(grad_b, "x")
        small[layer] = [sums1, sums2, *qv_sum, *fc1_sum]
        groups = [attn, mlp, *groups]

    block_out = run_leave(here, [lax.all_gather(last, "mp")], seq, mine, BF16)
    parts = [shift(grad_b, step) for step in (1, 3, 2)]
    attn.core = after(attn.core, grad_b)
    attn.away()
    kept = mlp.near(parts[0])
    kept = attn.near(kept, block_out, *parts)
    parts = [after(part, kept) for part in parts]
    input_grad = run_leave(here, [grad_b, *parts], seq, mine, F32)
    total = run_collect(here, fc2_sum, [part for group in small for part in group])
    total = after(total, kept)
    for axis in ("core", "x", "y"):
        total = total + swap(total, axis)
    for bit in range(n_far.bit_length() - 1):
        pairs = [(index, index ^ (1 << bit)) for index in range(n_far)]
        total = total + lax.ppermute(total, "far", pairs)
    total = after(total, *parts)
    for bit in range(n_mp.bit_length() - 1):
        pairs = [(index, index ^ (1 << bit)) for index in range(n_mp)]
        total = total + lax.ppermute(total, "mp", pairs)
    n1g, n1b, pb, n2g, n2b, f2b, qv, fc1 = run_release(here, total)

    ready = [group.result() for group in groups]
    if n_far == 1:
        parts = [part for stay, move in ready for part in (stay, swap(move, "x"))]
    else:
        parts = [part for stay, move in ready for part in spread_rows(stay, move)]
    g_qkv, g_proj, g_fc1, g_fc2 = run_finish(here, parts)
    block_out, input_grad = (
        value.reshape(seq, images, -1).transpose(1, 0, 2) for value in (block_out, input_grad)
    )
    return (
        block_out, input_grad, n1g, n1b, g_qkv.transpose(0, 2, 1, 3), qv, g_proj, pb, n2g, n2b,
        g_fc1, fc1, g_fc2, f2b,
    )


def spread_rows(stay, move):
    pair = lax.axis_index("x")
    value = jnp.stack(
        [jnp.where(pair == 0, stay, move), jnp.where(pair == 0, move, stay)]
    ).astype(F32)
    value = lax.psum(value, "far")
    value = lax.all_gather(value, ("y", "x", "core"))
    rows, span = value.shape[2:]
    value = value.reshape(2, 2, 2, 2, rows, span).transpose(0, 3, 2, 4, 1, 5)
    value = value.reshape(8 * rows, 2, span)
    count = rows // lax.axis_size("far")
    place = lax.axis_index(("far", "y", "x", "core"))
    value = lax.dynamic_slice_in_dim(value, place * count, count, 0)
    mine = lax.dynamic_index_in_dim(value, pair, 1, keepdims=False)
    other = lax.dynamic_index_in_dim(value, 1 - pair, 1, keepdims=False)
    return mine, other


def solution(mesh):
    n_dp, n_mp = mesh.shape["dp"], mesh.shape["mp"]
    fine = Mesh(mesh.devices.reshape(n_dp // 8, 2, 2, 2, n_mp), ("far", "y", "x", "core", "mp"))
    dp = ("far", "y", "x", "core")
    return jax.shard_map(
        on_device,
        mesh=fine,
        in_specs=(
            P(dp, None, None),
            P(dp, None, None),
            P(),
            P(),
            P(None, None, None, "mp"),
            P(None, None, "mp"),
            P(None, "mp", None),
            P(),
            P(),
            P(),
            P(None, None, "mp"),
            P(None, "mp"),
            P(None, "mp", None),
            P(),
        ),
        out_specs=(
            P(dp, None, None),
            P(dp, None, None),
            P(),
            P(),
            P(None, dp, None, "mp"),
            P(None, None, "mp"),
            P(None, "mp", dp),
            P(),
            P(),
            P(),
            P(None, dp, "mp"),
            P(None, "mp"),
            P(None, "mp", dp),
            P(),
        ),
        check_vma=False,
    )
```

```python
import functools

import jax
import jax.numpy as jnp
from jax import lax
from jax.experimental import pallas as pl
from jax.experimental.pallas import tpu as pltpu
from jax.sharding import Mesh
from jax.sharding import PartitionSpec as P

HEAD_DIM = 64
EPS = 1e-06
F32 = jnp.float32
BF16 = jnp.bfloat16
ROWS = 304
WIN = 112
WIN_STEP = 96
BIG_NEG = -1e30
VMEM_LIMIT = 60 * 1024 * 1024


def dot_nn(a, b):
    return lax.dot_general(a, b, (((1,), (0,)), ((), ())), preferred_element_type=F32)


def dot_nt(a, b):
    return lax.dot_general(a, b, (((1,), (1,)), ((), ())), preferred_element_type=F32)


def dot_tn(a, b):
    return lax.dot_general(a, b, (((0,), (0,)), ((), ())), preferred_element_type=F32)


COST = 4e9


def params(micros):
    return dict(
        compiler_params=pltpu.CompilerParams(vmem_limit_bytes=VMEM_LIMIT),
        cost_estimate=pl.CostEstimate(
            flops=int(micros * COST), bytes_accessed=0, transcendentals=0
        ),
    )


VM = pl.BlockSpec(memory_space=pltpu.VMEM)
SM = pl.BlockSpec(memory_space=pltpu.SMEM)
HB = pl.BlockSpec(memory_space=pl.ANY)


def layer_norm(x, gain, bias):
    mean = jnp.mean(x, axis=-1, keepdims=True)
    centered = x - mean
    variance = jnp.mean(centered * centered, axis=-1, keepdims=True)
    return centered * lax.rsqrt(variance + EPS) * gain + bias


def own_selector(place, seq, mine):
    images = 4 * mine
    row = lax.broadcasted_iota(jnp.int32, (ROWS, images * seq), 0)
    col = lax.broadcasted_iota(jnp.int32, (ROWS, images * seq), 1)
    token = col // images
    image = col - token * images - place[DEPTH] * mine
    hit = (image >= 0) & (image < mine) & (row == image * seq + token)
    return jnp.where(hit, 1.0, 0.0).astype(BF16)


def enter_kernel(seq, mine, place, x_ref, gain_ref, beta_ref, x1_ref, a_ref):
    x = dot_nn(own_selector(place, seq, mine), x_ref[...])
    x1_ref[...] = x
    a_ref[...] = layer_norm(x, gain_ref[...], beta_ref[...]).astype(BF16)


def enter_back_kernel(seq, mine, place, x_ref, g_ref, gb_ref, sum_ref):
    g = dot_nn(own_selector(place, seq, mine), x_ref[...])
    g_ref[...] = g
    gb_ref[...] = g.astype(BF16)
    sum_ref[...] = jnp.broadcast_to(jnp.sum(g, axis=0, keepdims=True), sum_ref.shape)


def leave_kernel(seq, mine, place, *refs):
    parts, out_ref = refs[:-1], refs[-1]
    images = 4 * mine
    count = images * seq
    row = lax.broadcasted_iota(jnp.int32, (count, ROWS), 0)
    col = lax.broadcasted_iota(jnp.int32, (count, ROWS), 1)
    token = row // images
    want = row - token * images
    total = None
    for index, step in enumerate((0, 1, 3, 2)):
        depth, rows = index, parts[0].at[index] if len(parts) == 1 else parts[index]
        if len(parts) > 1:
            depth = (place[DEPTH] - step) & 3
        image = want - depth * mine
        hit = (image >= 0) & (image < mine) & (col == image * seq + token)
        part = dot_nn(jnp.where(hit, 1.0, 0.0).astype(BF16), rows[...])
        total = part if total is None else total + part
    out_ref[...] = total.astype(out_ref.dtype)


def residual_norm_kernel(
    x_ref, own_ref, far_ref, bias_ref, gain_ref, beta_ref, x1_ref, a_ref, far, sem
):
    copy = pltpu.make_async_copy(far_ref, far, sem)
    copy.start()
    keep = lax.broadcasted_iota(jnp.int32, (ROWS, 1), 0) < 300
    bias = jnp.where(keep, bias_ref[...], 0.0)
    copy.wait()
    x1 = x_ref[...] + own_ref[...].astype(F32) + far[...].astype(F32) + bias
    x1_ref[...] = x1
    a_ref[...] = layer_norm(x1, gain_ref[...], beta_ref[...]).astype(BF16)


def residual_kernel(x_ref, own_ref, far_ref, bias_ref, x1_ref, far, sem):
    copy = pltpu.make_async_copy(far_ref, far, sem)
    copy.start()
    copy.wait()
    x1 = x_ref[...] + own_ref[...].astype(F32) + far[...].astype(F32) + bias_ref[...]
    x1_ref[...] = x1.astype(BF16)


def norm_back_kernel(
    g_ref, own_ref, far_ref, x_ref, gain_ref, g1_ref, g1b_ref, sums_ref, far, sem
):
    copy = pltpu.make_async_copy(far_ref, far, sem)
    copy.start()
    x = x_ref[...]
    mean = jnp.mean(x, axis=-1, keepdims=True)
    centered = x - mean
    variance = jnp.mean(centered * centered, axis=-1, keepdims=True)
    inverse = lax.rsqrt(variance + EPS)
    xhat = centered * inverse
    copy.wait()
    da = own_ref[...].astype(F32) + far[...].astype(F32)
    inner = da * gain_ref[...]
    mean_inner = jnp.mean(inner, axis=-1, keepdims=True)
    mean_proj = jnp.mean(inner * xhat, axis=-1, keepdims=True)
    g1 = g_ref[...] + inverse * (inner - mean_inner - xhat * mean_proj)
    g1_ref[...] = g1
    g1b_ref[...] = g1.astype(BF16)
    sums_ref[...] = jnp.zeros(sums_ref.shape, F32)
    sums_ref[0:1, :] = jnp.sum(da * xhat, axis=0, keepdims=True)
    sums_ref[1:2, :] = jnp.sum(da, axis=0, keepdims=True)
    sums_ref[2:3, :] = jnp.sum(g1, axis=0, keepdims=True)


def run_enter(place, images, mine, gain, beta):
    count, seq, width = images.shape
    flat = images.transpose(1, 0, 2).reshape(count * seq, width)
    return pl.pallas_call(
        functools.partial(enter_kernel, seq, mine),
        out_shape=(
            jax.ShapeDtypeStruct((ROWS, width), F32),
            jax.ShapeDtypeStruct((ROWS, width), BF16),
        ),
        in_specs=[SM, VM, VM, VM],
        out_specs=(VM, VM),
        **params(5),
    )(place, flat, gain[None], beta[None])


def run_enter_back(place, images, mine):
    count, seq, width = images.shape
    flat = images.transpose(1, 0, 2).reshape(count * seq, width)
    return pl.pallas_call(
        functools.partial(enter_back_kernel, seq, mine),
        out_shape=(
            jax.ShapeDtypeStruct((ROWS, width), F32),
            jax.ShapeDtypeStruct((ROWS, width), BF16),
            jax.ShapeDtypeStruct((8, width), F32),
        ),
        in_specs=[SM, VM],
        out_specs=(VM, VM, VM),
        **params(5),
    )(place, flat)


def run_leave(place, parts, seq, mine, dtype):
    images, width = 4 * mine, parts[0].shape[-1]
    flat = pl.pallas_call(
        functools.partial(leave_kernel, seq, mine),
        out_shape=jax.ShapeDtypeStruct((images * seq, width), dtype),
        in_specs=[SM] + [VM] * len(parts),
        out_specs=VM,
        **params(9),
    )(place, *parts)
    return flat


def run_residual_norm(x, own, far, bias, gain, beta):
    return pl.pallas_call(
        residual_norm_kernel,
        out_shape=(
            jax.ShapeDtypeStruct(x.shape, F32),
            jax.ShapeDtypeStruct(x.shape, BF16),
        ),
        in_specs=[VM, VM, HB, VM, VM, VM],
        out_specs=(VM, VM),
        scratch_shapes=[pltpu.VMEM((ROWS, x.shape[1]), BF16), pltpu.SemaphoreType.DMA],
        **params(3),
    )(x, own, far, bias[None], gain[None], beta[None])


def run_residual(x, own, far, bias):
    return pl.pallas_call(
        residual_kernel,
        out_shape=jax.ShapeDtypeStruct(x.shape, BF16),
        in_specs=[VM, VM, HB, VM],
        out_specs=VM,
        scratch_shapes=[pltpu.VMEM((ROWS, x.shape[1]), BF16), pltpu.SemaphoreType.DMA],
        **params(2),
    )(x, own, far, bias[None])


def run_norm_back(g, own, far, x, gain):
    return pl.pallas_call(
        norm_back_kernel,
        out_shape=(
            jax.ShapeDtypeStruct(x.shape, F32),
            jax.ShapeDtypeStruct(x.shape, BF16),
            jax.ShapeDtypeStruct((8, x.shape[1]), F32),
        ),
        in_specs=[VM, VM, HB, VM, VM],
        out_specs=(VM, VM, VM),
        scratch_shapes=[pltpu.VMEM((ROWS, x.shape[1]), BF16), pltpu.SemaphoreType.DMA],
        **params(4),
    )(g, own, far, x, gain[None])


SIDE, CORE, PAIR, DEPTH, PARTS = 0, 1, 2, 3, 4

ATTN_ROWS, MLP_ROWS = 272, 528
ATTN_SPAN, MLP_SPAN = pl.ds(MLP_ROWS, ATTN_ROWS), pl.ds(0, MLP_ROWS)


def exact_rows(bias):
    high = bias.astype(BF16)
    rest = bias - high.astype(F32)
    mid = rest.astype(BF16)
    low = (rest - mid.astype(F32)).astype(BF16)
    return jnp.concatenate([high, mid, low, jnp.zeros((13, bias.shape[1]), BF16)], axis=0)


def pack_kernel(
    place, wqkv, wproj, w1, w2, bqv, b1, attn0, middle, mlp1, sems
):
    row = aligned(place[PARTS], 256)
    narrow, wide = aligned(place[PAIR], 128), aligned(place[PAIR], 512)
    copies = []
    mlp0, attn1 = middle.at[0:MLP_ROWS], middle.at[MLP_ROWS:]
    for layer, (attn, mlp) in enumerate(((attn0, mlp0), (attn1, mlp1))):
        for item in range(3):
            copies.append(
                (
                    wqkv.at[layer, item, pl.ds(row, 256), pl.ds(narrow, 128)],
                    attn.at[0:256, pl.ds(item * 128, 128)],
                )
            )
        for half in range(2):
            copies.append(
                (
                    wproj.at[layer, pl.ds(narrow, 128), pl.ds(row + half * 128, 128)],
                    attn.at[pl.ds(half * 128, 128), 384:512],
                )
            )
            copies.append(
                (
                    w2.at[layer, pl.ds(wide + half * 256, 256), pl.ds(row, 256)],
                    mlp.at[256:512, pl.ds(half * 256, 256)],
                )
            )
        copies.append(
            (w1.at[layer, pl.ds(row, 256), pl.ds(wide, 512)], mlp.at[0:256, :])
        )
    copies = [
        pltpu.make_async_copy(src, dst, sems.at[index])
        for index, (src, dst) in enumerate(copies)
    ]
    for copy in copies:
        copy.start()
    for layer, (attn, mlp) in enumerate(((attn0, mlp0), (attn1, mlp1))):
        zero = jnp.zeros((1, 128), F32)
        bias = [bqv[layer, pl.ds(item, 1), pl.ds(narrow, 128)] for item in range(2)]
        attn[256:272, :] = exact_rows(jnp.concatenate([bias[0], zero, bias[1], zero], axis=1))
        mlp[512:528, :] = exact_rows(b1[pl.ds(layer, 1), pl.ds(wide, 512)])
    for copy in copies:
        copy.wait()


def run_pack(place, wqkv, wproj, w1, w2, bqv, b1):
    return pl.pallas_call(
        pack_kernel,
        out_shape=tuple(
            jax.ShapeDtypeStruct((rows, 512), BF16)
            for rows in (ATTN_ROWS, MLP_ROWS + ATTN_ROWS, MLP_ROWS)
        ),
        in_specs=[SM, HB, HB, HB, HB, VM, VM],
        out_specs=(VM, VM, VM),
        scratch_shapes=[pltpu.SemaphoreType.DMA((16,))],
        **params(3),
    )(place, wqkv, wproj, w1, w2, bqv, b1)


def piece_sources(place, pieces, own):
    if not own:
        array, rows = pieces
        return [
            (depth, 2 * side + core, array.at[side, core, depth, rows])
            for depth in range(4)
            for side in range(2)
            for core in range(2)
        ]
    return [
        ((place[DEPTH] - step) & 3, place[PARTS + slot], pieces[4 * step - 4 + slot])
        for step in range(1, 4)
        for slot in range(4)
    ]


def aligned(index, step):
    if isinstance(index, int):
        return index * step
    return pl.multiple_of(index * step, step)


def start_attention_copies(layer, place, wqkv, wproj, bqv, pieces, wq, wp, sems, bs=None):
    own = len(pieces) > 2
    for index, (depth, part, src) in enumerate(piece_sources(place, pieces, own)):
        row = aligned(part, 256)
        pltpu.make_async_copy(
            src.at[0:256, 0:384], wq.at[depth, pl.ds(row, 256), :], sems.at[0, depth]
        ).start()
        for side in range(2):
            pltpu.make_async_copy(
                src.at[pl.ds(side * 128, 128), 384:512],
                wp.at[depth, :, pl.ds(row + side * 128, 128)],
                sems.at[1, depth],
            ).start()
        if bs is not None and index % 4 == 0:
            pltpu.make_async_copy(src.at[256:272, 0:384], bs.at[depth], sems.at[2, depth]).start()
    if own:
        depth, narrow = place[DEPTH], aligned(place[PAIR], 128)
        for item in range(3):
            pltpu.make_async_copy(
                wqkv.at[layer, item, :, pl.ds(narrow, 128)],
                wq.at[depth, :, pl.ds(item * 128, 128)],
                sems.at[0, depth],
            ).start()
        pltpu.make_async_copy(
            wproj.at[layer, pl.ds(narrow, 128), :], wp.at[depth], sems.at[1, depth]
        ).start()
        if bs is not None:
            bias = [bqv[layer, pl.ds(item, 1), pl.ds(narrow, 128)] for item in range(2)]
            zero = jnp.zeros((1, 128), F32)
            bs[depth] = exact_rows(jnp.concatenate([bias[0], zero, bias[1]], axis=1))


def start_mlp_copies(pieces, w1, w2, sems, bs=None):
    for index, (depth, part, src) in enumerate(piece_sources(None, pieces, False)):
        row = part * 256
        pltpu.make_async_copy(
            src.at[0:256, :], w1.at[depth, pl.ds(row, 256), :], sems.at[0, depth]
        ).start()
        for side in range(2):
            pltpu.make_async_copy(
                src.at[256:512, pl.ds(side * 256, 256)],
                w2.at[depth, pl.ds(side * 256, 256), pl.ds(row, 256)],
                sems.at[1, depth],
            ).start()
        if bs is not None and index % 4 == 0:
            pltpu.make_async_copy(src.at[512:528, :], bs.at[depth], sems.at[2, depth]).start()


def start_rows(source, rows, sems):
    copy = pltpu.make_async_copy(source, rows, sems.at[3, 0])
    copy.start()
    return copy


def wait_chunk(chunk, bufs, sems):
    for slot, buf in enumerate(bufs):
        pltpu.make_async_copy(buf.at[chunk], buf.at[chunk], sems.at[slot, chunk]).wait()


def wait_bias(chunk, bs, sems, own=None):
    def wait():
        pltpu.make_async_copy(bs.at[chunk], bs.at[chunk], sems.at[2, chunk]).wait()

    if own is None:
        wait()
    else:
        pl.when(chunk != own)(wait)


def window_masks(window):
    shape = (2 * WIN, WIN)
    row = lax.broadcasted_iota(jnp.int32, shape, 0)
    row = jnp.where(row >= WIN, row - WIN, row) - 4 * window
    col = lax.broadcasted_iota(jnp.int32, shape, 1) - 4 * window
    row_ok = (row >= 0) & (row < 100)
    col_ok = (col >= 0) & (col < 100)
    same = row_ok & col_ok & ((row >= 50) == (col >= 50))
    return jnp.where(same, 0.0, BIG_NEG).astype(F32)


def window_rows_ok(window):
    row = lax.broadcasted_iota(jnp.int32, (2 * WIN, 1), 0)
    row = jnp.where(row >= WIN, row - WIN, row) - 4 * window
    return (row >= 0) & (row < 100)


def stack_heads(values, first):
    zero = jnp.zeros_like(values)
    return jnp.concatenate(
        [jnp.where(first, values, zero), jnp.where(first, zero, values)], axis=0
    )


def first_head_lanes():
    return lax.broadcasted_iota(jnp.int32, (WIN, 2 * HEAD_DIM), 1) < HEAD_DIM


def window_probs(query, key, mask, rows_ok):
    scores = dot_nt(query, key) * (HEAD_DIM**-0.5) + mask
    top = jnp.max(scores, axis=-1, keepdims=True)
    expo = jnp.exp(scores - top)
    total = jnp.sum(expo, axis=-1, keepdims=True)
    return expo * jnp.where(rows_ok, 1.0 / total, 0.0)


def join_windows(parts):
    first, second, third = parts
    over = WIN - WIN_STEP
    return jnp.concatenate(
        [
            first[:WIN_STEP],
            first[WIN_STEP:] + second[:over],
            second[over:WIN_STEP],
            second[WIN_STEP:] + third[:over],
            third[over:],
        ],
        axis=0,
    )


def attention_forward_kernel(layer, count, place, a_ref, wqkv, wproj, bqv, *refs):
    pieces = refs[:count] if count > 1 else (refs[0], ATTN_SPAN)
    qkv_ref, probs_ref, o_ref, r_ref, wq, wp, bs, rows, total, masks, sems = refs[count:]
    own_quarter = place[DEPTH] if count > 1 else None
    copy = start_rows(a_ref, rows, sems)
    start_attention_copies(layer, place, wqkv, wproj, bqv, pieces, wq, wp, sems, bs)
    for window in range(3):
        masks[window] = window_masks(window)
    copy.wait()

    def chunk_step(chunk, carry):
        wait_chunk(chunk, (wq, wp), sems)
        wait_bias(chunk, bs, sems, own_quarter)
        bias = jnp.sum(bs[chunk].astype(F32), axis=0, keepdims=True)
        qkv_ref[chunk] = (dot_nn(rows[...], wq[chunk]) + bias).astype(BF16)
        first = first_head_lanes()
        outs = []
        for window in range(3):
            span = pl.ds(window * WIN_STEP, WIN)
            query = stack_heads(qkv_ref[chunk, span, 0:128], first)
            probs = window_probs(
                query, qkv_ref[chunk, span, 128:256], masks[window], window_rows_ok(window)
            )
            probs_ref[chunk, window] = probs.astype(BF16)
            mixed = dot_nn(probs.astype(BF16), qkv_ref[chunk, span, 256:384])
            outs.append(jnp.where(first, mixed[:WIN], mixed[WIN:]))
        o_ref[chunk] = join_windows(outs).astype(BF16)
        add_part(chunk, total, dot_nn(o_ref[chunk], wp[chunk]))
        return carry

    lax.fori_loop(0, 4, chunk_step, 0, unroll=True)
    r_ref[...] = total[...].astype(BF16)


def add_part(chunk, total, part):
    @pl.when(chunk == 0)
    def _():
        total[...] = part

    @pl.when(chunk > 0)
    def _():
        total[...] += part


def run_attention_forward(layer, place, rows, weights, pieces):
    width = rows.shape[1]
    return pl.pallas_call(
        functools.partial(attention_forward_kernel, layer, len(pieces)),
        out_shape=(
            jax.ShapeDtypeStruct((4, ROWS, 384), BF16),
            jax.ShapeDtypeStruct((4, 3, 2 * WIN, WIN), BF16),
            jax.ShapeDtypeStruct((4, ROWS, 128), BF16),
            jax.ShapeDtypeStruct((ROWS, width), BF16),
        ),
        in_specs=[SM, HB, HB, HB, VM] + [HB] * len(pieces),
        out_specs=(VM,) * 4,
        scratch_shapes=[
            pltpu.VMEM((4, width, 384), BF16),
            pltpu.VMEM((4, 128, width), BF16),
            pltpu.VMEM((4, 16, 384), BF16),
            pltpu.VMEM((ROWS, width), BF16),
            pltpu.VMEM((ROWS, width), F32),
            pltpu.VMEM((3, 2 * WIN, WIN), F32),
            pltpu.SemaphoreType.DMA((4, 4)),
        ],
        **params(7),
    )(place, rows, *weights, *pieces)


def attention_backward_kernel(
    layer, count, place, g_ref, qkv_ref, probs_ref, wqkv, wproj, *refs
):
    pieces = refs[:count] if count > 1 else (refs[0], ATTN_SPAN)
    dqkv_ref, sums_ref, d_ref, wq, wp, rows, total, gmix, sems = refs[count:]
    copy = start_rows(g_ref, rows, sems)
    start_attention_copies(layer, place, wqkv, wproj, None, pieces, wq, wp, sems)
    copy.wait()

    def chunk_step(chunk, carry):
        wait_chunk(chunk, (wq, wp), sems)
        gmix[...] = dot_nt(rows[...], wp[chunk]).astype(BF16)
        first = first_head_lanes()
        scale = HEAD_DIM**-0.5
        outs = []
        for window in range(3):
            span = pl.ds(window * WIN_STEP, WIN)
            query = stack_heads(qkv_ref[chunk, span, 0:128], first)
            key = qkv_ref[chunk, span, 128:256]
            grad = stack_heads(gmix[span, :], first)
            probs = probs_ref[chunk, window]
            gprobs = dot_nt(grad, qkv_ref[chunk, span, 256:384])
            gvalue = dot_tn(probs, grad)
            probs = probs.astype(F32)
            inner = jnp.sum(gprobs * probs, axis=-1, keepdims=True)
            gscores = (probs * (gprobs - inner)).astype(BF16)
            gquery = dot_nn(gscores, key) * scale
            gkey = dot_tn(gscores, query) * scale
            outs.append((jnp.where(first, gquery[:WIN], gquery[WIN:]), gkey, gvalue))
        joined = jnp.concatenate(
            [join_windows([out[item] for out in outs]) for item in range(3)], axis=1
        ).astype(BF16)
        dqkv_ref[chunk] = joined
        sums_ref[chunk] = jnp.broadcast_to(
            jnp.sum(joined.astype(F32), axis=0, keepdims=True), (8, 384)
        )
        add_part(chunk, total, dot_nt(dqkv_ref[chunk], wq[chunk]))
        return carry

    lax.fori_loop(0, 4, chunk_step, 0, unroll=True)
    d_ref[...] = total[...].astype(BF16)


def run_attention_backward(layer, place, grad, qkv, probs, weights, pieces):
    width = grad.shape[1]
    return pl.pallas_call(
        functools.partial(attention_backward_kernel, layer, len(pieces)),
        out_shape=(
            jax.ShapeDtypeStruct((4, ROWS, 384), BF16),
            jax.ShapeDtypeStruct((4, 8, 384), F32),
            jax.ShapeDtypeStruct((ROWS, width), BF16),
        ),
        in_specs=[SM, HB, VM, VM, HB, HB] + [HB] * len(pieces),
        out_specs=(VM,) * 3,
        scratch_shapes=[
            pltpu.VMEM((4, width, 384), BF16),
            pltpu.VMEM((4, 128, width), BF16),
            pltpu.VMEM((ROWS, width), BF16),
            pltpu.VMEM((ROWS, width), F32),
            pltpu.VMEM((ROWS, 128), BF16),
            pltpu.SemaphoreType.DMA((4, 4)),
        ],
        **params(12),
    )(place, grad, qkv, probs, *weights[:2], *pieces)


def gelu_pair(u):
    size = jnp.abs(u) * (0.5**0.5)
    t = 1.0 / (1.0 + 0.3275911 * size)
    poly = t * (
        0.254829592
        + t * (-0.284496736 + t * (1.421413741 + t * (-1.453152027 + t * 1.061405429)))
    )
    bell = jnp.exp(-0.5 * u * u)
    tail = 0.5 * poly * bell
    phi = jnp.where(u >= 0.0, 1.0 - tail, tail)
    return u * phi, phi + u * bell * 0.3989422804014327


def mlp_forward_kernel(
    a_ref, pieces, h_ref, slope_ref, m_ref, w1, w2, bs, rows, total, sems
):
    copy = start_rows(a_ref, rows, sems)
    start_mlp_copies((pieces, MLP_SPAN), w1, w2, sems, bs)
    copy.wait()

    def chunk_step(chunk, carry):
        wait_chunk(chunk, (w1, w2), sems)
        wait_bias(chunk, bs, sems)
        bias = jnp.sum(bs[chunk].astype(F32), axis=0, keepdims=True)
        value, slope = gelu_pair(dot_nn(rows[...], w1[chunk]) + bias)
        h_ref[chunk] = value.astype(BF16)
        slope_ref[chunk] = slope.astype(BF16)
        add_part(chunk, total, dot_nn(h_ref[chunk], w2[chunk]))
        return carry

    lax.fori_loop(0, 4, chunk_step, 0, unroll=True)
    m_ref[...] = total[...].astype(BF16)


def run_mlp_forward(rows, pieces):
    width = rows.shape[1]
    return pl.pallas_call(
        mlp_forward_kernel,
        out_shape=(
            jax.ShapeDtypeStruct((4, ROWS, 512), BF16),
            jax.ShapeDtypeStruct((4, ROWS, 512), BF16),
            jax.ShapeDtypeStruct((ROWS, width), BF16),
        ),
        in_specs=[HB, HB],
        out_specs=(VM,) * 3,
        scratch_shapes=[
            pltpu.VMEM((4, width, 512), BF16),
            pltpu.VMEM((4, 512, width), BF16),
            pltpu.VMEM((4, 16, 512), BF16),
            pltpu.VMEM((ROWS, width), BF16),
            pltpu.VMEM((ROWS, width), F32),
            pltpu.SemaphoreType.DMA((4, 4)),
        ],
        **params(8),
    )(rows, pieces)


def mlp_backward_kernel(
    g_ref, slope_ref, pieces, du_ref, sums_ref, d_ref, w1, w2, rows, total, sems
):
    copy = start_rows(g_ref, rows, sems)
    start_mlp_copies((pieces, MLP_SPAN), w1, w2, sems)
    copy.wait()

    def chunk_step(chunk, carry):
        wait_chunk(chunk, (w1, w2), sems)
        grad = dot_nt(rows[...], w2[chunk]) * slope_ref[chunk].astype(F32)
        grad = grad.astype(BF16)
        du_ref[chunk] = grad
        sums_ref[chunk] = jnp.broadcast_to(
            jnp.sum(grad.astype(F32), axis=0, keepdims=True), (8, 512)
        )
        add_part(chunk, total, dot_nt(du_ref[chunk], w1[chunk]))
        return carry

    lax.fori_loop(0, 4, chunk_step, 0, unroll=True)
    d_ref[...] = total[...].astype(BF16)


def run_mlp_backward(grad, slope, pieces):
    width = grad.shape[1]
    return pl.pallas_call(
        mlp_backward_kernel,
        out_shape=(
            jax.ShapeDtypeStruct((4, ROWS, 512), BF16),
            jax.ShapeDtypeStruct((4, 8, 512), F32),
            jax.ShapeDtypeStruct((ROWS, width), BF16),
        ),
        in_specs=[HB, VM, HB],
        out_specs=(VM,) * 3,
        scratch_shapes=[
            pltpu.VMEM((4, width, 512), BF16),
            pltpu.VMEM((4, 512, width), BF16),
            pltpu.VMEM((ROWS, width), BF16),
            pltpu.VMEM((ROWS, width), F32),
            pltpu.SemaphoreType.DMA((4, 4)),
        ],
        **params(7),
    )(grad, slope, pieces)


SEND, AWAY, NEAR, ALL = 0, 1, 2, 3
STAGE_SLOTS = (((0, 1), (1, 1)), ((1, 0),), ((0, 0),), ((0, 0), (0, 1), (1, 0), (1, 1)))


def weight_grad_kernel(
    stage, place, x1_own, x1_far, y1_own, y1_far, x2_own, x2_far, y2_own, y2_far, *refs
):
    slots = STAGE_SLOTS[stage]
    (xs, y1, y2, turned, added, sems), refs = refs[-6:], refs[:-6]
    out_ref = refs[-1]
    got = [refs[0].at[0 if stage == NEAR else 1], *refs[1:-1]] if stage in (AWAY, NEAR) else []
    outs = [out_ref.at[slot] for slot in range(len(slots))] if len(slots) > 1 else [out_ref]
    copies = []
    for slot, (side, core) in enumerate(slots):
        if stage != ALL:
            side, core = place[SIDE] ^ side, place[CORE] ^ core
        start = aligned(4 * side + core, 128)
        for index, sources in enumerate(((x1_own, x1_far), (x2_own, x2_far))):
            for half, source in enumerate(sources):
                for run in range(2):
                    copies.append(
                        pltpu.make_async_copy(
                            source.at[:, pl.ds(start + 256 * run, 128)],
                            xs.at[index, slot, pl.ds(ROWS * half, ROWS), pl.ds(128 * run, 128)],
                            sems.at[4, 8 * slot + 4 * index + 2 * half + run],
                        )
                    )
    for copy in copies:
        copy.start()
    for chunk in range(4):
        for index, (source, target) in enumerate(
            ((y1_own, y1), (y1_far, y1), (y2_own, y2), (y2_far, y2))
        ):
            pltpu.make_async_copy(
                source.at[chunk],
                target.at[chunk, pl.ds(ROWS * (index % 2), ROWS)],
                sems.at[chunk, index],
            ).start()
        for index, source in enumerate(got):
            pltpu.make_async_copy(
                source.at[chunk], added.at[index, chunk], sems.at[chunk, 4 + index]
            ).start()
    for copy in copies:
        copy.wait()
    for slot in range(len(slots)):
        for index in range(2):
            turned[index, slot] = xs[index, slot].T
    span1 = y1.shape[2]

    def chunk_step(chunk, carry):
        for index, target in enumerate((y1, y1, y2, y2)):
            half = target.at[chunk, pl.ds(ROWS * (index % 2), ROWS)]
            pltpu.make_async_copy(half, half, sems.at[chunk, index]).wait()
        for index in range(len(got)):
            array = added.at[index, chunk]
            pltpu.make_async_copy(array, array, sems.at[chunk, 4 + index]).wait()
        for slot, out in enumerate(outs):
            first = dot_nn(turned[0, slot], y1[chunk])
            second = dot_nn(turned[1, slot], y2[chunk])
            for index in range(len(got)):
                first += added[index, chunk, :, 0:span1].astype(F32)
                second += added[index, chunk, :, span1:].astype(F32)
            out[chunk, :, 0:span1] = first.astype(BF16)
            out[chunk, :, span1:] = second.astype(BF16)
        return carry

    lax.fori_loop(0, 4, chunk_step, 0, unroll=True)


def run_weight_grad(stage, place, x1, y1, x2, y2, *got):
    rows, width = 2 * ROWS, x1[0].shape[1]
    span1, span2 = y1[0].shape[2], y2[0].shape[2]
    part = width // 4
    shape = (4, part, span1 + span2)
    slots = len(STAGE_SLOTS[stage])
    return pl.pallas_call(
        functools.partial(weight_grad_kernel, stage),
        out_shape=jax.ShapeDtypeStruct((slots, *shape) if slots > 1 else shape, BF16),
        in_specs=[SM] + [HB] * (8 + len(got)),
        out_specs=VM,
        scratch_shapes=[
            pltpu.VMEM((2, slots, rows, part), BF16),
            pltpu.VMEM((4, rows, span1), BF16),
            pltpu.VMEM((4, rows, span2), BF16),
            pltpu.VMEM((2, slots, part, rows), BF16),
            pltpu.VMEM((max(len(got), 1), *shape), BF16),
            pltpu.SemaphoreType.DMA((5, 32)),
        ],
        **params((4 if span1 > 384 else 3) * slots + 2),
    )(place, *x1, *y1, *x2, *y2, *got)


def add_depth_kernel(place, *refs):
    parts, (stay, move) = refs[:-2], refs[-2:]
    total = parts[0][...].astype(F32)
    for part in parts[1:]:
        total += part[...].astype(F32)
    half = total.shape[0] // 2
    low, high = total[:half], total[half:]
    even = place[PAIR] == 0
    stay[...] = jnp.where(even, low, high).astype(BF16)
    move[...] = jnp.where(even, high, low).astype(BF16)


def run_add_depth(place, parts):
    rows, span = parts[0].shape
    shape = jax.ShapeDtypeStruct((rows // 2, span), BF16)
    return pl.pallas_call(
        add_depth_kernel,
        out_shape=(shape, shape),
        in_specs=[SM] + [VM] * len(parts),
        out_specs=(VM, VM),
        **params(2),
    )(place, *parts)


def collect_kernel(place, fc2_last, *refs):
    out = refs[-1]
    layers = (len(refs) - 1) // 6
    narrow, wide = aligned(place[PAIR], 128), aligned(place[PAIR], 512)
    out[...] = jnp.zeros(out.shape, F32)
    for layer in range(layers):
        sums1, sums2, qv_own, qv_far, fc1_own, fc1_far = refs[6 * layer : 6 * layer + 6]
        row = 12 * layer
        out[row : row + 2, :] = sums1[0:2, :]
        out[row + 2 : row + 3, :] = sums2[2:3, :]
        out[row + 3 : row + 5, :] = sums2[0:2, :]
        above = refs[6 * layer + 6][2:3, :] if layer + 1 < layers else fc2_last[0:1, :]
        out[row + 5 : row + 6, :] = above
        for depth in range(4):
            qv = qv_own[depth, 0:1, :] + qv_far[depth, 0:1, :]
            for item in range(2):
                out[row + 6 + item, pl.ds(depth * 256 + narrow, 128)] = qv[
                    0, 256 * item : 256 * item + 128
                ]
            fc1 = fc1_own[depth, 0:1, :] + fc1_far[depth, 0:1, :]
            out[pl.ds(row + 8 + depth, 1), pl.ds(wide, 512)] = fc1


def run_collect(place, fc2_last, parts):
    layers = len(parts) // 6
    return pl.pallas_call(
        collect_kernel,
        out_shape=jax.ShapeDtypeStruct((12 * layers, 1024), F32),
        in_specs=[SM] + [VM] * (1 + len(parts)),
        out_specs=VM,
        **params(2),
    )(place, fc2_last, *parts)


def release_kernel(place, total, *outs):
    rows, (qv, fc1) = outs[:6], outs[6:]
    quarter = aligned(place[DEPTH], 256)
    for layer in range(fc1.shape[0]):
        for index, out in enumerate(rows):
            out[layer : layer + 1, :] = total[pl.ds(12 * layer + index, 1), :]
        for item in range(2):
            qv[layer, item : item + 1, :] = total[
                pl.ds(12 * layer + 6 + item, 1), pl.ds(quarter, 256)
            ]
        fc1[layer : layer + 1, :] = total[pl.ds(12 * layer + 8 + place[DEPTH], 1), :]


def run_release(place, total):
    layers = total.shape[0] // 12
    row = jax.ShapeDtypeStruct((layers, 1024), F32)
    return pl.pallas_call(
        release_kernel,
        out_shape=(row,) * 6 + (jax.ShapeDtypeStruct((layers, 2, 256), F32), row),
        in_specs=[SM, VM],
        out_specs=(VM,) * 8,
        **params(2),
    )(place, total)


def finish_kernel(place, *refs):
    layers = (len(refs) - 4) // 4
    ins, (qkv, proj, fc1, fc2) = refs[: 4 * layers], refs[4 * layers :]
    for layer in range(layers):
        for side in range(2):
            attn, mlp = ins[4 * layer + side], ins[4 * layer + 2 + side]
            pair = place[PAIR] if side == 0 else 1 - place[PAIR]
            narrow, wide = aligned(pair, 128), aligned(pair, 512)
            for item in range(3):
                qkv[layer, item, :, pl.ds(narrow, 128)] = attn[
                    :, item * 128 : item * 128 + 128
                ].astype(F32)
            proj[layer, pl.ds(narrow, 128), :] = attn[:, 384:512].astype(F32).T
            fc1[layer, :, pl.ds(wide, 512)] = mlp[:, 0:512].astype(F32)
            fc2[layer, pl.ds(wide, 512), :] = mlp[:, 512:1024].astype(F32).T


def run_finish(place, parts):
    rows = parts[0].shape[0]
    return pl.pallas_call(
        finish_kernel,
        out_shape=(
            jax.ShapeDtypeStruct((2, 3, rows, 256), F32),
            jax.ShapeDtypeStruct((2, 256, rows), F32),
            jax.ShapeDtypeStruct((2, rows, 1024), F32),
            jax.ShapeDtypeStruct((2, 1024, rows), F32),
        ),
        in_specs=[SM] + [VM] * len(parts),
        out_specs=(VM,) * 4,
        **params(4),
    )(place, *parts)


def on_device(*args):
    (
        images_in, out_cotangent, norm1_gain, norm1_bias, qkv_weight, qv_bias, proj_weight,
        proj_bias, norm2_gain, norm2_bias, fc1_weight, fc1_bias, fc2_weight, fc2_bias,
    ) = args
    images, seq, _ = images_in.shape
    layers = qkv_weight.shape[0]
    n_far, n_mp = lax.axis_size("far"), lax.axis_size("mp")
    mine = images // n_mp

    side, pair, core = lax.axis_index("y"), lax.axis_index("x"), lax.axis_index("core")
    depth = lax.axis_index("mp")
    here = jnp.stack(
        [
            side, core, pair, depth,
            side * 2 + core, (1 - side) * 2 + core, side * 2 + 1 - core, (1 - side) * 2 + 1 - core,
        ]
    ).astype(jnp.int32)

    def swap(value, axis):
        return lax.ppermute(value, axis, [(0, 1), (1, 0)])

    def shift(value, step):
        return lax.ppermute(
            value, "mp", [(index, (index + step) % n_mp) for index in range(n_mp)]
        )

    def after(value, *others):
        return lax.optimization_barrier((value, *others))[0]

    wqkv = qkv_weight.transpose(0, 2, 1, 3)
    attn_weights = (wqkv, proj_weight, qv_bias)
    packed = run_pack(here, wqkv, proj_weight, fc1_weight, fc2_weight, qv_bias, fc1_bias)
    attn_pieces, mlp_pieces = [[]], []
    moved = []
    for step in (1, 3, 2):
        same = shift(packed[0], step)
        moved.append(same)
        other = swap(same, "y")
        attn_pieces[0].append((step, [same, other, swap(same, "core"), swap(other, "core")]))
    attn_pieces[0] = [array for _, arrays in sorted(attn_pieces[0]) for array in arrays]
    stream, normed = run_enter(here, images_in, mine, norm1_gain[0], norm1_bias[0])
    grad, grad_b, fc2_sum = run_enter_back(here, out_cotangent, mine)
    grad_b_far = swap(grad_b, "x")
    gathered = []
    for index in (1, 2):
        gathered = lax.all_gather((after(packed[index], *gathered) if gathered else packed[index]), ("y", "core", "mp"))
        value = gathered.reshape(2, 2, n_mp, *gathered.shape[1:])
        mlp_pieces.append(value)
        attn_pieces.append([value])
        gathered = [gathered]

    def both(run, own, far, *waits):
        results = run(own)
        return list(zip(results, run(after(far, *waits) if waits else far)))

    saved = []
    for layer in range(layers):
        normed_far = swap(normed, "x")
        qkv, probs, mixed, part = both(
            lambda rows: run_attention_forward(layer, here, rows, attn_weights, attn_pieces[layer]),
            normed, normed_far,
        )
        middle, normed2 = run_residual_norm(
            stream, part[0], swap(part[1], "x"), proj_bias[layer], norm2_gain[layer],
            norm2_bias[layer],
        )
        normed2_far = swap(normed2, "x")
        active, slope, part = both(
            lambda rows: run_mlp_forward(rows, mlp_pieces[layer]),
            after(normed2, grad_b_far), normed2_far,
        )
        saved.append(
            (stream, (normed, normed_far), list(zip(qkv, probs)), mixed, middle, (normed2, normed2_far), active, slope)
        )
        if layer + 1 < layers:
            stream, normed = run_residual_norm(
                middle, part[0], swap(part[1], "x"), fc2_bias[layer], norm1_gain[layer + 1],
                norm1_bias[layer + 1],
            )
        else:
            last = run_residual(middle, part[0], swap(part[1], "x"), fc2_bias[layer])

    class Sum:
        def __init__(self, *arrays):
            self.arrays = arrays
            self.core = swap(run_weight_grad(SEND, here, *arrays), "core")

        def away(self):
            kept = run_weight_grad(AWAY, here, *self.arrays, self.core)
            self.side = swap(kept, "y")
            return kept

        def near(self, *waits):
            side = after(self.side, *waits) if waits else self.side
            kept = run_weight_grad(NEAR, here, *self.arrays, self.core, side)
            flat = kept.reshape(-1, kept.shape[-1])
            self.total = lax.psum_scatter(flat, "mp", tiled=True)
            return kept

        def result(self):
            return run_add_depth(here, [self.total])

    class SumAtOnce(Sum):
        def __init__(self, *arrays):
            grads = run_weight_grad(ALL, here, *arrays)
            flat = grads.reshape(-1, grads.shape[-1])
            self.total = lax.psum_scatter(flat, ("y", "core", "mp"), tiled=True)

    attn, mlp, groups = None, None, []
    small = [None] * layers
    for layer in reversed(range(layers)):
        stream, normed, qkv, mixed, middle, normed2, active, slope = saved[layer]
        slopes, qkvs = list(slope), list(qkv)
        du, fc1_sum, part = both(
            lambda rows: run_mlp_backward(rows, slopes.pop(0), mlp_pieces[layer]),
            grad_b, grad_b_far, *([attn.away()] if attn else []),
        )
        mlp = (SumAtOnce if layer else Sum)(normed2, du, (grad_b, grad_b_far), active)
        if layer:
            last = after(last, mlp.total)
        grad, grad_b, sums2 = run_norm_back(
            grad, part[0], swap(part[1], "x"), middle, norm2_gain[layer]
        )
        grad_b_far = swap(grad_b, "x")
        dqkv, qv_sum, part = both(
            lambda rows: run_attention_backward(
                layer, here, rows, *qkvs.pop(0), attn_weights, attn_pieces[layer]
            ),
            grad_b, grad_b_far, *([] if layer else [mlp.away()]),
        )
        above, attn = attn, Sum(normed, dqkv, (grad_b, grad_b_far), mixed)
        if above:
            grad = after(grad, above.near())
        grad, grad_b, sums1 = run_norm_back(
            grad, part[0], swap(part[1], "x"), stream, norm1_gain[layer]
        )
        if layer:
            grad_b_far = swap(grad_b, "x")
        small[layer] = [sums1, sums2, *qv_sum, *fc1_sum]
        groups = [attn, mlp, *groups]

    block_out = run_leave(here, [lax.all_gather(last, "mp")], seq, mine, BF16)
    parts = [shift(grad_b, step) for step in (1, 3, 2)]
    attn.core = after(attn.core, grad_b)
    attn.away()
    kept = mlp.near()
    kept = attn.near(kept, block_out, *parts)
    parts = [after(part, kept) for part in parts]
    input_grad = run_leave(here, [grad_b, *parts], seq, mine, F32)
    total = run_collect(here, fc2_sum, [part for group in small for part in group])
    total = after(total, kept)
    for axis in ("core", "x", "y"):
        total = total + swap(total, axis)
    for bit in range(n_far.bit_length() - 1):
        pairs = [(index, index ^ (1 << bit)) for index in range(n_far)]
        total = total + lax.ppermute(total, "far", pairs)
    total = after(total, *parts)
    for bit in range(n_mp.bit_length() - 1):
        pairs = [(index, index ^ (1 << bit)) for index in range(n_mp)]
        total = total + lax.ppermute(total, "mp", pairs)
    n1g, n1b, pb, n2g, n2b, f2b, qv, fc1 = run_release(here, total)

    ready = [group.result() for group in groups]
    if n_far == 1:
        parts = [part for stay, move in ready for part in (stay, swap(move, "x"))]
    else:
        parts = [part for stay, move in ready for part in spread_rows(stay, move)]
    g_qkv, g_proj, g_fc1, g_fc2 = run_finish(here, parts)
    block_out, input_grad = (
        value.reshape(seq, images, -1).transpose(1, 0, 2) for value in (block_out, input_grad)
    )
    return (
        block_out, input_grad, n1g, n1b, g_qkv.transpose(0, 2, 1, 3), qv, g_proj, pb, n2g, n2b,
        g_fc1, fc1, g_fc2, f2b,
    )


def spread_rows(stay, move):
    pair = lax.axis_index("x")
    value = jnp.stack(
        [jnp.where(pair == 0, stay, move), jnp.where(pair == 0, move, stay)]
    ).astype(F32)
    value = lax.psum(value, "far")
    value = lax.all_gather(value, ("y", "x", "core"))
    rows, span = value.shape[2:]
    value = value.reshape(2, 2, 2, 2, rows, span).transpose(0, 3, 2, 4, 1, 5)
    value = value.reshape(8 * rows, 2, span)
    count = rows // lax.axis_size("far")
    place = lax.axis_index(("far", "y", "x", "core"))
    value = lax.dynamic_slice_in_dim(value, place * count, count, 0)
    mine = lax.dynamic_index_in_dim(value, pair, 1, keepdims=False)
    other = lax.dynamic_index_in_dim(value, 1 - pair, 1, keepdims=False)
    return mine, other


def solution(mesh):
    n_dp, n_mp = mesh.shape["dp"], mesh.shape["mp"]
    fine = Mesh(mesh.devices.reshape(n_dp // 8, 2, 2, 2, n_mp), ("far", "y", "x", "core", "mp"))
    dp = ("far", "y", "x", "core")
    return jax.shard_map(
        on_device,
        mesh=fine,
        in_specs=(
            P(dp, None, None),
            P(dp, None, None),
            P(),
            P(),
            P(None, None, None, "mp"),
            P(None, None, "mp"),
            P(None, "mp", None),
            P(),
            P(),
            P(),
            P(None, None, "mp"),
            P(None, "mp"),
            P(None, "mp", None),
            P(),
        ),
        out_specs=(
            P(dp, None, None),
            P(dp, None, None),
            P(),
            P(),
            P(None, dp, None, "mp"),
            P(None, None, "mp"),
            P(None, "mp", dp),
            P(),
            P(),
            P(),
            P(None, dp, "mp"),
            P(None, "mp"),
            P(None, "mp", dp),
            P(),
        ),
        check_vma=False,
    )
```

```python
import functools

import jax
import jax.numpy as jnp
from jax import lax
from jax.experimental import pallas as pl
from jax.experimental.pallas import tpu as pltpu
from jax.sharding import Mesh
from jax.sharding import PartitionSpec as P

HEAD_DIM = 64
EPS = 1e-06
F32 = jnp.float32
BF16 = jnp.bfloat16
ROWS = 304
WIN = 112
WIN_STEP = 96
BIG_NEG = -1e30
VMEM_LIMIT = 60 * 1024 * 1024


def dot_nn(a, b):
    return lax.dot_general(a, b, (((1,), (0,)), ((), ())), preferred_element_type=F32)


def dot_nt(a, b):
    return lax.dot_general(a, b, (((1,), (1,)), ((), ())), preferred_element_type=F32)


def dot_tn(a, b):
    return lax.dot_general(a, b, (((0,), (0,)), ((), ())), preferred_element_type=F32)


COST = 4e9


def params(micros):
    return dict(
        compiler_params=pltpu.CompilerParams(vmem_limit_bytes=VMEM_LIMIT),
        cost_estimate=pl.CostEstimate(
            flops=int(micros * COST), bytes_accessed=0, transcendentals=0
        ),
    )


VM = pl.BlockSpec(memory_space=pltpu.VMEM)
SM = pl.BlockSpec(memory_space=pltpu.SMEM)
HB = pl.BlockSpec(memory_space=pl.ANY)


def layer_norm(x, gain, bias):
    mean = jnp.mean(x, axis=-1, keepdims=True)
    centered = x - mean
    variance = jnp.mean(centered * centered, axis=-1, keepdims=True)
    return centered * lax.rsqrt(variance + EPS) * gain + bias


def own_selector(place, seq, mine):
    images = 4 * mine
    row = lax.broadcasted_iota(jnp.int32, (ROWS, images * seq), 0)
    col = lax.broadcasted_iota(jnp.int32, (ROWS, images * seq), 1)
    token = col // images
    image = col - token * images - place[DEPTH] * mine
    hit = (image >= 0) & (image < mine) & (row == image * seq + token)
    return jnp.where(hit, 1.0, 0.0).astype(BF16)


def enter_kernel(seq, mine, place, x_ref, gain_ref, beta_ref, x1_ref, a_ref):
    x = dot_nn(own_selector(place, seq, mine), x_ref[...])
    x1_ref[...] = x
    a_ref[...] = layer_norm(x, gain_ref[...], beta_ref[...]).astype(BF16)


def enter_back_kernel(seq, mine, place, x_ref, g_ref, gb_ref, sum_ref):
    g = dot_nn(own_selector(place, seq, mine), x_ref[...])
    g_ref[...] = g
    gb_ref[...] = g.astype(BF16)
    sum_ref[...] = jnp.broadcast_to(jnp.sum(g, axis=0, keepdims=True), sum_ref.shape)


def leave_kernel(seq, mine, place, *refs):
    parts, out_ref = refs[:-1], refs[-1]
    images = 4 * mine
    count = images * seq
    row = lax.broadcasted_iota(jnp.int32, (count, ROWS), 0)
    col = lax.broadcasted_iota(jnp.int32, (count, ROWS), 1)
    token = row // images
    want = row - token * images
    total = None
    for index, step in enumerate((0, 1, 3, 2)):
        depth, rows = index, parts[0].at[index] if len(parts) == 1 else parts[index]
        if len(parts) > 1:
            depth = (place[DEPTH] - step) & 3
        image = want - depth * mine
        hit = (image >= 0) & (image < mine) & (col == image * seq + token)
        part = dot_nn(jnp.where(hit, 1.0, 0.0).astype(BF16), rows[...])
        total = part if total is None else total + part
    out_ref[...] = total.astype(out_ref.dtype)


def residual_norm_kernel(
    x_ref, own_ref, far_ref, bias_ref, gain_ref, beta_ref, x1_ref, a_ref, far, sem
):
    copy = pltpu.make_async_copy(far_ref, far, sem)
    copy.start()
    keep = lax.broadcasted_iota(jnp.int32, (ROWS, 1), 0) < 300
    bias = jnp.where(keep, bias_ref[...], 0.0)
    copy.wait()
    x1 = x_ref[...] + own_ref[...].astype(F32) + far[...].astype(F32) + bias
    x1_ref[...] = x1
    a_ref[...] = layer_norm(x1, gain_ref[...], beta_ref[...]).astype(BF16)


def residual_kernel(x_ref, own_ref, far_ref, bias_ref, x1_ref, far, sem):
    copy = pltpu.make_async_copy(far_ref, far, sem)
    copy.start()
    copy.wait()
    x1 = x_ref[...] + own_ref[...].astype(F32) + far[...].astype(F32) + bias_ref[...]
    x1_ref[...] = x1.astype(BF16)


def norm_back_kernel(
    g_ref, own_ref, far_ref, x_ref, gain_ref, g1_ref, g1b_ref, sums_ref, far, sem
):
    copy = pltpu.make_async_copy(far_ref, far, sem)
    copy.start()
    x = x_ref[...]
    mean = jnp.mean(x, axis=-1, keepdims=True)
    centered = x - mean
    variance = jnp.mean(centered * centered, axis=-1, keepdims=True)
    inverse = lax.rsqrt(variance + EPS)
    xhat = centered * inverse
    copy.wait()
    da = own_ref[...].astype(F32) + far[...].astype(F32)
    inner = da * gain_ref[...]
    mean_inner = jnp.mean(inner, axis=-1, keepdims=True)
    mean_proj = jnp.mean(inner * xhat, axis=-1, keepdims=True)
    g1 = g_ref[...] + inverse * (inner - mean_inner - xhat * mean_proj)
    g1_ref[...] = g1
    g1b_ref[...] = g1.astype(BF16)
    sums_ref[...] = jnp.zeros(sums_ref.shape, F32)
    sums_ref[0:1, :] = jnp.sum(da * xhat, axis=0, keepdims=True)
    sums_ref[1:2, :] = jnp.sum(da, axis=0, keepdims=True)
    sums_ref[2:3, :] = jnp.sum(g1, axis=0, keepdims=True)


def run_enter(place, images, mine, gain, beta):
    count, seq, width = images.shape
    flat = images.transpose(1, 0, 2).reshape(count * seq, width)
    return pl.pallas_call(
        functools.partial(enter_kernel, seq, mine),
        out_shape=(
            jax.ShapeDtypeStruct((ROWS, width), F32),
            jax.ShapeDtypeStruct((ROWS, width), BF16),
        ),
        in_specs=[SM, VM, VM, VM],
        out_specs=(VM, VM),
        **params(5),
    )(place, flat, gain[None], beta[None])


def run_enter_back(place, images, mine):
    count, seq, width = images.shape
    flat = images.transpose(1, 0, 2).reshape(count * seq, width)
    return pl.pallas_call(
        functools.partial(enter_back_kernel, seq, mine),
        out_shape=(
            jax.ShapeDtypeStruct((ROWS, width), F32),
            jax.ShapeDtypeStruct((ROWS, width), BF16),
            jax.ShapeDtypeStruct((8, width), F32),
        ),
        in_specs=[SM, VM],
        out_specs=(VM, VM, VM),
        **params(5),
    )(place, flat)


def run_leave(place, parts, seq, mine, dtype):
    images, width = 4 * mine, parts[0].shape[-1]
    flat = pl.pallas_call(
        functools.partial(leave_kernel, seq, mine),
        out_shape=jax.ShapeDtypeStruct((images * seq, width), dtype),
        in_specs=[SM] + [VM] * len(parts),
        out_specs=VM,
        **params(9),
    )(place, *parts)
    return flat


def run_residual_norm(x, own, far, bias, gain, beta):
    return pl.pallas_call(
        residual_norm_kernel,
        out_shape=(
            jax.ShapeDtypeStruct(x.shape, F32),
            jax.ShapeDtypeStruct(x.shape, BF16),
        ),
        in_specs=[VM, VM, HB, VM, VM, VM],
        out_specs=(VM, VM),
        scratch_shapes=[pltpu.VMEM((ROWS, x.shape[1]), BF16), pltpu.SemaphoreType.DMA],
        **params(3),
    )(x, own, far, bias[None], gain[None], beta[None])


def run_residual(x, own, far, bias):
    return pl.pallas_call(
        residual_kernel,
        out_shape=jax.ShapeDtypeStruct(x.shape, BF16),
        in_specs=[VM, VM, HB, VM],
        out_specs=VM,
        scratch_shapes=[pltpu.VMEM((ROWS, x.shape[1]), BF16), pltpu.SemaphoreType.DMA],
        **params(2),
    )(x, own, far, bias[None])


def run_norm_back(g, own, far, x, gain):
    return pl.pallas_call(
        norm_back_kernel,
        out_shape=(
            jax.ShapeDtypeStruct(x.shape, F32),
            jax.ShapeDtypeStruct(x.shape, BF16),
            jax.ShapeDtypeStruct((8, x.shape[1]), F32),
        ),
        in_specs=[VM, VM, HB, VM, VM],
        out_specs=(VM, VM, VM),
        scratch_shapes=[pltpu.VMEM((ROWS, x.shape[1]), BF16), pltpu.SemaphoreType.DMA],
        **params(4),
    )(g, own, far, x, gain[None])


SIDE, CORE, PAIR, DEPTH, PARTS = 0, 1, 2, 3, 4

ATTN_ROWS, MLP_ROWS = 272, 528
ATTN_SPAN, MLP_SPAN = pl.ds(MLP_ROWS, ATTN_ROWS), pl.ds(0, MLP_ROWS)


def exact_rows(bias):
    high = bias.astype(BF16)
    rest = bias - high.astype(F32)
    mid = rest.astype(BF16)
    low = (rest - mid.astype(F32)).astype(BF16)
    return jnp.concatenate([high, mid, low, jnp.zeros((13, bias.shape[1]), BF16)], axis=0)


def pack_kernel(
    place, wqkv, wproj, w1, w2, bqv, b1, attn0, middle, mlp1, sems
):
    row = aligned(place[PARTS], 256)
    narrow, wide = aligned(place[PAIR], 128), aligned(place[PAIR], 512)
    copies = []
    mlp0, attn1 = middle.at[0:MLP_ROWS], middle.at[MLP_ROWS:]
    for layer, (attn, mlp) in enumerate(((attn0, mlp0), (attn1, mlp1))):
        for item in range(3):
            copies.append(
                (
                    wqkv.at[layer, item, pl.ds(row, 256), pl.ds(narrow, 128)],
                    attn.at[0:256, pl.ds(item * 128, 128)],
                )
            )
        for half in range(2):
            copies.append(
                (
                    wproj.at[layer, pl.ds(narrow, 128), pl.ds(row + half * 128, 128)],
                    attn.at[pl.ds(half * 128, 128), 384:512],
                )
            )
            copies.append(
                (
                    w2.at[layer, pl.ds(wide + half * 256, 256), pl.ds(row, 256)],
                    mlp.at[256:512, pl.ds(half * 256, 256)],
                )
            )
        copies.append(
            (w1.at[layer, pl.ds(row, 256), pl.ds(wide, 512)], mlp.at[0:256, :])
        )
    copies = [
        pltpu.make_async_copy(src, dst, sems.at[index])
        for index, (src, dst) in enumerate(copies)
    ]
    for copy in copies:
        copy.start()
    for layer, (attn, mlp) in enumerate(((attn0, mlp0), (attn1, mlp1))):
        zero = jnp.zeros((1, 128), F32)
        bias = [bqv[layer, pl.ds(item, 1), pl.ds(narrow, 128)] for item in range(2)]
        attn[256:272, :] = exact_rows(jnp.concatenate([bias[0], zero, bias[1], zero], axis=1))
        mlp[512:528, :] = exact_rows(b1[pl.ds(layer, 1), pl.ds(wide, 512)])
    for copy in copies:
        copy.wait()


def run_pack(place, wqkv, wproj, w1, w2, bqv, b1):
    return pl.pallas_call(
        pack_kernel,
        out_shape=tuple(
            jax.ShapeDtypeStruct((rows, 512), BF16)
            for rows in (ATTN_ROWS, MLP_ROWS + ATTN_ROWS, MLP_ROWS)
        ),
        in_specs=[SM, HB, HB, HB, HB, VM, VM],
        out_specs=(VM, VM, VM),
        scratch_shapes=[pltpu.SemaphoreType.DMA((16,))],
        **params(3),
    )(place, wqkv, wproj, w1, w2, bqv, b1)


def piece_sources(place, pieces, own):
    if not own:
        array, rows = pieces
        return [
            (depth, 2 * side + core, array.at[side, core, depth, rows])
            for depth in range(4)
            for side in range(2)
            for core in range(2)
        ]
    return [
        ((place[DEPTH] - step) & 3, place[PARTS + slot], pieces[4 * step - 4 + slot])
        for step in range(1, 4)
        for slot in range(4)
    ]


def aligned(index, step):
    if isinstance(index, int):
        return index * step
    return pl.multiple_of(index * step, step)


def start_attention_copies(layer, place, wqkv, wproj, bqv, pieces, wq, wp, sems, bs=None):
    own = len(pieces) > 2
    for index, (depth, part, src) in enumerate(piece_sources(place, pieces, own)):
        row = aligned(part, 256)
        pltpu.make_async_copy(
            src.at[0:256, 0:384], wq.at[depth, pl.ds(row, 256), :], sems.at[0, depth]
        ).start()
        for side in range(2):
            pltpu.make_async_copy(
                src.at[pl.ds(side * 128, 128), 384:512],
                wp.at[depth, :, pl.ds(row + side * 128, 128)],
                sems.at[1, depth],
            ).start()
        if bs is not None and index % 4 == 0:
            pltpu.make_async_copy(src.at[256:272, 0:384], bs.at[depth], sems.at[2, depth]).start()
    if own:
        depth, narrow = place[DEPTH], aligned(place[PAIR], 128)
        for item in range(3):
            pltpu.make_async_copy(
                wqkv.at[layer, item, :, pl.ds(narrow, 128)],
                wq.at[depth, :, pl.ds(item * 128, 128)],
                sems.at[0, depth],
            ).start()
        pltpu.make_async_copy(
            wproj.at[layer, pl.ds(narrow, 128), :], wp.at[depth], sems.at[1, depth]
        ).start()
        if bs is not None:
            bias = [bqv[layer, pl.ds(item, 1), pl.ds(narrow, 128)] for item in range(2)]
            zero = jnp.zeros((1, 128), F32)
            bs[depth] = exact_rows(jnp.concatenate([bias[0], zero, bias[1]], axis=1))


def start_mlp_copies(pieces, w1, w2, sems, bs=None):
    for index, (depth, part, src) in enumerate(piece_sources(None, pieces, False)):
        row = part * 256
        pltpu.make_async_copy(
            src.at[0:256, :], w1.at[depth, pl.ds(row, 256), :], sems.at[0, depth]
        ).start()
        for side in range(2):
            pltpu.make_async_copy(
                src.at[256:512, pl.ds(side * 256, 256)],
                w2.at[depth, pl.ds(side * 256, 256), pl.ds(row, 256)],
                sems.at[1, depth],
            ).start()
        if bs is not None and index % 4 == 0:
            pltpu.make_async_copy(src.at[512:528, :], bs.at[depth], sems.at[2, depth]).start()


def start_rows(source, rows, sems):
    copy = pltpu.make_async_copy(source, rows, sems.at[3, 0])
    copy.start()
    return copy


def wait_chunk(chunk, bufs, sems):
    for slot, buf in enumerate(bufs):
        pltpu.make_async_copy(buf.at[chunk], buf.at[chunk], sems.at[slot, chunk]).wait()


def wait_bias(chunk, bs, sems, own=None):
    def wait():
        pltpu.make_async_copy(bs.at[chunk], bs.at[chunk], sems.at[2, chunk]).wait()

    if own is None:
        wait()
    else:
        pl.when(chunk != own)(wait)


def window_masks(window):
    shape = (2 * WIN, WIN)
    row = lax.broadcasted_iota(jnp.int32, shape, 0)
    row = jnp.where(row >= WIN, row - WIN, row) - 4 * window
    col = lax.broadcasted_iota(jnp.int32, shape, 1) - 4 * window
    row_ok = (row >= 0) & (row < 100)
    col_ok = (col >= 0) & (col < 100)
    same = row_ok & col_ok & ((row >= 50) == (col >= 50))
    return jnp.where(same, 0.0, BIG_NEG).astype(F32)


def window_rows_ok(window):
    row = lax.broadcasted_iota(jnp.int32, (2 * WIN, 1), 0)
    row = jnp.where(row >= WIN, row - WIN, row) - 4 * window
    return (row >= 0) & (row < 100)


def stack_heads(values, first):
    zero = jnp.zeros_like(values)
    return jnp.concatenate(
        [jnp.where(first, values, zero), jnp.where(first, zero, values)], axis=0
    )


def first_head_lanes():
    return lax.broadcasted_iota(jnp.int32, (WIN, 2 * HEAD_DIM), 1) < HEAD_DIM


def window_probs(query, key, mask, rows_ok):
    scores = dot_nt(query, key) * (HEAD_DIM**-0.5) + mask
    top = jnp.max(scores, axis=-1, keepdims=True)
    expo = jnp.exp(scores - top)
    total = jnp.sum(expo, axis=-1, keepdims=True)
    return expo * jnp.where(rows_ok, 1.0 / total, 0.0)


def join_windows(parts):
    first, second, third = parts
    over = WIN - WIN_STEP
    return jnp.concatenate(
        [
            first[:WIN_STEP],
            first[WIN_STEP:] + second[:over],
            second[over:WIN_STEP],
            second[WIN_STEP:] + third[:over],
            third[over:],
        ],
        axis=0,
    )


def attention_forward_kernel(layer, count, place, a_ref, wqkv, wproj, bqv, *refs):
    pieces = refs[:count] if count > 1 else (refs[0], ATTN_SPAN)
    qkv_ref, probs_ref, o_ref, r_ref, wq, wp, bs, rows, total, masks, sems = refs[count:]
    own_quarter = place[DEPTH] if count > 1 else None
    copy = start_rows(a_ref, rows, sems)
    start_attention_copies(layer, place, wqkv, wproj, bqv, pieces, wq, wp, sems, bs)
    for window in range(3):
        masks[window] = window_masks(window)
    copy.wait()

    def chunk_step(chunk, carry):
        wait_chunk(chunk, (wq, wp), sems)
        wait_bias(chunk, bs, sems, own_quarter)
        bias = jnp.sum(bs[chunk].astype(F32), axis=0, keepdims=True)
        qkv_ref[chunk] = (dot_nn(rows[...], wq[chunk]) + bias).astype(BF16)
        first = first_head_lanes()
        outs = []
        for window in range(3):
            span = pl.ds(window * WIN_STEP, WIN)
            query = stack_heads(qkv_ref[chunk, span, 0:128], first)
            probs = window_probs(
                query, qkv_ref[chunk, span, 128:256], masks[window], window_rows_ok(window)
            )
            probs_ref[chunk, window] = probs.astype(BF16)
            mixed = dot_nn(probs.astype(BF16), qkv_ref[chunk, span, 256:384])
            outs.append(jnp.where(first, mixed[:WIN], mixed[WIN:]))
        o_ref[chunk] = join_windows(outs).astype(BF16)
        add_part(chunk, total, dot_nn(o_ref[chunk], wp[chunk]))
        return carry

    lax.fori_loop(0, 4, chunk_step, 0, unroll=True)
    r_ref[...] = total[...].astype(BF16)


def add_part(chunk, total, part):
    @pl.when(chunk == 0)
    def _():
        total[...] = part

    @pl.when(chunk > 0)
    def _():
        total[...] += part


def run_attention_forward(layer, place, rows, weights, pieces):
    width = rows.shape[1]
    return pl.pallas_call(
        functools.partial(attention_forward_kernel, layer, len(pieces)),
        out_shape=(
            jax.ShapeDtypeStruct((4, ROWS, 384), BF16),
            jax.ShapeDtypeStruct((4, 3, 2 * WIN, WIN), BF16),
            jax.ShapeDtypeStruct((4, ROWS, 128), BF16),
            jax.ShapeDtypeStruct((ROWS, width), BF16),
        ),
        in_specs=[SM, HB, HB, HB, VM] + [HB] * len(pieces),
        out_specs=(VM,) * 4,
        scratch_shapes=[
            pltpu.VMEM((4, width, 384), BF16),
            pltpu.VMEM((4, 128, width), BF16),
            pltpu.VMEM((4, 16, 384), BF16),
            pltpu.VMEM((ROWS, width), BF16),
            pltpu.VMEM((ROWS, width), F32),
            pltpu.VMEM((3, 2 * WIN, WIN), F32),
            pltpu.SemaphoreType.DMA((4, 4)),
        ],
        **params(7),
    )(place, rows, *weights, *pieces)


def attention_backward_kernel(
    layer, count, place, g_ref, qkv_ref, probs_ref, wqkv, wproj, *refs
):
    pieces = refs[:count] if count > 1 else (refs[0], ATTN_SPAN)
    dqkv_ref, sums_ref, d_ref, wq, wp, rows, total, gmix, sems = refs[count:]
    copy = start_rows(g_ref, rows, sems)
    start_attention_copies(layer, place, wqkv, wproj, None, pieces, wq, wp, sems)
    copy.wait()

    def chunk_step(chunk, carry):
        wait_chunk(chunk, (wq, wp), sems)
        gmix[...] = dot_nt(rows[...], wp[chunk]).astype(BF16)
        first = first_head_lanes()
        scale = HEAD_DIM**-0.5
        outs = []
        for window in range(3):
            span = pl.ds(window * WIN_STEP, WIN)
            query = stack_heads(qkv_ref[chunk, span, 0:128], first)
            key = qkv_ref[chunk, span, 128:256]
            grad = stack_heads(gmix[span, :], first)
            probs = probs_ref[chunk, window]
            gprobs = dot_nt(grad, qkv_ref[chunk, span, 256:384])
            gvalue = dot_tn(probs, grad)
            probs = probs.astype(F32)
            inner = jnp.sum(gprobs * probs, axis=-1, keepdims=True)
            gscores = (probs * (gprobs - inner)).astype(BF16)
            gquery = dot_nn(gscores, key) * scale
            gkey = dot_tn(gscores, query) * scale
            outs.append((jnp.where(first, gquery[:WIN], gquery[WIN:]), gkey, gvalue))
        joined = jnp.concatenate(
            [join_windows([out[item] for out in outs]) for item in range(3)], axis=1
        ).astype(BF16)
        dqkv_ref[chunk] = joined
        sums_ref[chunk] = jnp.broadcast_to(
            jnp.sum(joined.astype(F32), axis=0, keepdims=True), (8, 384)
        )
        add_part(chunk, total, dot_nt(dqkv_ref[chunk], wq[chunk]))
        return carry

    lax.fori_loop(0, 4, chunk_step, 0, unroll=True)
    d_ref[...] = total[...].astype(BF16)


def run_attention_backward(layer, place, grad, qkv, probs, weights, pieces):
    width = grad.shape[1]
    return pl.pallas_call(
        functools.partial(attention_backward_kernel, layer, len(pieces)),
        out_shape=(
            jax.ShapeDtypeStruct((4, ROWS, 384), BF16),
            jax.ShapeDtypeStruct((4, 8, 384), F32),
            jax.ShapeDtypeStruct((ROWS, width), BF16),
        ),
        in_specs=[SM, HB, VM, VM, HB, HB] + [HB] * len(pieces),
        out_specs=(VM,) * 3,
        scratch_shapes=[
            pltpu.VMEM((4, width, 384), BF16),
            pltpu.VMEM((4, 128, width), BF16),
            pltpu.VMEM((ROWS, width), BF16),
            pltpu.VMEM((ROWS, width), F32),
            pltpu.VMEM((ROWS, 128), BF16),
            pltpu.SemaphoreType.DMA((4, 4)),
        ],
        **params(12),
    )(place, grad, qkv, probs, *weights[:2], *pieces)


def gelu_pair(u):
    size = jnp.abs(u) * (0.5**0.5)
    t = 1.0 / (1.0 + 0.3275911 * size)
    poly = t * (
        0.254829592
        + t * (-0.284496736 + t * (1.421413741 + t * (-1.453152027 + t * 1.061405429)))
    )
    bell = jnp.exp(-0.5 * u * u)
    tail = 0.5 * poly * bell
    phi = jnp.where(u >= 0.0, 1.0 - tail, tail)
    return u * phi, phi + u * bell * 0.3989422804014327


def mlp_forward_kernel(
    a_ref, pieces, h_ref, slope_ref, m_ref, w1, w2, bs, rows, total, sems
):
    copy = start_rows(a_ref, rows, sems)
    start_mlp_copies((pieces, MLP_SPAN), w1, w2, sems, bs)
    copy.wait()

    def chunk_step(chunk, carry):
        wait_chunk(chunk, (w1, w2), sems)
        wait_bias(chunk, bs, sems)
        bias = jnp.sum(bs[chunk].astype(F32), axis=0, keepdims=True)
        value, slope = gelu_pair(dot_nn(rows[...], w1[chunk]) + bias)
        h_ref[chunk] = value.astype(BF16)
        slope_ref[chunk] = slope.astype(BF16)
        add_part(chunk, total, dot_nn(h_ref[chunk], w2[chunk]))
        return carry

    lax.fori_loop(0, 4, chunk_step, 0, unroll=True)
    m_ref[...] = total[...].astype(BF16)


def run_mlp_forward(rows, pieces):
    width = rows.shape[1]
    return pl.pallas_call(
        mlp_forward_kernel,
        out_shape=(
            jax.ShapeDtypeStruct((4, ROWS, 512), BF16),
            jax.ShapeDtypeStruct((4, ROWS, 512), BF16),
            jax.ShapeDtypeStruct((ROWS, width), BF16),
        ),
        in_specs=[HB, HB],
        out_specs=(VM,) * 3,
        scratch_shapes=[
            pltpu.VMEM((4, width, 512), BF16),
            pltpu.VMEM((4, 512, width), BF16),
            pltpu.VMEM((4, 16, 512), BF16),
            pltpu.VMEM((ROWS, width), BF16),
            pltpu.VMEM((ROWS, width), F32),
            pltpu.SemaphoreType.DMA((4, 4)),
        ],
        **params(8),
    )(rows, pieces)


def mlp_backward_kernel(
    g_ref, slope_ref, pieces, du_ref, sums_ref, d_ref, w1, w2, rows, total, sems
):
    copy = start_rows(g_ref, rows, sems)
    start_mlp_copies((pieces, MLP_SPAN), w1, w2, sems)
    copy.wait()

    def chunk_step(chunk, carry):
        wait_chunk(chunk, (w1, w2), sems)
        grad = dot_nt(rows[...], w2[chunk]) * slope_ref[chunk].astype(F32)
        grad = grad.astype(BF16)
        du_ref[chunk] = grad
        sums_ref[chunk] = jnp.broadcast_to(
            jnp.sum(grad.astype(F32), axis=0, keepdims=True), (8, 512)
        )
        add_part(chunk, total, dot_nt(du_ref[chunk], w1[chunk]))
        return carry

    lax.fori_loop(0, 4, chunk_step, 0, unroll=True)
    d_ref[...] = total[...].astype(BF16)


def mlp_both_kernel(
    a_ref, g_ref, pieces, h_ref, m_ref, du_ref, sums_ref, d_ref,
    w1, w2, bs, rows, grads, total, back, sems,
):
    copy = start_rows(a_ref, rows, sems)
    other = pltpu.make_async_copy(g_ref, grads, sems.at[3, 1])
    other.start()
    start_mlp_copies((pieces, MLP_SPAN), w1, w2, sems, bs)
    copy.wait()
    other.wait()

    def chunk_step(chunk, carry):
        wait_chunk(chunk, (w1, w2), sems)
        wait_bias(chunk, bs, sems)
        bias = jnp.sum(bs[chunk].astype(F32), axis=0, keepdims=True)
        value, slope = gelu_pair(dot_nn(rows[...], w1[chunk]) + bias)
        h_ref[chunk] = value.astype(BF16)
        grad = (dot_nt(grads[...], w2[chunk]) * slope).astype(BF16)
        du_ref[chunk] = grad
        sums_ref[chunk] = jnp.broadcast_to(
            jnp.sum(grad.astype(F32), axis=0, keepdims=True), (8, 512)
        )
        add_part(chunk, total, dot_nn(h_ref[chunk], w2[chunk]))
        add_part(chunk, back, dot_nt(du_ref[chunk], w1[chunk]))
        return carry

    lax.fori_loop(0, 4, chunk_step, 0, unroll=True)
    m_ref[...] = total[...].astype(BF16)
    d_ref[...] = back[...].astype(BF16)


def run_mlp_both(rows, grad, pieces):
    width = rows.shape[1]
    return pl.pallas_call(
        mlp_both_kernel,
        out_shape=(
            jax.ShapeDtypeStruct((4, ROWS, 512), BF16),
            jax.ShapeDtypeStruct((ROWS, width), BF16),
            jax.ShapeDtypeStruct((4, ROWS, 512), BF16),
            jax.ShapeDtypeStruct((4, 8, 512), F32),
            jax.ShapeDtypeStruct((ROWS, width), BF16),
        ),
        in_specs=[HB, HB, HB],
        out_specs=(VM,) * 5,
        scratch_shapes=[
            pltpu.VMEM((4, width, 512), BF16),
            pltpu.VMEM((4, 512, width), BF16),
            pltpu.VMEM((4, 16, 512), BF16),
            pltpu.VMEM((ROWS, width), BF16),
            pltpu.VMEM((ROWS, width), BF16),
            pltpu.VMEM((ROWS, width), F32),
            pltpu.VMEM((ROWS, width), F32),
            pltpu.SemaphoreType.DMA((4, 4)),
        ],
        **params(15),
    )(rows, grad, pieces)


def run_mlp_backward(grad, slope, pieces):
    width = grad.shape[1]
    return pl.pallas_call(
        mlp_backward_kernel,
        out_shape=(
            jax.ShapeDtypeStruct((4, ROWS, 512), BF16),
            jax.ShapeDtypeStruct((4, 8, 512), F32),
            jax.ShapeDtypeStruct((ROWS, width), BF16),
        ),
        in_specs=[HB, VM, HB],
        out_specs=(VM,) * 3,
        scratch_shapes=[
            pltpu.VMEM((4, width, 512), BF16),
            pltpu.VMEM((4, 512, width), BF16),
            pltpu.VMEM((ROWS, width), BF16),
            pltpu.VMEM((ROWS, width), F32),
            pltpu.SemaphoreType.DMA((4, 4)),
        ],
        **params(7),
    )(grad, slope, pieces)


SEND, AWAY, NEAR, ALL = 0, 1, 2, 3
STAGE_SLOTS = (((0, 1), (1, 1)), ((1, 0),), ((0, 0),), ((0, 0), (0, 1), (1, 0), (1, 1)))


def weight_grad_kernel(
    stage, place, x1_own, x1_far, y1_own, y1_far, x2_own, x2_far, y2_own, y2_far, *refs
):
    slots = STAGE_SLOTS[stage]
    (xs, y1, y2, turned, added, sems), refs = refs[-6:], refs[:-6]
    out_ref = refs[-1]
    got = [refs[0].at[0 if stage == NEAR else 1], *refs[1:-1]] if stage in (AWAY, NEAR) else []
    whole = out_ref
    if stage == ALL:
        out_ref = added
    outs = [out_ref.at[slot] for slot in range(len(slots))] if len(slots) > 1 else [out_ref]
    copies = []
    for slot, (side, core) in enumerate(slots):
        if stage != ALL:
            side, core = place[SIDE] ^ side, place[CORE] ^ core
        start = aligned(4 * side + core, 128)
        for index, sources in enumerate(((x1_own, x1_far), (x2_own, x2_far))):
            for half, source in enumerate(sources):
                for run in range(2):
                    copies.append(
                        pltpu.make_async_copy(
                            source.at[:, pl.ds(start + 256 * run, 128)],
                            xs.at[index, slot, pl.ds(ROWS * half, ROWS), pl.ds(128 * run, 128)],
                            sems.at[4, 8 * slot + 4 * index + 2 * half + run],
                        )
                    )
    for copy in copies:
        copy.start()
    for chunk in range(4):
        for index, (source, target) in enumerate(
            ((y1_own, y1), (y1_far, y1), (y2_own, y2), (y2_far, y2))
        ):
            pltpu.make_async_copy(
                source.at[chunk],
                target.at[chunk, pl.ds(ROWS * (index % 2), ROWS)],
                sems.at[chunk, index],
            ).start()
        for index, source in enumerate(got):
            pltpu.make_async_copy(
                source.at[chunk], added.at[index, chunk], sems.at[chunk, 4 + index]
            ).start()
    for copy in copies:
        copy.wait()
    for slot in range(len(slots)):
        for index in range(2):
            turned[index, slot] = xs[index, slot].T
    span1 = y1.shape[2]

    def chunk_step(chunk, carry):
        for index, target in enumerate((y1, y1, y2, y2)):
            half = target.at[chunk, pl.ds(ROWS * (index % 2), ROWS)]
            pltpu.make_async_copy(half, half, sems.at[chunk, index]).wait()
        for index in range(len(got)):
            array = added.at[index, chunk]
            pltpu.make_async_copy(array, array, sems.at[chunk, 4 + index]).wait()
        for slot, out in enumerate(outs):
            first = dot_nn(turned[0, slot], y1[chunk])
            second = dot_nn(turned[1, slot], y2[chunk])
            for index in range(len(got)):
                first += added[index, chunk, :, 0:span1].astype(F32)
                second += added[index, chunk, :, span1:].astype(F32)
            out[chunk, :, 0:span1] = first.astype(BF16)
            out[chunk, :, span1:] = second.astype(BF16)
            if stage == ALL:
                pltpu.make_async_copy(
                    out.at[chunk], whole.at[slot, chunk], sems.at[chunk, 8 + slot]
                ).start()
        return carry

    lax.fori_loop(0, 4, chunk_step, 0, unroll=True)
    if stage == ALL:
        for chunk in range(4):
            for slot, out in enumerate(outs):
                pltpu.make_async_copy(
                    out.at[chunk], whole.at[slot, chunk], sems.at[chunk, 8 + slot]
                ).wait()


def run_weight_grad(stage, place, x1, y1, x2, y2, *got):
    rows, width = 2 * ROWS, x1[0].shape[1]
    span1, span2 = y1[0].shape[2], y2[0].shape[2]
    part = width // 4
    shape = (4, part, span1 + span2)
    slots = len(STAGE_SLOTS[stage])
    return pl.pallas_call(
        functools.partial(weight_grad_kernel, stage),
        out_shape=jax.ShapeDtypeStruct((slots, *shape) if slots > 1 else shape, BF16),
        in_specs=[SM] + [HB] * (8 + len(got)),
        out_specs=HB if stage == ALL else VM,
        scratch_shapes=[
            pltpu.VMEM((2, slots, rows, part), BF16),
            pltpu.VMEM((4, rows, span1), BF16),
            pltpu.VMEM((4, rows, span2), BF16),
            pltpu.VMEM((2, slots, part, rows), BF16),
            pltpu.VMEM((4 if stage == ALL else max(len(got), 1), *shape), BF16),
            pltpu.SemaphoreType.DMA((5, 32)),
        ],
        **params((4 if span1 > 384 else 3) * slots + 2),
    )(place, *x1, *y1, *x2, *y2, *got)


def add_depth_kernel(place, *refs):
    parts, (stay, move) = refs[:-2], refs[-2:]
    total = parts[0][...].astype(F32)
    for part in parts[1:]:
        total += part[...].astype(F32)
    half = total.shape[0] // 2
    low, high = total[:half], total[half:]
    even = place[PAIR] == 0
    stay[...] = jnp.where(even, low, high).astype(BF16)
    move[...] = jnp.where(even, high, low).astype(BF16)


def run_add_depth(place, parts):
    rows, span = parts[0].shape
    shape = jax.ShapeDtypeStruct((rows // 2, span), BF16)
    return pl.pallas_call(
        add_depth_kernel,
        out_shape=(shape, shape),
        in_specs=[SM] + [VM] * len(parts),
        out_specs=(VM, VM),
        **params(2),
    )(place, *parts)


def collect_kernel(place, fc2_last, *refs):
    out = refs[-1]
    layers = (len(refs) - 1) // 6
    narrow, wide = aligned(place[PAIR], 128), aligned(place[PAIR], 512)
    out[...] = jnp.zeros(out.shape, F32)
    for layer in range(layers):
        sums1, sums2, qv_own, qv_far, fc1_own, fc1_far = refs[6 * layer : 6 * layer + 6]
        row = 12 * layer
        out[row : row + 2, :] = sums1[0:2, :]
        out[row + 2 : row + 3, :] = sums2[2:3, :]
        out[row + 3 : row + 5, :] = sums2[0:2, :]
        above = refs[6 * layer + 6][2:3, :] if layer + 1 < layers else fc2_last[0:1, :]
        out[row + 5 : row + 6, :] = above
        for depth in range(4):
            qv = qv_own[depth, 0:1, :] + qv_far[depth, 0:1, :]
            for item in range(2):
                out[row + 6 + item, pl.ds(depth * 256 + narrow, 128)] = qv[
                    0, 256 * item : 256 * item + 128
                ]
            fc1 = fc1_own[depth, 0:1, :] + fc1_far[depth, 0:1, :]
            out[pl.ds(row + 8 + depth, 1), pl.ds(wide, 512)] = fc1


def run_collect(place, fc2_last, parts):
    layers = len(parts) // 6
    return pl.pallas_call(
        collect_kernel,
        out_shape=jax.ShapeDtypeStruct((12 * layers, 1024), F32),
        in_specs=[SM] + [VM] * (1 + len(parts)),
        out_specs=VM,
        **params(2),
    )(place, fc2_last, *parts)


def release_kernel(place, total, *outs):
    rows, (qv, fc1) = outs[:6], outs[6:]
    quarter = aligned(place[DEPTH], 256)
    for layer in range(fc1.shape[0]):
        for index, out in enumerate(rows):
            out[layer : layer + 1, :] = total[pl.ds(12 * layer + index, 1), :]
        for item in range(2):
            qv[layer, item : item + 1, :] = total[
                pl.ds(12 * layer + 6 + item, 1), pl.ds(quarter, 256)
            ]
        fc1[layer : layer + 1, :] = total[pl.ds(12 * layer + 8 + place[DEPTH], 1), :]


def run_release(place, total):
    layers = total.shape[0] // 12
    row = jax.ShapeDtypeStruct((layers, 1024), F32)
    return pl.pallas_call(
        release_kernel,
        out_shape=(row,) * 6 + (jax.ShapeDtypeStruct((layers, 2, 256), F32), row),
        in_specs=[SM, VM],
        out_specs=(VM,) * 8,
        **params(2),
    )(place, total)


def finish_kernel(place, *refs):
    layers = (len(refs) - 4) // 4
    ins, (qkv, proj, fc1, fc2) = refs[: 4 * layers], refs[4 * layers :]
    for layer in range(layers):
        for side in range(2):
            attn, mlp = ins[4 * layer + side], ins[4 * layer + 2 + side]
            pair = place[PAIR] if side == 0 else 1 - place[PAIR]
            narrow, wide = aligned(pair, 128), aligned(pair, 512)
            for item in range(3):
                qkv[layer, item, :, pl.ds(narrow, 128)] = attn[
                    :, item * 128 : item * 128 + 128
                ].astype(F32)
            proj[layer, pl.ds(narrow, 128), :] = attn[:, 384:512].astype(F32).T
            fc1[layer, :, pl.ds(wide, 512)] = mlp[:, 0:512].astype(F32)
            fc2[layer, pl.ds(wide, 512), :] = mlp[:, 512:1024].astype(F32).T


def run_finish(place, parts):
    rows = parts[0].shape[0]
    return pl.pallas_call(
        finish_kernel,
        out_shape=(
            jax.ShapeDtypeStruct((2, 3, rows, 256), F32),
            jax.ShapeDtypeStruct((2, 256, rows), F32),
            jax.ShapeDtypeStruct((2, rows, 1024), F32),
            jax.ShapeDtypeStruct((2, 1024, rows), F32),
        ),
        in_specs=[SM] + [VM] * len(parts),
        out_specs=(VM,) * 4,
        **params(4),
    )(place, *parts)


def on_device(*args):
    (
        images_in, out_cotangent, norm1_gain, norm1_bias, qkv_weight, qv_bias, proj_weight,
        proj_bias, norm2_gain, norm2_bias, fc1_weight, fc1_bias, fc2_weight, fc2_bias,
    ) = args
    images, seq, _ = images_in.shape
    layers = qkv_weight.shape[0]
    n_far, n_mp = lax.axis_size("far"), lax.axis_size("mp")
    mine = images // n_mp

    side, pair, core = lax.axis_index("y"), lax.axis_index("x"), lax.axis_index("core")
    depth = lax.axis_index("mp")
    here = jnp.stack(
        [
            side, core, pair, depth,
            side * 2 + core, (1 - side) * 2 + core, side * 2 + 1 - core, (1 - side) * 2 + 1 - core,
        ]
    ).astype(jnp.int32)

    def swap(value, axis):
        return lax.ppermute(value, axis, [(0, 1), (1, 0)])

    def shift(value, step):
        return lax.ppermute(
            value, "mp", [(index, (index + step) % n_mp) for index in range(n_mp)]
        )

    def after(value, *others):
        return lax.optimization_barrier((value, *others))[0]

    wqkv = qkv_weight.transpose(0, 2, 1, 3)
    attn_weights = (wqkv, proj_weight, qv_bias)
    packed = run_pack(here, wqkv, proj_weight, fc1_weight, fc2_weight, qv_bias, fc1_bias)
    attn_pieces, mlp_pieces = [[]], []
    moved = []
    for step in (1, 3, 2):
        same = shift(packed[0], step)
        moved.append(same)
        other = swap(same, "y")
        attn_pieces[0].append((step, [same, other, swap(same, "core"), swap(other, "core")]))
    attn_pieces[0] = [array for _, arrays in sorted(attn_pieces[0]) for array in arrays]
    stream, normed = run_enter(here, images_in, mine, norm1_gain[0], norm1_bias[0])
    grad, grad_b, fc2_sum = run_enter_back(here, out_cotangent, mine)
    grad_b_far = swap(grad_b, "x")
    gathered = []
    for index in (1, 2):
        gathered = lax.all_gather((after(packed[index], *gathered) if gathered else packed[index]), ("y", "core", "mp"))
        value = gathered.reshape(2, 2, n_mp, *gathered.shape[1:])
        mlp_pieces.append(value)
        attn_pieces.append([value])
        gathered = [gathered]

    def both(run, own, far, *waits):
        results = run(own)
        return list(zip(results, run(after(far, *waits) if waits else far)))

    saved = []
    for layer in range(layers):
        normed_far = swap(normed, "x")
        qkv, probs, mixed, part = both(
            lambda rows: run_attention_forward(layer, here, rows, attn_weights, attn_pieces[layer]),
            normed, normed_far,
        )
        middle, normed2 = run_residual_norm(
            stream, part[0], swap(part[1], "x"), proj_bias[layer], norm2_gain[layer],
            norm2_bias[layer],
        )
        normed2_far = swap(normed2, "x")
        if layer + 1 < layers:
            active, slope, part = both(
                lambda rows: run_mlp_forward(rows, mlp_pieces[layer]),
                after(normed2, grad_b_far), normed2_far,
            )
        else:
            cotangents, slope = [grad_b, grad_b_far], None
            active, part, *last_back = both(
                lambda rows: run_mlp_both(rows, cotangents.pop(0), mlp_pieces[layer]),
                normed2, normed2_far,
            )
        saved.append(
            (stream, (normed, normed_far), list(zip(qkv, probs)), mixed, middle, (normed2, normed2_far), active, slope)
        )
        if layer + 1 < layers:
            stream, normed = run_residual_norm(
                middle, part[0], swap(part[1], "x"), fc2_bias[layer], norm1_gain[layer + 1],
                norm1_bias[layer + 1],
            )
        else:
            last = (middle, *part, fc2_bias[layer])

    class Sum:
        def __init__(self, *arrays):
            self.arrays = arrays
            self.core = swap(run_weight_grad(SEND, here, *arrays), "core")

        def away(self):
            kept = run_weight_grad(AWAY, here, *self.arrays, self.core)
            self.side = swap(kept, "y")
            return kept

        def near(self, *waits):
            side = after(self.side, *waits) if waits else self.side
            kept = run_weight_grad(NEAR, here, *self.arrays, self.core, side)
            flat = kept.reshape(-1, kept.shape[-1])
            self.total = lax.psum_scatter(flat, "mp", tiled=True)
            return kept

        def result(self):
            return run_add_depth(here, [self.total])

    class SumAtOnce(Sum):
        def __init__(self, *arrays):
            grads = run_weight_grad(ALL, here, *arrays)
            flat = grads.reshape(-1, grads.shape[-1])
            self.total = lax.psum_scatter(flat, ("y", "core", "mp"), tiled=True)

    attn, mlp, groups = None, None, []
    small = [None] * layers
    for layer in reversed(range(layers)):
        stream, normed, qkv, mixed, middle, normed2, active, slope = saved[layer]
        qkvs = list(qkv)
        if attn is None:
            du, fc1_sum, part = last_back
        else:
            slopes = list(slope)
            du, fc1_sum, part = both(
                lambda rows: run_mlp_backward(rows, slopes.pop(0), mlp_pieces[layer]),
                grad_b, grad_b_far, attn.away(),
            )
        mlp = (SumAtOnce if layer else Sum)(normed2, du, (grad_b, grad_b_far), active)
        grad, grad_b, sums2 = run_norm_back(
            grad, part[0], swap(part[1], "x"), middle, norm2_gain[layer]
        )
        grad_b_far = swap(grad_b, "x")
        dqkv, qv_sum, part = both(
            lambda rows: run_attention_backward(
                layer, here, rows, *qkvs.pop(0), attn_weights, attn_pieces[layer]
            ),
            grad_b, grad_b_far, *([] if layer else [mlp.away()]),
        )
        if layer:
            stream_in, near, away, bias = last
            last = run_residual(stream_in, near, swap(after(away, dqkv[0]), "x"), bias)
            last = after(last, mlp.total)
        above, attn = attn, Sum(normed, dqkv, (grad_b, grad_b_far), mixed)
        if above:
            grad = after(grad, above.near())
        grad, grad_b, sums1 = run_norm_back(
            grad, part[0], swap(part[1], "x"), stream, norm1_gain[layer]
        )
        if layer:
            grad_b_far = swap(grad_b, "x")
        small[layer] = [sums1, sums2, *qv_sum, *fc1_sum]
        groups = [attn, mlp, *groups]

    block_out = run_leave(here, [lax.all_gather(last, "mp")], seq, mine, BF16)
    parts = [shift(grad_b, step) for step in (1, 3, 2)]
    attn.core = after(attn.core, grad_b)
    attn.away()
    kept = mlp.near()
    kept = attn.near(kept, block_out, *parts)
    parts = [after(part, kept) for part in parts]
    input_grad = run_leave(here, [grad_b, *parts], seq, mine, F32)
    total = run_collect(here, fc2_sum, [part for group in small for part in group])
    total = after(total, kept)
    for axis in ("core", "x", "y"):
        total = total + swap(total, axis)
    for bit in range(n_far.bit_length() - 1):
        pairs = [(index, index ^ (1 << bit)) for index in range(n_far)]
        total = total + lax.ppermute(total, "far", pairs)
    total = after(total, *parts)
    for bit in range(n_mp.bit_length() - 1):
        pairs = [(index, index ^ (1 << bit)) for index in range(n_mp)]
        total = total + lax.ppermute(total, "mp", pairs)
    n1g, n1b, pb, n2g, n2b, f2b, qv, fc1 = run_release(here, total)

    ready = [group.result() for group in groups]
    if n_far == 1:
        parts = [part for stay, move in ready for part in (stay, swap(move, "x"))]
    else:
        parts = [part for stay, move in ready for part in spread_rows(stay, move)]
    g_qkv, g_proj, g_fc1, g_fc2 = run_finish(here, parts)
    block_out, input_grad = (
        value.reshape(seq, images, -1).transpose(1, 0, 2) for value in (block_out, input_grad)
    )
    return (
        block_out, input_grad, n1g, n1b, g_qkv.transpose(0, 2, 1, 3), qv, g_proj, pb, n2g, n2b,
        g_fc1, fc1, g_fc2, f2b,
    )


def spread_rows(stay, move):
    pair = lax.axis_index("x")
    value = jnp.stack(
        [jnp.where(pair == 0, stay, move), jnp.where(pair == 0, move, stay)]
    ).astype(F32)
    value = lax.psum(value, "far")
    value = lax.all_gather(value, ("y", "x", "core"))
    rows, span = value.shape[2:]
    value = value.reshape(2, 2, 2, 2, rows, span).transpose(0, 3, 2, 4, 1, 5)
    value = value.reshape(8 * rows, 2, span)
    count = rows // lax.axis_size("far")
    place = lax.axis_index(("far", "y", "x", "core"))
    value = lax.dynamic_slice_in_dim(value, place * count, count, 0)
    mine = lax.dynamic_index_in_dim(value, pair, 1, keepdims=False)
    other = lax.dynamic_index_in_dim(value, 1 - pair, 1, keepdims=False)
    return mine, other


def solution(mesh):
    n_dp, n_mp = mesh.shape["dp"], mesh.shape["mp"]
    fine = Mesh(mesh.devices.reshape(n_dp // 8, 2, 2, 2, n_mp), ("far", "y", "x", "core", "mp"))
    dp = ("far", "y", "x", "core")
    return jax.shard_map(
        on_device,
        mesh=fine,
        in_specs=(
            P(dp, None, None),
            P(dp, None, None),
            P(),
            P(),
            P(None, None, None, "mp"),
            P(None, None, "mp"),
            P(None, "mp", None),
            P(),
            P(),
            P(),
            P(None, None, "mp"),
            P(None, "mp"),
            P(None, "mp", None),
            P(),
        ),
        out_specs=(
            P(dp, None, None),
            P(dp, None, None),
            P(),
            P(),
            P(None, dp, None, "mp"),
            P(None, None, "mp"),
            P(None, "mp", dp),
            P(),
            P(),
            P(),
            P(None, dp, "mp"),
            P(None, "mp"),
            P(None, "mp", dp),
            P(),
        ),
        check_vma=False,
    )
```

```python
import functools

import jax
import jax.numpy as jnp
from jax import lax
from jax.experimental import pallas as pl
from jax.experimental.pallas import tpu as pltpu
from jax.sharding import Mesh
from jax.sharding import PartitionSpec as P

HEAD_DIM = 64
EPS = 1e-06
F32 = jnp.float32
BF16 = jnp.bfloat16
ROWS = 304
WIN = 112
WIN_STEP = 96
BIG_NEG = -1e30
VMEM_LIMIT = 60 * 1024 * 1024


def dot_nn(a, b):
    return lax.dot_general(a, b, (((1,), (0,)), ((), ())), preferred_element_type=F32)


def dot_nt(a, b):
    return lax.dot_general(a, b, (((1,), (1,)), ((), ())), preferred_element_type=F32)


def dot_tn(a, b):
    return lax.dot_general(a, b, (((0,), (0,)), ((), ())), preferred_element_type=F32)


COST = 4e9


def params(micros):
    return dict(
        compiler_params=pltpu.CompilerParams(vmem_limit_bytes=VMEM_LIMIT),
        cost_estimate=pl.CostEstimate(
            flops=int(micros * COST), bytes_accessed=0, transcendentals=0
        ),
    )


VM = pl.BlockSpec(memory_space=pltpu.VMEM)
SM = pl.BlockSpec(memory_space=pltpu.SMEM)
HB = pl.BlockSpec(memory_space=pl.ANY)


def layer_norm(x, gain, bias):
    mean = jnp.mean(x, axis=-1, keepdims=True)
    centered = x - mean
    variance = jnp.mean(centered * centered, axis=-1, keepdims=True)
    return centered * lax.rsqrt(variance + EPS) * gain + bias


def own_selector(place, seq, mine):
    images = 4 * mine
    row = lax.broadcasted_iota(jnp.int32, (ROWS, images * seq), 0)
    col = lax.broadcasted_iota(jnp.int32, (ROWS, images * seq), 1)
    token = col // images
    image = col - token * images - place[DEPTH] * mine
    hit = (image >= 0) & (image < mine) & (row == image * seq + token)
    return jnp.where(hit, 1.0, 0.0).astype(BF16)


def enter_kernel(seq, mine, place, x_ref, gain_ref, beta_ref, x1_ref, a_ref):
    x = dot_nn(own_selector(place, seq, mine), x_ref[...])
    x1_ref[...] = x
    a_ref[...] = layer_norm(x, gain_ref[...], beta_ref[...]).astype(BF16)


def enter_back_kernel(seq, mine, place, x_ref, g_ref, gb_ref, sum_ref):
    g = dot_nn(own_selector(place, seq, mine), x_ref[...])
    g_ref[...] = g
    gb_ref[...] = g.astype(BF16)
    sum_ref[...] = jnp.broadcast_to(jnp.sum(g, axis=0, keepdims=True), sum_ref.shape)


def leave_kernel(seq, mine, place, *refs):
    parts, out_ref = refs[:-1], refs[-1]
    images = 4 * mine
    count = images * seq
    row = lax.broadcasted_iota(jnp.int32, (count, ROWS), 0)
    col = lax.broadcasted_iota(jnp.int32, (count, ROWS), 1)
    token = row // images
    want = row - token * images
    total = None
    for index, step in enumerate((0, 1, 3, 2)):
        depth, rows = index, parts[0].at[index] if len(parts) == 1 else parts[index]
        if len(parts) > 1:
            depth = (place[DEPTH] - step) & 3
        image = want - depth * mine
        hit = (image >= 0) & (image < mine) & (col == image * seq + token)
        part = dot_nn(jnp.where(hit, 1.0, 0.0).astype(BF16), rows[...])
        total = part if total is None else total + part
    out_ref[...] = total.astype(out_ref.dtype)


def residual_norm_kernel(
    x_ref, own_ref, far_ref, bias_ref, gain_ref, beta_ref, x1_ref, a_ref, far, sem
):
    copy = pltpu.make_async_copy(far_ref, far, sem)
    copy.start()
    keep = lax.broadcasted_iota(jnp.int32, (ROWS, 1), 0) < 300
    bias = jnp.where(keep, bias_ref[...], 0.0)
    copy.wait()
    x1 = x_ref[...] + own_ref[...].astype(F32) + far[...].astype(F32) + bias
    x1_ref[...] = x1
    a_ref[...] = layer_norm(x1, gain_ref[...], beta_ref[...]).astype(BF16)


def residual_kernel(x_ref, own_ref, far_ref, bias_ref, x1_ref, far, sem):
    copy = pltpu.make_async_copy(far_ref, far, sem)
    copy.start()
    copy.wait()
    x1 = x_ref[...] + own_ref[...].astype(F32) + far[...].astype(F32) + bias_ref[...]
    x1_ref[...] = x1.astype(BF16)


def norm_back_kernel(
    g_ref, own_ref, far_ref, x_ref, gain_ref, g1_ref, g1b_ref, sums_ref, far, sem
):
    copy = pltpu.make_async_copy(far_ref, far, sem)
    copy.start()
    x = x_ref[...]
    mean = jnp.mean(x, axis=-1, keepdims=True)
    centered = x - mean
    variance = jnp.mean(centered * centered, axis=-1, keepdims=True)
    inverse = lax.rsqrt(variance + EPS)
    xhat = centered * inverse
    copy.wait()
    da = own_ref[...].astype(F32) + far[...].astype(F32)
    inner = da * gain_ref[...]
    mean_inner = jnp.mean(inner, axis=-1, keepdims=True)
    mean_proj = jnp.mean(inner * xhat, axis=-1, keepdims=True)
    g1 = g_ref[...] + inverse * (inner - mean_inner - xhat * mean_proj)
    g1_ref[...] = g1
    g1b_ref[...] = g1.astype(BF16)
    sums_ref[...] = jnp.zeros(sums_ref.shape, F32)
    sums_ref[0:1, :] = jnp.sum(da * xhat, axis=0, keepdims=True)
    sums_ref[1:2, :] = jnp.sum(da, axis=0, keepdims=True)
    sums_ref[2:3, :] = jnp.sum(g1, axis=0, keepdims=True)


def run_enter(place, images, mine, gain, beta):
    count, seq, width = images.shape
    flat = images.transpose(1, 0, 2).reshape(count * seq, width)
    return pl.pallas_call(
        functools.partial(enter_kernel, seq, mine),
        out_shape=(
            jax.ShapeDtypeStruct((ROWS, width), F32),
            jax.ShapeDtypeStruct((ROWS, width), BF16),
        ),
        in_specs=[SM, VM, VM, VM],
        out_specs=(VM, VM),
        **params(5),
    )(place, flat, gain[None], beta[None])


def run_enter_back(place, images, mine):
    count, seq, width = images.shape
    flat = images.transpose(1, 0, 2).reshape(count * seq, width)
    return pl.pallas_call(
        functools.partial(enter_back_kernel, seq, mine),
        out_shape=(
            jax.ShapeDtypeStruct((ROWS, width), F32),
            jax.ShapeDtypeStruct((ROWS, width), BF16),
            jax.ShapeDtypeStruct((8, width), F32),
        ),
        in_specs=[SM, VM],
        out_specs=(VM, VM, VM),
        **params(5),
    )(place, flat)


def run_leave(place, parts, seq, mine, dtype):
    images, width = 4 * mine, parts[0].shape[-1]
    flat = pl.pallas_call(
        functools.partial(leave_kernel, seq, mine),
        out_shape=jax.ShapeDtypeStruct((images * seq, width), dtype),
        in_specs=[SM] + [VM] * len(parts),
        out_specs=VM,
        **params(9),
    )(place, *parts)
    return flat


def run_residual_norm(x, own, far, bias, gain, beta):
    return pl.pallas_call(
        residual_norm_kernel,
        out_shape=(
            jax.ShapeDtypeStruct(x.shape, F32),
            jax.ShapeDtypeStruct(x.shape, BF16),
        ),
        in_specs=[VM, VM, HB, VM, VM, VM],
        out_specs=(VM, VM),
        scratch_shapes=[pltpu.VMEM((ROWS, x.shape[1]), BF16), pltpu.SemaphoreType.DMA],
        **params(3),
    )(x, own, far, bias[None], gain[None], beta[None])


def run_residual(x, own, far, bias):
    return pl.pallas_call(
        residual_kernel,
        out_shape=jax.ShapeDtypeStruct(x.shape, BF16),
        in_specs=[VM, VM, HB, VM],
        out_specs=VM,
        scratch_shapes=[pltpu.VMEM((ROWS, x.shape[1]), BF16), pltpu.SemaphoreType.DMA],
        **params(2),
    )(x, own, far, bias[None])


def run_norm_back(g, own, far, x, gain):
    return pl.pallas_call(
        norm_back_kernel,
        out_shape=(
            jax.ShapeDtypeStruct(x.shape, F32),
            jax.ShapeDtypeStruct(x.shape, BF16),
            jax.ShapeDtypeStruct((8, x.shape[1]), F32),
        ),
        in_specs=[VM, VM, HB, VM, VM],
        out_specs=(VM, VM, VM),
        scratch_shapes=[pltpu.VMEM((ROWS, x.shape[1]), BF16), pltpu.SemaphoreType.DMA],
        **params(4),
    )(g, own, far, x, gain[None])


SIDE, CORE, PAIR, DEPTH, PARTS = 0, 1, 2, 3, 4

ATTN_ROWS, MLP_ROWS = 272, 528
ATTN_SPAN, MLP_SPAN = pl.ds(MLP_ROWS, ATTN_ROWS), pl.ds(0, MLP_ROWS)


def exact_rows(bias):
    high = bias.astype(BF16)
    rest = bias - high.astype(F32)
    mid = rest.astype(BF16)
    low = (rest - mid.astype(F32)).astype(BF16)
    return jnp.concatenate([high, mid, low, jnp.zeros((13, bias.shape[1]), BF16)], axis=0)


def pack_kernel(
    place, wqkv, wproj, w1, w2, bqv, b1, attn0, middle, mlp1, sems
):
    row = aligned(place[PARTS], 256)
    narrow, wide = aligned(place[PAIR], 128), aligned(place[PAIR], 512)
    copies = []
    mlp0, attn1 = middle.at[0:MLP_ROWS], middle.at[MLP_ROWS:]
    for layer, (attn, mlp) in enumerate(((attn0, mlp0), (attn1, mlp1))):
        for item in range(3):
            copies.append(
                (
                    wqkv.at[layer, item, pl.ds(row, 256), pl.ds(narrow, 128)],
                    attn.at[0:256, pl.ds(item * 128, 128)],
                )
            )
        for half in range(2):
            copies.append(
                (
                    wproj.at[layer, pl.ds(narrow, 128), pl.ds(row + half * 128, 128)],
                    attn.at[pl.ds(half * 128, 128), 384:512],
                )
            )
            copies.append(
                (
                    w2.at[layer, pl.ds(wide + half * 256, 256), pl.ds(row, 256)],
                    mlp.at[256:512, pl.ds(half * 256, 256)],
                )
            )
        copies.append(
            (w1.at[layer, pl.ds(row, 256), pl.ds(wide, 512)], mlp.at[0:256, :])
        )
    copies = [
        pltpu.make_async_copy(src, dst, sems.at[index])
        for index, (src, dst) in enumerate(copies)
    ]
    for copy in copies:
        copy.start()
    for layer, (attn, mlp) in enumerate(((attn0, mlp0), (attn1, mlp1))):
        zero = jnp.zeros((1, 128), F32)
        bias = [bqv[layer, pl.ds(item, 1), pl.ds(narrow, 128)] for item in range(2)]
        attn[256:272, :] = exact_rows(jnp.concatenate([bias[0], zero, bias[1], zero], axis=1))
        mlp[512:528, :] = exact_rows(b1[pl.ds(layer, 1), pl.ds(wide, 512)])
    for copy in copies:
        copy.wait()


def run_pack(place, wqkv, wproj, w1, w2, bqv, b1):
    return pl.pallas_call(
        pack_kernel,
        out_shape=tuple(
            jax.ShapeDtypeStruct((rows, 512), BF16)
            for rows in (ATTN_ROWS, MLP_ROWS + ATTN_ROWS, MLP_ROWS)
        ),
        in_specs=[SM, HB, HB, HB, HB, VM, VM],
        out_specs=(VM, VM, VM),
        scratch_shapes=[pltpu.SemaphoreType.DMA((16,))],
        **params(3),
    )(place, wqkv, wproj, w1, w2, bqv, b1)


def piece_sources(place, pieces, own):
    if not own:
        array, rows = pieces
        return [
            (depth, 2 * side + core, array.at[side, core, depth, rows])
            for depth in range(4)
            for side in range(2)
            for core in range(2)
        ]
    return [
        ((place[DEPTH] - step) & 3, place[PARTS + slot], pieces[4 * step - 4 + slot])
        for step in range(1, 4)
        for slot in range(4)
    ]


def aligned(index, step):
    if isinstance(index, int):
        return index * step
    return pl.multiple_of(index * step, step)


def start_attention_copies(layer, place, wqkv, wproj, bqv, pieces, wq, wp, sems, bs=None):
    own = len(pieces) > 2
    for index, (depth, part, src) in enumerate(piece_sources(place, pieces, own)):
        row = aligned(part, 256)
        pltpu.make_async_copy(
            src.at[0:256, 0:384], wq.at[depth, pl.ds(row, 256), :], sems.at[0, depth]
        ).start()
        for side in range(2):
            pltpu.make_async_copy(
                src.at[pl.ds(side * 128, 128), 384:512],
                wp.at[depth, :, pl.ds(row + side * 128, 128)],
                sems.at[1, depth],
            ).start()
        if bs is not None and index % 4 == 0:
            pltpu.make_async_copy(src.at[256:272, 0:384], bs.at[depth], sems.at[2, depth]).start()
    if own:
        depth, narrow = place[DEPTH], aligned(place[PAIR], 128)
        for item in range(3):
            pltpu.make_async_copy(
                wqkv.at[layer, item, :, pl.ds(narrow, 128)],
                wq.at[depth, :, pl.ds(item * 128, 128)],
                sems.at[0, depth],
            ).start()
        pltpu.make_async_copy(
            wproj.at[layer, pl.ds(narrow, 128), :], wp.at[depth], sems.at[1, depth]
        ).start()
        if bs is not None:
            bias = [bqv[layer, pl.ds(item, 1), pl.ds(narrow, 128)] for item in range(2)]
            zero = jnp.zeros((1, 128), F32)
            bs[depth] = exact_rows(jnp.concatenate([bias[0], zero, bias[1]], axis=1))


def start_mlp_copies(pieces, w1, w2, sems, bs=None):
    for index, (depth, part, src) in enumerate(piece_sources(None, pieces, False)):
        row = part * 256
        pltpu.make_async_copy(
            src.at[0:256, :], w1.at[depth, pl.ds(row, 256), :], sems.at[0, depth]
        ).start()
        for side in range(2):
            pltpu.make_async_copy(
                src.at[256:512, pl.ds(side * 256, 256)],
                w2.at[depth, pl.ds(side * 256, 256), pl.ds(row, 256)],
                sems.at[1, depth],
            ).start()
        if bs is not None and index % 4 == 0:
            pltpu.make_async_copy(src.at[512:528, :], bs.at[depth], sems.at[2, depth]).start()


def start_rows(source, rows, sems):
    copy = pltpu.make_async_copy(source, rows, sems.at[3, 0])
    copy.start()
    return copy


def wait_chunk(chunk, bufs, sems):
    for slot, buf in enumerate(bufs):
        pltpu.make_async_copy(buf.at[chunk], buf.at[chunk], sems.at[slot, chunk]).wait()


def wait_bias(chunk, bs, sems, own=None):
    def wait():
        pltpu.make_async_copy(bs.at[chunk], bs.at[chunk], sems.at[2, chunk]).wait()

    if own is None:
        wait()
    else:
        pl.when(chunk != own)(wait)


def window_masks(window):
    shape = (2 * WIN, WIN)
    row = lax.broadcasted_iota(jnp.int32, shape, 0)
    row = jnp.where(row >= WIN, row - WIN, row) - 4 * window
    col = lax.broadcasted_iota(jnp.int32, shape, 1) - 4 * window
    row_ok = (row >= 0) & (row < 100)
    col_ok = (col >= 0) & (col < 100)
    same = row_ok & col_ok & ((row >= 50) == (col >= 50))
    return jnp.where(same, 0.0, BIG_NEG).astype(F32)


def window_rows_ok(window):
    row = lax.broadcasted_iota(jnp.int32, (2 * WIN, 1), 0)
    row = jnp.where(row >= WIN, row - WIN, row) - 4 * window
    return (row >= 0) & (row < 100)


def stack_heads(values, first):
    zero = jnp.zeros_like(values)
    return jnp.concatenate(
        [jnp.where(first, values, zero), jnp.where(first, zero, values)], axis=0
    )


def first_head_lanes():
    return lax.broadcasted_iota(jnp.int32, (WIN, 2 * HEAD_DIM), 1) < HEAD_DIM


def window_probs(query, key, mask, rows_ok):
    scores = dot_nt(query, key) * (HEAD_DIM**-0.5) + mask
    top = jnp.max(scores, axis=-1, keepdims=True)
    expo = jnp.exp(scores - top)
    total = jnp.sum(expo, axis=-1, keepdims=True)
    return expo * jnp.where(rows_ok, 1.0 / total, 0.0)


def join_windows(parts):
    first, second, third = parts
    over = WIN - WIN_STEP
    return jnp.concatenate(
        [
            first[:WIN_STEP],
            first[WIN_STEP:] + second[:over],
            second[over:WIN_STEP],
            second[WIN_STEP:] + third[:over],
            third[over:],
        ],
        axis=0,
    )


def attention_forward_kernel(layer, count, place, a_ref, wqkv, wproj, bqv, *refs):
    pieces = refs[:count] if count > 1 else (refs[0], ATTN_SPAN)
    qkv_ref, probs_ref, o_ref, r_ref, wq, wp, bs, rows, total, masks, sems = refs[count:]
    own_quarter = place[DEPTH] if count > 1 else None
    copy = start_rows(a_ref, rows, sems)
    start_attention_copies(layer, place, wqkv, wproj, bqv, pieces, wq, wp, sems, bs)
    for window in range(3):
        masks[window] = window_masks(window)
    copy.wait()

    def chunk_step(chunk, carry):
        wait_chunk(chunk, (wq, wp), sems)
        wait_bias(chunk, bs, sems, own_quarter)
        bias = jnp.sum(bs[chunk].astype(F32), axis=0, keepdims=True)
        qkv_ref[chunk] = (dot_nn(rows[...], wq[chunk]) + bias).astype(BF16)
        first = first_head_lanes()
        outs = []
        for window in range(3):
            span = pl.ds(window * WIN_STEP, WIN)
            query = stack_heads(qkv_ref[chunk, span, 0:128], first)
            probs = window_probs(
                query, qkv_ref[chunk, span, 128:256], masks[window], window_rows_ok(window)
            )
            probs_ref[chunk, window] = probs.astype(BF16)
            mixed = dot_nn(probs.astype(BF16), qkv_ref[chunk, span, 256:384])
            outs.append(jnp.where(first, mixed[:WIN], mixed[WIN:]))
        o_ref[chunk] = join_windows(outs).astype(BF16)
        add_part(chunk, total, dot_nn(o_ref[chunk], wp[chunk]))
        return carry

    lax.fori_loop(0, 4, chunk_step, 0, unroll=True)
    r_ref[...] = total[...].astype(BF16)


def add_part(chunk, total, part):
    @pl.when(chunk == 0)
    def _():
        total[...] = part

    @pl.when(chunk > 0)
    def _():
        total[...] += part


def run_attention_forward(layer, place, rows, weights, pieces):
    width = rows.shape[1]
    return pl.pallas_call(
        functools.partial(attention_forward_kernel, layer, len(pieces)),
        out_shape=(
            jax.ShapeDtypeStruct((4, ROWS, 384), BF16),
            jax.ShapeDtypeStruct((4, 3, 2 * WIN, WIN), BF16),
            jax.ShapeDtypeStruct((4, ROWS, 128), BF16),
            jax.ShapeDtypeStruct((ROWS, width), BF16),
        ),
        in_specs=[SM, HB, HB, HB, VM] + [HB] * len(pieces),
        out_specs=(VM,) * 4,
        scratch_shapes=[
            pltpu.VMEM((4, width, 384), BF16),
            pltpu.VMEM((4, 128, width), BF16),
            pltpu.VMEM((4, 16, 384), BF16),
            pltpu.VMEM((ROWS, width), BF16),
            pltpu.VMEM((ROWS, width), F32),
            pltpu.VMEM((3, 2 * WIN, WIN), F32),
            pltpu.SemaphoreType.DMA((4, 4)),
        ],
        **params(7),
    )(place, rows, *weights, *pieces)


def attention_backward_kernel(
    layer, count, place, g_ref, qkv_ref, probs_ref, wqkv, wproj, *refs
):
    pieces = refs[:count] if count > 1 else (refs[0], ATTN_SPAN)
    dqkv_ref, sums_ref, d_ref, wq, wp, rows, total, gmix, sems = refs[count:]
    copy = start_rows(g_ref, rows, sems)
    start_attention_copies(layer, place, wqkv, wproj, None, pieces, wq, wp, sems)
    copy.wait()

    def chunk_step(chunk, carry):
        wait_chunk(chunk, (wq, wp), sems)
        gmix[...] = dot_nt(rows[...], wp[chunk]).astype(BF16)
        first = first_head_lanes()
        scale = HEAD_DIM**-0.5
        outs = []
        for window in range(3):
            span = pl.ds(window * WIN_STEP, WIN)
            query = stack_heads(qkv_ref[chunk, span, 0:128], first)
            key = qkv_ref[chunk, span, 128:256]
            grad = stack_heads(gmix[span, :], first)
            probs = probs_ref[chunk, window]
            gprobs = dot_nt(grad, qkv_ref[chunk, span, 256:384])
            gvalue = dot_tn(probs, grad)
            probs = probs.astype(F32)
            inner = jnp.sum(gprobs * probs, axis=-1, keepdims=True)
            gscores = (probs * (gprobs - inner)).astype(BF16)
            gquery = dot_nn(gscores, key) * scale
            gkey = dot_tn(gscores, query) * scale
            outs.append((jnp.where(first, gquery[:WIN], gquery[WIN:]), gkey, gvalue))
        joined = jnp.concatenate(
            [join_windows([out[item] for out in outs]) for item in range(3)], axis=1
        ).astype(BF16)
        dqkv_ref[chunk] = joined
        sums_ref[chunk] = jnp.broadcast_to(
            jnp.sum(joined.astype(F32), axis=0, keepdims=True), (8, 384)
        )
        add_part(chunk, total, dot_nt(dqkv_ref[chunk], wq[chunk]))
        return carry

    lax.fori_loop(0, 4, chunk_step, 0, unroll=True)
    d_ref[...] = total[...].astype(BF16)


def run_attention_backward(layer, place, grad, qkv, probs, weights, pieces):
    width = grad.shape[1]
    return pl.pallas_call(
        functools.partial(attention_backward_kernel, layer, len(pieces)),
        out_shape=(
            jax.ShapeDtypeStruct((4, ROWS, 384), BF16),
            jax.ShapeDtypeStruct((4, 8, 384), F32),
            jax.ShapeDtypeStruct((ROWS, width), BF16),
        ),
        in_specs=[SM, HB, VM, VM, HB, HB] + [HB] * len(pieces),
        out_specs=(VM,) * 3,
        scratch_shapes=[
            pltpu.VMEM((4, width, 384), BF16),
            pltpu.VMEM((4, 128, width), BF16),
            pltpu.VMEM((ROWS, width), BF16),
            pltpu.VMEM((ROWS, width), F32),
            pltpu.VMEM((ROWS, 128), BF16),
            pltpu.SemaphoreType.DMA((4, 4)),
        ],
        **params(12),
    )(place, grad, qkv, probs, *weights[:2], *pieces)


def gelu_pair(u):
    size = jnp.abs(u) * (0.5**0.5)
    t = 1.0 / (1.0 + 0.3275911 * size)
    poly = t * (
        0.254829592
        + t * (-0.284496736 + t * (1.421413741 + t * (-1.453152027 + t * 1.061405429)))
    )
    bell = jnp.exp(-0.5 * u * u)
    tail = 0.5 * poly * bell
    phi = jnp.where(u >= 0.0, 1.0 - tail, tail)
    return u * phi, phi + u * bell * 0.3989422804014327


def mlp_forward_kernel(
    a_ref, pieces, h_ref, slope_ref, m_ref, w1, w2, bs, rows, total, sems
):
    copy = start_rows(a_ref, rows, sems)
    start_mlp_copies((pieces, MLP_SPAN), w1, w2, sems, bs)
    copy.wait()

    def chunk_step(chunk, carry):
        wait_chunk(chunk, (w1, w2), sems)
        wait_bias(chunk, bs, sems)
        bias = jnp.sum(bs[chunk].astype(F32), axis=0, keepdims=True)
        value, slope = gelu_pair(dot_nn(rows[...], w1[chunk]) + bias)
        h_ref[chunk] = value.astype(BF16)
        slope_ref[chunk] = slope.astype(BF16)
        add_part(chunk, total, dot_nn(h_ref[chunk], w2[chunk]))
        return carry

    lax.fori_loop(0, 4, chunk_step, 0, unroll=True)
    m_ref[...] = total[...].astype(BF16)


def run_mlp_forward(rows, pieces):
    width = rows.shape[1]
    return pl.pallas_call(
        mlp_forward_kernel,
        out_shape=(
            jax.ShapeDtypeStruct((4, ROWS, 512), BF16),
            jax.ShapeDtypeStruct((4, ROWS, 512), BF16),
            jax.ShapeDtypeStruct((ROWS, width), BF16),
        ),
        in_specs=[HB, HB],
        out_specs=(VM,) * 3,
        scratch_shapes=[
            pltpu.VMEM((4, width, 512), BF16),
            pltpu.VMEM((4, 512, width), BF16),
            pltpu.VMEM((4, 16, 512), BF16),
            pltpu.VMEM((ROWS, width), BF16),
            pltpu.VMEM((ROWS, width), F32),
            pltpu.SemaphoreType.DMA((4, 4)),
        ],
        **params(8),
    )(rows, pieces)


def mlp_backward_kernel(
    g_ref, slope_ref, pieces, du_ref, sums_ref, d_ref, w1, w2, rows, total, sems
):
    copy = start_rows(g_ref, rows, sems)
    start_mlp_copies((pieces, MLP_SPAN), w1, w2, sems)
    copy.wait()

    def chunk_step(chunk, carry):
        wait_chunk(chunk, (w1, w2), sems)
        grad = dot_nt(rows[...], w2[chunk]) * slope_ref[chunk].astype(F32)
        grad = grad.astype(BF16)
        du_ref[chunk] = grad
        sums_ref[chunk] = jnp.broadcast_to(
            jnp.sum(grad.astype(F32), axis=0, keepdims=True), (8, 512)
        )
        add_part(chunk, total, dot_nt(du_ref[chunk], w1[chunk]))
        return carry

    lax.fori_loop(0, 4, chunk_step, 0, unroll=True)
    d_ref[...] = total[...].astype(BF16)


def mlp_both_kernel(
    a_ref, g_ref, pieces, h_ref, m_ref, du_ref, sums_ref, d_ref,
    w1, w2, bs, rows, grads, total, back, sems,
):
    copy = start_rows(a_ref, rows, sems)
    other = pltpu.make_async_copy(g_ref, grads, sems.at[3, 1])
    other.start()
    start_mlp_copies((pieces, MLP_SPAN), w1, w2, sems, bs)
    copy.wait()
    other.wait()

    def chunk_step(chunk, carry):
        wait_chunk(chunk, (w1, w2), sems)
        wait_bias(chunk, bs, sems)
        bias = jnp.sum(bs[chunk].astype(F32), axis=0, keepdims=True)
        value, slope = gelu_pair(dot_nn(rows[...], w1[chunk]) + bias)
        h_ref[chunk] = value.astype(BF16)
        grad = (dot_nt(grads[...], w2[chunk]) * slope).astype(BF16)
        du_ref[chunk] = grad
        sums_ref[chunk] = jnp.broadcast_to(
            jnp.sum(grad.astype(F32), axis=0, keepdims=True), (8, 512)
        )
        add_part(chunk, total, dot_nn(h_ref[chunk], w2[chunk]))
        add_part(chunk, back, dot_nt(du_ref[chunk], w1[chunk]))
        return carry

    lax.fori_loop(0, 4, chunk_step, 0, unroll=True)
    m_ref[...] = total[...].astype(BF16)
    d_ref[...] = back[...].astype(BF16)


def run_mlp_both(rows, grad, pieces):
    width = rows.shape[1]
    return pl.pallas_call(
        mlp_both_kernel,
        out_shape=(
            jax.ShapeDtypeStruct((4, ROWS, 512), BF16),
            jax.ShapeDtypeStruct((ROWS, width), BF16),
            jax.ShapeDtypeStruct((4, ROWS, 512), BF16),
            jax.ShapeDtypeStruct((4, 8, 512), F32),
            jax.ShapeDtypeStruct((ROWS, width), BF16),
        ),
        in_specs=[HB, HB, HB],
        out_specs=(VM,) * 5,
        scratch_shapes=[
            pltpu.VMEM((4, width, 512), BF16),
            pltpu.VMEM((4, 512, width), BF16),
            pltpu.VMEM((4, 16, 512), BF16),
            pltpu.VMEM((ROWS, width), BF16),
            pltpu.VMEM((ROWS, width), BF16),
            pltpu.VMEM((ROWS, width), F32),
            pltpu.VMEM((ROWS, width), F32),
            pltpu.SemaphoreType.DMA((4, 4)),
        ],
        **params(15),
    )(rows, grad, pieces)


def run_mlp_backward(grad, slope, pieces):
    width = grad.shape[1]
    return pl.pallas_call(
        mlp_backward_kernel,
        out_shape=(
            jax.ShapeDtypeStruct((4, ROWS, 512), BF16),
            jax.ShapeDtypeStruct((4, 8, 512), F32),
            jax.ShapeDtypeStruct((ROWS, width), BF16),
        ),
        in_specs=[HB, VM, HB],
        out_specs=(VM,) * 3,
        scratch_shapes=[
            pltpu.VMEM((4, width, 512), BF16),
            pltpu.VMEM((4, 512, width), BF16),
            pltpu.VMEM((ROWS, width), BF16),
            pltpu.VMEM((ROWS, width), F32),
            pltpu.SemaphoreType.DMA((4, 4)),
        ],
        **params(7),
    )(grad, slope, pieces)


SEND, AWAY, NEAR, ALL = 0, 1, 2, 3
STAGE_SLOTS = (((0, 1), (1, 1)), ((1, 0),), ((0, 0),), ((0, 0), (0, 1), (1, 0), (1, 1)))


def weight_grad_kernel(
    stage, place, x1_own, x1_far, y1_own, y1_far, x2_own, x2_far, y2_own, y2_far, *refs
):
    slots = STAGE_SLOTS[stage]
    (xs, y1, y2, turned, added, sems), refs = refs[-6:], refs[:-6]
    out_ref = refs[-1]
    got = [refs[0].at[0 if stage == NEAR else 1], *refs[1:-1]] if stage in (AWAY, NEAR) else []
    whole = out_ref
    if stage == ALL:
        out_ref = added
    outs = [out_ref.at[slot] for slot in range(len(slots))] if len(slots) > 1 else [out_ref]
    copies = []
    for slot, (side, core) in enumerate(slots):
        if stage != ALL:
            side, core = place[SIDE] ^ side, place[CORE] ^ core
        start = aligned(4 * side + core, 128)
        for index, sources in enumerate(((x1_own, x1_far), (x2_own, x2_far))):
            for half, source in enumerate(sources):
                for run in range(2):
                    copies.append(
                        pltpu.make_async_copy(
                            source.at[:, pl.ds(start + 256 * run, 128)],
                            xs.at[index, slot, pl.ds(ROWS * half, ROWS), pl.ds(128 * run, 128)],
                            sems.at[4, 8 * slot + 4 * index + 2 * half + run],
                        )
                    )
    for copy in copies:
        copy.start()
    for chunk in range(4):
        for index, (source, target) in enumerate(
            ((y1_own, y1), (y1_far, y1), (y2_own, y2), (y2_far, y2))
        ):
            pltpu.make_async_copy(
                source.at[chunk],
                target.at[chunk, pl.ds(ROWS * (index % 2), ROWS)],
                sems.at[chunk, index],
            ).start()
        for index, source in enumerate(got):
            pltpu.make_async_copy(
                source.at[chunk], added.at[index, chunk], sems.at[chunk, 4 + index]
            ).start()
    for copy in copies:
        copy.wait()
    span1 = y1.shape[2]

    def chunk_step(chunk):
        for index, target in enumerate((y1, y1, y2, y2)):
            half = target.at[chunk, pl.ds(ROWS * (index % 2), ROWS)]
            pltpu.make_async_copy(half, half, sems.at[chunk, index]).wait()
        for index in range(len(got)):
            array = added.at[index, chunk]
            pltpu.make_async_copy(array, array, sems.at[chunk, 4 + index]).wait()
        for slot, out in enumerate(outs):
            if chunk == 0:
                for index in range(2):
                    turned[index, slot] = xs[index, slot].T
            first = dot_nn(turned[0, slot], y1[chunk])
            second = dot_nn(turned[1, slot], y2[chunk])
            for index in range(len(got)):
                first += added[index, chunk, :, 0:span1].astype(F32)
                second += added[index, chunk, :, span1:].astype(F32)
            out[chunk, :, 0:span1] = first.astype(BF16)
            out[chunk, :, span1:] = second.astype(BF16)
            if stage == ALL:
                pltpu.make_async_copy(
                    out.at[chunk], whole.at[slot, chunk], sems.at[chunk, 8 + slot]
                ).start()

    for chunk in range(4):
        chunk_step(chunk)
    if stage == ALL:
        for chunk in range(4):
            for slot, out in enumerate(outs):
                pltpu.make_async_copy(
                    out.at[chunk], whole.at[slot, chunk], sems.at[chunk, 8 + slot]
                ).wait()


def run_weight_grad(stage, place, x1, y1, x2, y2, *got):
    rows, width = 2 * ROWS, x1[0].shape[1]
    span1, span2 = y1[0].shape[2], y2[0].shape[2]
    part = width // 4
    shape = (4, part, span1 + span2)
    slots = len(STAGE_SLOTS[stage])
    return pl.pallas_call(
        functools.partial(weight_grad_kernel, stage),
        out_shape=jax.ShapeDtypeStruct((slots, *shape) if slots > 1 else shape, BF16),
        in_specs=[SM] + [HB] * (8 + len(got)),
        out_specs=HB if stage == ALL else VM,
        scratch_shapes=[
            pltpu.VMEM((2, slots, rows, part), BF16),
            pltpu.VMEM((4, rows, span1), BF16),
            pltpu.VMEM((4, rows, span2), BF16),
            pltpu.VMEM((2, slots, part, rows), BF16),
            pltpu.VMEM((4 if stage == ALL else max(len(got), 1), *shape), BF16),
            pltpu.SemaphoreType.DMA((5, 32)),
        ],
        **params((4 if span1 > 384 else 3) * slots + 2),
    )(place, *x1, *y1, *x2, *y2, *got)


def add_depth_kernel(place, *refs):
    parts, (stay, move) = refs[:-2], refs[-2:]
    total = parts[0][...].astype(F32)
    for part in parts[1:]:
        total += part[...].astype(F32)
    half = total.shape[0] // 2
    low, high = total[:half], total[half:]
    even = place[PAIR] == 0
    stay[...] = jnp.where(even, low, high).astype(BF16)
    move[...] = jnp.where(even, high, low).astype(BF16)


def run_add_depth(place, parts):
    rows, span = parts[0].shape
    shape = jax.ShapeDtypeStruct((rows // 2, span), BF16)
    return pl.pallas_call(
        add_depth_kernel,
        out_shape=(shape, shape),
        in_specs=[SM] + [VM] * len(parts),
        out_specs=(VM, VM),
        **params(2),
    )(place, *parts)


def collect_kernel(place, fc2_last, *refs):
    out = refs[-1]
    layers = (len(refs) - 1) // 6
    narrow, wide = aligned(place[PAIR], 128), aligned(place[PAIR], 512)
    out[...] = jnp.zeros(out.shape, F32)
    for layer in range(layers):
        sums1, sums2, qv_own, qv_far, fc1_own, fc1_far = refs[6 * layer : 6 * layer + 6]
        row = 12 * layer
        out[row : row + 2, :] = sums1[0:2, :]
        out[row + 2 : row + 3, :] = sums2[2:3, :]
        out[row + 3 : row + 5, :] = sums2[0:2, :]
        above = refs[6 * layer + 6][2:3, :] if layer + 1 < layers else fc2_last[0:1, :]
        out[row + 5 : row + 6, :] = above
        for depth in range(4):
            qv = qv_own[depth, 0:1, :] + qv_far[depth, 0:1, :]
            for item in range(2):
                out[row + 6 + item, pl.ds(depth * 256 + narrow, 128)] = qv[
                    0, 256 * item : 256 * item + 128
                ]
            fc1 = fc1_own[depth, 0:1, :] + fc1_far[depth, 0:1, :]
            out[pl.ds(row + 8 + depth, 1), pl.ds(wide, 512)] = fc1


def run_collect(place, fc2_last, parts):
    layers = len(parts) // 6
    return pl.pallas_call(
        collect_kernel,
        out_shape=jax.ShapeDtypeStruct((12 * layers, 1024), F32),
        in_specs=[SM] + [VM] * (1 + len(parts)),
        out_specs=VM,
        **params(2),
    )(place, fc2_last, *parts)


def release_kernel(place, total, *outs):
    rows, (qv, fc1) = outs[:6], outs[6:]
    quarter = aligned(place[DEPTH], 256)
    for layer in range(fc1.shape[0]):
        for index, out in enumerate(rows):
            out[layer : layer + 1, :] = total[pl.ds(12 * layer + index, 1), :]
        for item in range(2):
            qv[layer, item : item + 1, :] = total[
                pl.ds(12 * layer + 6 + item, 1), pl.ds(quarter, 256)
            ]
        fc1[layer : layer + 1, :] = total[pl.ds(12 * layer + 8 + place[DEPTH], 1), :]


def run_release(place, total):
    layers = total.shape[0] // 12
    row = jax.ShapeDtypeStruct((layers, 1024), F32)
    return pl.pallas_call(
        release_kernel,
        out_shape=(row,) * 6 + (jax.ShapeDtypeStruct((layers, 2, 256), F32), row),
        in_specs=[SM, VM],
        out_specs=(VM,) * 8,
        **params(2),
    )(place, total)


def finish_kernel(place, *refs):
    layers = (len(refs) - 4) // 4
    ins, (qkv, proj, fc1, fc2) = refs[: 4 * layers], refs[4 * layers :]
    for layer in range(layers):
        for side in range(2):
            attn, mlp = ins[4 * layer + side], ins[4 * layer + 2 + side]
            pair = place[PAIR] if side == 0 else 1 - place[PAIR]
            narrow, wide = aligned(pair, 128), aligned(pair, 512)
            for item in range(3):
                qkv[layer, item, :, pl.ds(narrow, 128)] = attn[
                    :, item * 128 : item * 128 + 128
                ].astype(F32)
            proj[layer, pl.ds(narrow, 128), :] = attn[:, 384:512].T.astype(F32)
            fc1[layer, :, pl.ds(wide, 512)] = mlp[:, 0:512].astype(F32)
            fc2[layer, pl.ds(wide, 512), :] = mlp[:, 512:1024].T.astype(F32)


def run_finish(place, parts):
    rows = parts[0].shape[0]
    return pl.pallas_call(
        finish_kernel,
        out_shape=(
            jax.ShapeDtypeStruct((2, 3, rows, 256), F32),
            jax.ShapeDtypeStruct((2, 256, rows), F32),
            jax.ShapeDtypeStruct((2, rows, 1024), F32),
            jax.ShapeDtypeStruct((2, 1024, rows), F32),
        ),
        in_specs=[SM] + [VM] * len(parts),
        out_specs=(VM,) * 4,
        **params(4),
    )(place, *parts)


def on_device(*args):
    (
        images_in, out_cotangent, norm1_gain, norm1_bias, qkv_weight, qv_bias, proj_weight,
        proj_bias, norm2_gain, norm2_bias, fc1_weight, fc1_bias, fc2_weight, fc2_bias,
    ) = args
    images, seq, _ = images_in.shape
    layers = qkv_weight.shape[0]
    n_far, n_mp = lax.axis_size("far"), lax.axis_size("mp")
    mine = images // n_mp

    side, pair, core = lax.axis_index("y"), lax.axis_index("x"), lax.axis_index("core")
    depth = lax.axis_index("mp")
    here = jnp.stack(
        [
            side, core, pair, depth,
            side * 2 + core, (1 - side) * 2 + core, side * 2 + 1 - core, (1 - side) * 2 + 1 - core,
        ]
    ).astype(jnp.int32)

    def swap(value, axis):
        return lax.ppermute(value, axis, [(0, 1), (1, 0)])

    def shift(value, step):
        return lax.ppermute(
            value, "mp", [(index, (index + step) % n_mp) for index in range(n_mp)]
        )

    def after(value, *others):
        return lax.optimization_barrier((value, *others))[0]

    wqkv = qkv_weight.transpose(0, 2, 1, 3)
    attn_weights = (wqkv, proj_weight, qv_bias)
    packed = run_pack(here, wqkv, proj_weight, fc1_weight, fc2_weight, qv_bias, fc1_bias)
    attn_pieces, mlp_pieces = [[]], []
    moved = []
    for step in (1, 3, 2):
        same = shift(packed[0], step)
        moved.append(same)
        other = swap(same, "y")
        attn_pieces[0].append((step, [same, other, swap(same, "core"), swap(other, "core")]))
    attn_pieces[0] = [array for _, arrays in sorted(attn_pieces[0]) for array in arrays]
    stream, normed = run_enter(here, images_in, mine, norm1_gain[0], norm1_bias[0])
    grad, grad_b, fc2_sum = run_enter_back(here, out_cotangent, mine)
    grad_b_far = swap(grad_b, "x")
    gathered = []
    for index in (1, 2):
        gathered = lax.all_gather((after(packed[index], *gathered) if gathered else packed[index]), ("y", "core", "mp"))
        value = gathered.reshape(2, 2, n_mp, *gathered.shape[1:])
        mlp_pieces.append(value)
        attn_pieces.append([value])
        gathered = [gathered]

    def both(run, own, far, *waits):
        results = run(own)
        return list(zip(results, run(after(far, *waits) if waits else far)))

    saved = []
    for layer in range(layers):
        normed_far = swap(normed, "x")
        qkv, probs, mixed, part = both(
            lambda rows: run_attention_forward(layer, here, rows, attn_weights, attn_pieces[layer]),
            normed, normed_far,
        )
        middle, normed2 = run_residual_norm(
            stream, part[0], swap(part[1], "x"), proj_bias[layer], norm2_gain[layer],
            norm2_bias[layer],
        )
        normed2_far = swap(normed2, "x")
        if layer + 1 < layers:
            active, slope, part = both(
                lambda rows: run_mlp_forward(rows, mlp_pieces[layer]),
                after(normed2, grad_b_far), normed2_far,
            )
        else:
            cotangents, slope = [grad_b, grad_b_far], None
            active, part, *last_back = both(
                lambda rows: run_mlp_both(rows, cotangents.pop(0), mlp_pieces[layer]),
                normed2, normed2_far,
            )
        saved.append(
            (stream, (normed, normed_far), list(zip(qkv, probs)), mixed, middle, (normed2, normed2_far), active, slope)
        )
        if layer + 1 < layers:
            stream, normed = run_residual_norm(
                middle, part[0], swap(part[1], "x"), fc2_bias[layer], norm1_gain[layer + 1],
                norm1_bias[layer + 1],
            )
        else:
            last = (middle, *part, fc2_bias[layer])

    class Sum:
        def __init__(self, *arrays):
            self.arrays = arrays
            self.core = swap(run_weight_grad(SEND, here, *arrays), "core")

        def away(self):
            kept = run_weight_grad(AWAY, here, *self.arrays, self.core)
            self.side = swap(kept, "y")
            return kept

        def near(self, *waits):
            side = after(self.side, *waits) if waits else self.side
            kept = run_weight_grad(NEAR, here, *self.arrays, self.core, side)
            flat = kept.reshape(-1, kept.shape[-1])
            self.total = lax.psum_scatter(flat, "mp", tiled=True)
            return kept

        def result(self):
            return run_add_depth(here, [self.total])

    class SumAtOnce(Sum):
        def __init__(self, *arrays):
            grads = run_weight_grad(ALL, here, *arrays)
            flat = grads.reshape(-1, grads.shape[-1])
            self.total = lax.psum_scatter(flat, ("y", "core", "mp"), tiled=True)

    attn, mlp, groups = None, None, []
    small = [None] * layers
    for layer in reversed(range(layers)):
        stream, normed, qkv, mixed, middle, normed2, active, slope = saved[layer]
        qkvs = list(qkv)
        if attn is None:
            du, fc1_sum, part = last_back
        else:
            slopes = list(slope)
            du, fc1_sum, part = both(
                lambda rows: run_mlp_backward(rows, slopes.pop(0), mlp_pieces[layer]),
                grad_b, grad_b_far, attn.away(),
            )
        mlp = (SumAtOnce if layer else Sum)(normed2, du, (grad_b, grad_b_far), active)
        grad, grad_b, sums2 = run_norm_back(
            grad, part[0], swap(part[1], "x"), middle, norm2_gain[layer]
        )
        grad_b_far = swap(grad_b, "x")
        dqkv, qv_sum, part = both(
            lambda rows: run_attention_backward(
                layer, here, rows, *qkvs.pop(0), attn_weights, attn_pieces[layer]
            ),
            grad_b, grad_b_far, *([] if layer else [mlp.away()]),
        )
        if layer:
            stream_in, near, away, bias = last
            last = run_residual(stream_in, near, swap(after(away, dqkv[0]), "x"), bias)
            last = after(last, mlp.total)
        above, attn = attn, Sum(normed, dqkv, (grad_b, grad_b_far), mixed)
        if above:
            grad = after(grad, above.near())
        grad, grad_b, sums1 = run_norm_back(
            grad, part[0], swap(part[1], "x"), stream, norm1_gain[layer]
        )
        if layer:
            grad_b_far = swap(grad_b, "x")
        small[layer] = [sums1, sums2, *qv_sum, *fc1_sum]
        groups = [attn, mlp, *groups]

    block_out = run_leave(here, [lax.all_gather(last, "mp")], seq, mine, BF16)
    parts = [shift(grad_b, step) for step in (1, 3, 2)]
    attn.core = after(attn.core, grad_b)
    attn.away()
    kept = mlp.near()
    kept = attn.near(kept, block_out, *parts)
    parts = [after(part, kept) for part in parts]
    input_grad = run_leave(here, [grad_b, *parts], seq, mine, F32)
    total = run_collect(here, fc2_sum, [part for group in small for part in group])
    total = after(total, kept)
    for axis in ("core", "x", "y"):
        total = total + swap(total, axis)
    for bit in range(n_far.bit_length() - 1):
        pairs = [(index, index ^ (1 << bit)) for index in range(n_far)]
        total = total + lax.ppermute(total, "far", pairs)
    total = after(total, *parts)
    for bit in range(n_mp.bit_length() - 1):
        pairs = [(index, index ^ (1 << bit)) for index in range(n_mp)]
        total = total + lax.ppermute(total, "mp", pairs)
    n1g, n1b, pb, n2g, n2b, f2b, qv, fc1 = run_release(here, total)

    ready = [group.result() for group in groups]
    if n_far == 1:
        parts = [part for stay, move in ready for part in (stay, swap(move, "x"))]
    else:
        parts = [part for stay, move in ready for part in spread_rows(stay, move)]
    g_qkv, g_proj, g_fc1, g_fc2 = run_finish(here, parts)
    block_out, input_grad = (
        value.reshape(seq, images, -1).transpose(1, 0, 2) for value in (block_out, input_grad)
    )
    return (
        block_out, input_grad, n1g, n1b, g_qkv.transpose(0, 2, 1, 3), qv, g_proj, pb, n2g, n2b,
        g_fc1, fc1, g_fc2, f2b,
    )


def spread_rows(stay, move):
    pair = lax.axis_index("x")
    value = jnp.stack(
        [jnp.where(pair == 0, stay, move), jnp.where(pair == 0, move, stay)]
    ).astype(F32)
    value = lax.psum(value, "far")
    value = lax.all_gather(value, ("y", "x", "core"))
    rows, span = value.shape[2:]
    value = value.reshape(2, 2, 2, 2, rows, span).transpose(0, 3, 2, 4, 1, 5)
    value = value.reshape(8 * rows, 2, span)
    count = rows // lax.axis_size("far")
    place = lax.axis_index(("far", "y", "x", "core"))
    value = lax.dynamic_slice_in_dim(value, place * count, count, 0)
    mine = lax.dynamic_index_in_dim(value, pair, 1, keepdims=False)
    other = lax.dynamic_index_in_dim(value, 1 - pair, 1, keepdims=False)
    return mine, other


def solution(mesh):
    n_dp, n_mp = mesh.shape["dp"], mesh.shape["mp"]
    fine = Mesh(mesh.devices.reshape(n_dp // 8, 2, 2, 2, n_mp), ("far", "y", "x", "core", "mp"))
    dp = ("far", "y", "x", "core")
    return jax.shard_map(
        on_device,
        mesh=fine,
        in_specs=(
            P(dp, None, None),
            P(dp, None, None),
            P(),
            P(),
            P(None, None, None, "mp"),
            P(None, None, "mp"),
            P(None, "mp", None),
            P(),
            P(),
            P(),
            P(None, None, "mp"),
            P(None, "mp"),
            P(None, "mp", None),
            P(),
        ),
        out_specs=(
            P(dp, None, None),
            P(dp, None, None),
            P(),
            P(),
            P(None, dp, None, "mp"),
            P(None, None, "mp"),
            P(None, "mp", dp),
            P(),
            P(),
            P(),
            P(None, dp, "mp"),
            P(None, "mp"),
            P(None, "mp", dp),
            P(),
        ),
        check_vma=False,
    )
```
